32 devices in a mesh: expert: 8 (over y, x, core), fsdp: 4 (over z).
Axes of the slice: x: 2, y: 2, z: 4, core: 2. Of those that a mesh axis runs over, the one named last changes fastest.
Arguments:
- tokens: bfloat16 [4096, 2048], P(('expert', 'fsdp')), may hold values from -6 to 6
- lengths: int32 [32, 4], P(('expert', 'fsdp')), may hold values from 1 to 96, 128 in all within a row
- routes: int32 [4096, 8], P(('expert', 'fsdp')), may hold values from 0 to 15, all different within a row; in each aligned block of 128 rows (0 to 127, 128 to 255, ...) at most 96 rows name the same one
- attn_gain: bfloat16 [2048], P('fsdp'), may hold values from 0.25 to 1.75
- w_query: bfloat16 [2048, 4096], P('fsdp'), may hold values from -0.125 to 0.125
- key_projection: bfloat16 [2048, 512], P('fsdp'), may hold values from -0.125 to 0.125
- value_projection: bfloat16 [2048, 512], P('fsdp'), may hold values from -0.125 to 0.125
- w_out: bfloat16 [4096, 2048], P('fsdp'), may hold values from -0.375 to 0.375
- query_gain: bfloat16 [128], P('fsdp'), may hold values from 0.25 to 1.75
- key_gain: bfloat16 [128], P('fsdp'), may hold values from 0.25 to 1.75
- ffn_gain: bfloat16 [2048], P('fsdp'), may hold values from 0.25 to 1.75
- w_router: bfloat16 [2048, 16], P('fsdp'), may hold values from -0.0625 to 0.0625
- w_gate: bfloat16 [16, 2048, 768], P('expert', None, 'fsdp'), may hold values from -0.125 to 0.125
- w_up: bfloat16 [16, 2048, 768], P('expert', None, 'fsdp'), may hold values from -0.125 to 0.125
- w_down: bfloat16 [16, 768, 2048], P('expert', 'fsdp'), may hold values from -0.625 to 0.625
- cotangent: bfloat16 [4096, 2048], P(('expert', 'fsdp')), may hold values from -6 to 6
Outputs:
- block_out: bfloat16 [4096, 2048], P(('expert', 'fsdp'))
- grad_tokens: float32 [4096, 2048], P(('expert', 'fsdp'))
- grad_attn_gain: float32 [2048], P('fsdp')
- grad_w_query: float32 [2048, 4096], P('fsdp')
- grad_w_key: float32 [2048, 512], P('fsdp')
- grad_w_value: float32 [2048, 512], P('fsdp')
- grad_w_out: float32 [4096, 2048], P('fsdp')
- grad_query_gain: float32 [128], P('fsdp')
- grad_key_gain: float32 [128], P('fsdp')
- grad_ffn_gain: float32 [2048], P('fsdp')
- grad_w_router: float32 [2048, 16], P('fsdp')
- grad_w_gate: float32 [16, 2048, 768], P('expert', None, 'fsdp')
- grad_w_up: float32 [16, 2048, 768], P('expert', None, 'fsdp')
- grad_w_down: float32 [16, 768, 2048], P('expert', 'fsdp')
The draws below stay inside these ranges and needn't reach their ends.
Inputs may be any that keep to these rules, and one draw needn't show every extreme that they name: The lengths of one device sum to 128; each device holds one sequence of exactly 96 tokens. `routes`: A token names 8 different experts. Among the 128 tokens of one device no expert is named more than 96 times, and some expert reaches 96 on some device.
All inputs are finite; a program needn't handle non-finite values.
Results may differ from the reference program's by a relative error of at most 0.024.
Values may be sent and summed in bfloat16 or wider, within the bound.
A program may use at most 448 MiB of HBM per device.

```python
import math
from functools import partial
import jax
import jax.numpy as jnp
import numpy as np
from jax import lax

MODEL_WIDTH = 2048
QUERY_HEADS = 32
KEY_VALUE_HEADS = 4
HEAD_WIDTH = 128
FF = 768
TOPK = 8
DEVICE_TOKENS = 128
SEQ_SLOTS = 4
EXPERTS = 16
TOKEN_TOTAL = 4096
SEQ_MOST = 96
CAP = 96
DEVICES = 32


def block_levels(own_key, extent, pieces, smallest, largest):
    gain = 1.0
    for axis_at, parts in pieces:
        heights = jax.random.uniform(jax.random.fold_in(jax.random.fold_in(own_key, 6), axis_at), (parts,), jnp.float32, smallest / len(pieces), largest / len(pieces))
        gain = gain * jnp.repeat(jnp.exp(heights), extent[axis_at] // parts).reshape((-1,) + (1,) * (len(extent) - 1 - axis_at))
    return gain


def length_profile(amount, total, limit, skew):
    weights = [(1 << 20) // math.isqrt(rank ** skew) + 1 for rank in range(2, amount + 1)]
    rest, holding = total - limit - (amount - 1), [1] * (amount - 1)
    while rest > 0:
        movable = [i for i in range(amount - 1) if holding[i] < limit]
        mass, remaining = sum([weights[i] for i in movable]), rest
        for i in movable:
            addition = min(limit - holding[i], max(1, remaining * weights[i] // mass), rest)
            holding[i] = holding[i] + addition
            rest = rest - addition
    return np.array([limit] + holding)


def uneven(rng, number_of, total, bound, lean):
    if number_of == 2:
        one = jax.random.randint(rng, (), max(1, total - bound), min(bound, total - 1) + 1)
        return jnp.stack([one, total - one])
    tallies = jnp.asarray(length_profile(number_of, total, bound, lean), jnp.int32)
    couples = (number_of - 1) // 2
    giver, receiver = tallies[1:1 + 2 * couples:2], tallies[2:2 + 2 * couples:2]
    slack = jnp.minimum(giver - 1, bound - receiver)
    shifted = jax.random.randint(jax.random.fold_in(rng, 1), (couples,), 0, 1 << 20) % (slack + 1)
    tallies = tallies.at[1:1 + 2 * couples:2].set(giver - shifted).at[2:2 + 2 * couples:2].set(receiver + shifted)
    return tallies[jax.random.permutation(jax.random.fold_in(rng, 2), number_of)]


def assign_block(stream_key, own, number, rows, number_of, top, bound, lean):
    sequence = jax.random.permutation(stream_key, number_of)
    heavy_load, usual = load_shares(number_of, rows * top, bound, lean, True), load_shares(number_of, rows * top, bound, lean, False)
    places = jnp.arange(number_of)

    def named(tallies, turn):
        used = int((tallies > 0).sum())
        fixed = max(1, used // 4)
        moved = fixed + (places - fixed + turn * (used - fixed)) % max(1, number_of - fixed)
        return jnp.zeros((number_of,), jnp.int32).at[sequence[jnp.where(places < fixed, places, moved)]].set(jnp.asarray(tallies, jnp.int32))

    tallies = jnp.where(number % 4 == 0, named(heavy_load, number // 4), named(usual, number - number // 4 - 1))
    mixed = jax.random.permutation(jax.random.fold_in(own, 3), number_of)
    giver, sink = mixed[0:number_of // 2 * 2:2], mixed[1:number_of // 2 * 2:2]
    margin = jnp.minimum(tallies[giver] - 1, bound - tallies[sink]) // 2
    margin = jnp.where((giver == sequence[0]) | (sink == sequence[0]) | (tallies[sink] == 0), 0, jnp.maximum(margin, 0))
    moved = jax.random.randint(jax.random.fold_in(own, 4), (number_of // 2,), 0, 1 << 20) % (margin + 1)
    tallies = tallies.at[giver].add(-moved).at[sink].add(moved)
    items = jnp.searchsorted(jnp.cumsum(tallies), jnp.arange(rows * top), side="right").astype(jnp.int32)
    table = items.reshape(top, rows).T
    table = table[jax.random.permutation(jax.random.fold_in(own, 1), rows)]
    turn = jax.random.randint(jax.random.fold_in(own, 2), (rows, 1), 0, top)
    return jnp.take_along_axis(table, (jnp.arange(top)[None, :] + turn) % top, axis=1)


def load_shares(amount, total, most, skew, full):
    loads = [(1 << 20) // math.isqrt(standing ** skew) + 1 for standing in range(1, amount + 1)]
    largest = most if full else min(most, max(-(-total // amount), total * loads[0] // sum(loads)))
    least = 1 if total - largest >= amount - 1 else 0
    holding, surplus = [largest] + [least] * (amount - 1), total - largest - least * (amount - 1)
    while surplus > 0:
        candidates = [i for i in range(1, amount) if holding[i] < largest] or [i for i in range(1, amount) if holding[i] < most]
        pool, budget = sum([loads[i] for i in candidates]), surplus
        for i in candidates:
            addition = min(most - holding[i], max(1, budget * loads[i] // pool), surplus)
            holding[i] = holding[i] + addition
            surplus = surplus - addition
    return np.array(holding)


def normal_values(stream_key, shape, spread, most, cuts=(), kind=jnp.bfloat16):
    values = jax.random.normal(stream_key, shape, jnp.float32) * spread
    if len(cuts) > 0:
        values = block_levels(stream_key, shape, cuts, -0.22, 0.18) * values
    return jnp.clip(values, min=-most, max=most).astype(kind)


def setup_inputs(seed: int = 0) -> dict:
    arg_keys = jax.random.split(jax.random.key(seed), 17)
    tokens = normal_values(arg_keys[0], (TOKEN_TOTAL, MODEL_WIDTH), 1.0, 6.0, ((0, 32),))
    lengths = jax.vmap(lambda own: uneven(own, SEQ_SLOTS, DEVICE_TOKENS, SEQ_MOST, 2))(jax.random.split(arg_keys[1], DEVICES)).reshape((DEVICES, SEQ_SLOTS)).astype(jnp.int32)
    routes_keys = jax.random.split(jax.random.fold_in(arg_keys[2], 1), TOKEN_TOTAL // DEVICE_TOKENS)
    routes_turns = jax.random.permutation(jax.random.fold_in(arg_keys[2], 3), TOKEN_TOTAL // DEVICE_TOKENS)
    routes = jax.vmap(lambda own, number: assign_block(jax.random.fold_in(arg_keys[2], 2), own, number, DEVICE_TOKENS, EXPERTS, TOPK, CAP, 2))(routes_keys, routes_turns).reshape((TOKEN_TOTAL, TOPK))
    attn_gain = jnp.clip(1.0 + 0.15 * jax.random.normal(arg_keys[3], (MODEL_WIDTH,), jnp.float32), 0.25, 1.75).astype(jnp.bfloat16)
    w_query = normal_values(arg_keys[4], (MODEL_WIDTH, QUERY_HEADS * HEAD_WIDTH), MODEL_WIDTH ** -0.5, 0.125, ((0, 4),))
    key_projection = normal_values(arg_keys[5], (MODEL_WIDTH, KEY_VALUE_HEADS * HEAD_WIDTH), MODEL_WIDTH ** -0.5, 0.125, ((0, 4),))
    value_projection = normal_values(arg_keys[6], (MODEL_WIDTH, KEY_VALUE_HEADS * HEAD_WIDTH), MODEL_WIDTH ** -0.5, 0.125, ((0, 4),))
    w_out = normal_values(arg_keys[7], (QUERY_HEADS * HEAD_WIDTH, MODEL_WIDTH), (QUERY_HEADS * HEAD_WIDTH // 16) ** -0.5, 0.375, ((0, 4),))
    query_gain = jnp.clip(1.0 + 0.15 * jax.random.normal(arg_keys[8], (HEAD_WIDTH,), jnp.float32), 0.25, 1.75).astype(jnp.bfloat16)
    key_gain = jnp.clip(1.0 + 0.15 * jax.random.normal(arg_keys[9], (HEAD_WIDTH,), jnp.float32), 0.25, 1.75).astype(jnp.bfloat16)
    ffn_gain = jnp.clip(1.0 + 0.15 * jax.random.normal(arg_keys[10], (MODEL_WIDTH,), jnp.float32), 0.25, 1.75).astype(jnp.bfloat16)
    w_router = normal_values(arg_keys[11], (MODEL_WIDTH, EXPERTS), (4 * MODEL_WIDTH) ** -0.5, 0.0625, ((0, 4),))
    w_gate = normal_values(arg_keys[12], (EXPERTS, MODEL_WIDTH, FF), MODEL_WIDTH ** -0.5, 0.125, ((0, 8), (2, 4)))
    w_up = normal_values(arg_keys[13], (EXPERTS, MODEL_WIDTH, FF), MODEL_WIDTH ** -0.5, 0.125, ((0, 8), (2, 4)))
    w_down = normal_values(arg_keys[14], (EXPERTS, FF, MODEL_WIDTH), (FF // 8) ** -0.5, 0.625, ((0, 8), (1, 4)))
    cotangent = normal_values(arg_keys[15], (TOKEN_TOTAL, MODEL_WIDTH), 1.0, 6.0, ((0, 32),))
    return {"tokens": tokens, "lengths": lengths, "routes": routes, "attn_gain": attn_gain, "w_query": w_query, "key_projection": key_projection, "value_projection": value_projection, "w_out": w_out, "query_gain": query_gain, "key_gain": key_gain, "ffn_gain": ffn_gain, "w_router": w_router, "w_gate": w_gate, "w_up": w_up, "w_down": w_down, "cotangent": cotangent}


@jax.custom_vjp
def lower_cast(v):
    return lax.optimization_barrier(v.astype(jnp.bfloat16)).astype(jnp.float32)

@jax.custom_vjp
def lower_cast_back(v):
    return v

def low_keep(v):
    return (lower_cast(v), None)

def low_pass(kept, grad):
    return (grad,)

def back_keep(v):
    return (v, None)

def back_low(kept, grad):
    return (lower_cast(grad),)
lower_cast.defvjp(low_keep, low_pass)
lower_cast_back.defvjp(back_keep, back_low)
epsilon = 1e-06
rope_base = 1000000.0
masked_score = -1e+30
highest = lax.Precision.HIGHEST

def matrix_product(left, right):
    return jnp.dot(left, right, precision=highest, preferred_element_type=jnp.float32)

def rms_scale(values, gain_vec):
    return values * lax.rsqrt(lax.optimization_barrier(jnp.mean(values * values, axis=-1, keepdims=True)) + epsilon) * gain_vec

def rotate(values, cosine, sine_table):
    half_width = values.shape[-1] // 2
    turned = jnp.concatenate([-values[..., half_width:], values[..., :half_width]], axis=-1)
    return values * cosine + turned * sine_table

def rope_tables(places):
    frequency = rope_base ** (-jnp.arange(0, HEAD_WIDTH, 2, dtype=jnp.float32) / HEAD_WIDTH)
    angles = places.astype(jnp.float32)[:, None] * frequency[None, :]
    angles = jnp.concatenate([angles, angles], axis=-1)
    return (jnp.cos(angles)[:, None, :], jnp.sin(angles)[:, None, :])

def layout(lengths_row):
    seq_ends = jnp.cumsum(lengths_row).astype(jnp.int32)
    starts = seq_ends - lengths_row.astype(jnp.int32)
    places = jnp.arange(DEVICE_TOKENS, dtype=jnp.int32)
    segment = lax.optimization_barrier(jnp.sum((places[:, None] >= seq_ends[None, :]).astype(jnp.int32), axis=1)).astype(jnp.int32)
    member = segment[:, None] == jnp.arange(SEQ_SLOTS, dtype=jnp.int32)[None, :]
    start_of = lax.optimization_barrier(jnp.sum(jnp.where(member, starts[None, :], 0), axis=1)).astype(jnp.int32)
    return (places - start_of, segment)

def attend_heads(blocks):
    query_tile, key_block, value_block, segment = blocks
    group_width = QUERY_HEADS // KEY_VALUE_HEADS
    grouped_heads = query_tile.reshape(DEVICE_TOKENS, KEY_VALUE_HEADS, group_width, HEAD_WIDTH)
    scores = lower_cast_back(jnp.einsum('qhgd,khd->hgqk', grouped_heads, key_block, precision=highest) * HEAD_WIDTH ** (-0.5))
    places = jnp.arange(DEVICE_TOKENS, dtype=jnp.int32)
    allowed = (segment[:, None] == segment[None, :]) & (places[None, :] <= places[:, None])
    scores = jnp.where(allowed, scores, masked_score)
    weights = jnp.exp(scores - lax.optimization_barrier(jnp.max(scores, axis=-1, keepdims=True)))
    probabilities = lower_cast(weights / lax.optimization_barrier(jnp.sum(weights, axis=-1, keepdims=True)))
    attended = jnp.einsum('hgqk,khd->qhgd', probabilities, value_block, precision=highest)
    return attended.reshape(DEVICE_TOKENS, QUERY_HEADS * HEAD_WIDTH)

def expert_step(second, running, expert_item):
    gate_weight, up_weight, down_weight, share = expert_item
    inputs = lower_cast_back(second)
    gate_act = lower_cast_back(matrix_product(inputs, gate_weight))
    up_act = lower_cast_back(matrix_product(inputs, up_weight))
    hidden = lower_cast(jax.nn.silu(gate_act) * up_act)
    produced = lower_cast(lower_cast_back(matrix_product(hidden, down_weight)))
    return (running + share[:, None] * produced, None)

def forward_layer(params, routes, places, segment_ids):
    tokens, attn_gain, w_query, key_projection, value_projection, w_out, query_gain, key_gain, ffn_gain, w_router, w_gate, w_up, w_down = params
    cosine, sine_table = rope_tables(places.reshape(TOKEN_TOTAL))
    normed_input = lower_cast(rms_scale(tokens, attn_gain))
    query_rows = lower_cast_back(matrix_product(normed_input, w_query)).reshape(TOKEN_TOTAL, QUERY_HEADS, HEAD_WIDTH)
    key = lower_cast_back(matrix_product(normed_input, key_projection)).reshape(TOKEN_TOTAL, KEY_VALUE_HEADS, HEAD_WIDTH)
    value_rows = lower_cast(lower_cast_back(matrix_product(normed_input, value_projection))).reshape(TOKEN_TOTAL, KEY_VALUE_HEADS, HEAD_WIDTH)
    query_rows = lower_cast(rotate(rms_scale(query_rows, query_gain), cosine, sine_table))
    key = lower_cast(rotate(rms_scale(key, key_gain), cosine, sine_table))
    mixed_output = lax.map(jax.checkpoint(attend_heads), (query_rows.reshape(DEVICES, DEVICE_TOKENS, QUERY_HEADS, HEAD_WIDTH), key.reshape(DEVICES, DEVICE_TOKENS, KEY_VALUE_HEADS, HEAD_WIDTH), value_rows.reshape(DEVICES, DEVICE_TOKENS, KEY_VALUE_HEADS, HEAD_WIDTH), segment_ids))
    mixed_output = lower_cast(lower_cast_back(mixed_output.reshape(TOKEN_TOTAL, QUERY_HEADS * HEAD_WIDTH)))
    branch = lower_cast_back(matrix_product(mixed_output, w_out))
    middle = tokens + branch
    second = lower_cast(rms_scale(middle, ffn_gain))
    logits = lower_cast_back(matrix_product(second, w_router))
    picked = jnp.take_along_axis(logits, routes, axis=1)
    picked = jnp.exp(picked - lax.optimization_barrier(jnp.max(picked, axis=1, keepdims=True)))
    gate_share = picked / lax.optimization_barrier(jnp.sum(picked, axis=1, keepdims=True))
    chosen = (routes[:, :, None] == jnp.arange(EXPERTS, dtype=jnp.int32)[None, None, :]).astype(jnp.float32)
    shares = jnp.einsum('tk,tke->et', gate_share, chosen, precision=highest)
    stepper = jax.checkpoint(partial(expert_step, second))
    routed, _ = lax.scan(stepper, jnp.zeros_like(middle), (w_gate, w_up, w_down, shares))
    return middle + routed

def reference(tokens, lengths, routes, attn_gain, w_query, key_projection, value_projection, w_out, query_gain, key_gain, ffn_gain, w_router, w_gate, w_up, w_down, cotangent):
    places, segment_ids = jax.vmap(layout)(lengths)
    params = tuple((value_rows.astype(jnp.float32) for value_rows in (tokens, attn_gain, w_query, key_projection, value_projection, w_out, query_gain, key_gain, ffn_gain, w_router, w_gate, w_up, w_down)))
    result, pullback = jax.vjp(lambda *values: forward_layer(values, routes, places, segment_ids), *params)
    gradients = pullback(cotangent.astype(jnp.float32))
    return (result.astype(jnp.bfloat16), gradients[0], gradients[1], gradients[2], gradients[3], gradients[4], gradients[5], gradients[6], gradients[7], gradients[8], gradients[9], gradients[10], gradients[11], gradients[12])
```

```python
import jax
import jax.numpy as jnp
import ml_dtypes
import numpy as np
from jax import lax
from jax.experimental import pallas as pl
from jax.experimental.pallas import tpu as pltpu
from jax.sharding import PartitionSpec as P

MODEL_WIDTH = 2048
QUERY_HEADS = 32
KEY_VALUE_HEADS = 4
HEAD_WIDTH = 128
TOPK = 8
DEVICE_TOKENS = 128
SEQ_SLOTS = 4

epsilon = 1e-06
rope_base = 1000000.0
masked_score = -1e30
BF = jnp.bfloat16
F32 = jnp.float32


def layout(lengths_row, tok_count, slot_count):
    seq_ends = jnp.cumsum(lengths_row)
    starts = seq_ends - lengths_row
    places = jnp.arange(tok_count, dtype=jnp.int32)
    segment = jnp.sum((places[:, None] >= seq_ends[None, :]).astype(jnp.int32), axis=1)
    member = segment[:, None] == jnp.arange(slot_count, dtype=jnp.int32)[None, :]
    start_of = jnp.sum(jnp.where(member, starts[None, :], 0), axis=1)
    return (places - start_of, segment)


def rope_tables(places, head_size):
    frequency = rope_base ** (-jnp.arange(0, head_size, 2, dtype=jnp.float32) / head_size)
    angles = places.astype(jnp.float32)[..., None] * frequency
    angles = jnp.concatenate([angles, angles], axis=-1)
    return (jnp.cos(angles), jnp.sin(angles))


def rotate(values, cosine, sine_table):
    half_width = values.shape[-1] // 2
    turned = jnp.concatenate([-values[..., half_width:], values[..., :half_width]], axis=-1)
    return values * cosine + turned * sine_table


def unrotate(gradient, cosine, sine_table):
    scaled = gradient * sine_table
    half_width = gradient.shape[-1] // 2
    return gradient * cosine + jnp.concatenate(
        [scaled[..., half_width:], -scaled[..., :half_width]], axis=-1
    )


def norm_back(gradient, unit_value, inverse):
    return inverse * (
        gradient - unit_value * jnp.mean(gradient * unit_value, axis=-1, keepdims=True)
    )


def dot(a, b, dims):
    return lax.dot_general(a, b, (dims, ((), ())), preferred_element_type=F32)


NN = ((1,), (0,))
NT = ((1,), (1,))
TN = ((0,), (0,))
VMEM_BYTES = 63 * 1024 * 1024

MESH = pl.DeviceIdType.MESH
EXTRA = 128
DIAG, XCOL, YCOL, OWN = 0, 1, 2, 3


def remote(src, dst, send, recv, device):
    return pltpu.make_async_remote_copy(
        src_ref=src,
        dst_ref=dst,
        send_sem=send,
        recv_sem=recv,
        device_id=device,
        device_id_type=MESH,
    )


class Place:
    def __init__(self):
        e = lax.axis_index("expert")
        z = lax.axis_index("fsdp")
        self.e, self.z = e, z
        self.core = lax.rem(e, 2)
        self.x = lax.rem(lax.div(e, 2), 2)
        self.y = lax.div(e, 4)
        self.x_near = (e + 2 - 4 * self.x, z)
        self.y_near = (e + 4 - 8 * self.y, z)
        self.sibling = (e + 1 - 2 * self.core, z)
        self.diagonal = (1 - self.y) * 4 + (1 - self.x) * 2 + self.core
        self.partner = z + 1 - 2 * lax.rem(z, 2)
        self.half = lax.div(z, 2)

    def plane(self, k):
        far = jnp.where(self.half == 0, k, 3 - k)
        return jnp.where(k == 0, self.z, jnp.where(k == 1, self.partner, far))

    def turn_at(self, z_there):
        far = jnp.where(z_there < 2, self.z, 3 - self.z)
        return jnp.where(z_there == self.partner, 1, far)

    def column_base(self, q):
        x = self.x if q in (YCOL, OWN) else 1 - self.x
        y = self.y if q in (XCOL, OWN) else 1 - self.y
        return (y * 2 + x) * 2

    def own(self, q):
        return self.column_base(q) + self.core

    def everyone(self):
        return [self.x_near, self.y_near, self.sibling] + [(self.e, self.plane(k)) for k in (1, 2, 3)]


def when(condition):
    def run(body):
        if isinstance(condition, bool):
            if condition:
                body()
        else:
            pl.when(condition)(body)

    return run


def greet(devices):
    barrier = pltpu.get_barrier_semaphore()
    for device in devices:
        pl.semaphore_signal(barrier, inc=1, device_id=device, device_id_type=MESH)


def meet(devices, greeted=False):
    if not greeted:
        greet(devices)
    pl.semaphore_wait(pltpu.get_barrier_semaphore(), len(devices))


class Line:
    def __init__(self, at, block, sems):
        self.at, self.block = at, block
        self.send, self.recv = sems

    def up(self, b):
        block = self.block(b)
        return remote(
            block, block, self.send.at[0, b], self.recv.at[b], (self.at.e, self.at.z + 1)
        )

    def down(self, b):
        block = self.block(b)
        return remote(
            block, block, self.send.at[1, b], self.recv.at[b], (self.at.e, self.at.z - 1)
        )

    def begin(self):
        z = self.at.z

        @pl.when(z < 3)
        def _():
            self.up(z).start()

        @pl.when(z > 0)
        def _():
            self.down(z).start()

    def arrive(self, k):
        z = self.at.z
        b = self.at.plane(k)
        block = self.block(b)
        remote(block, block, self.send.at[0, b], self.recv.at[b], self.at.sibling).wait_recv()

        @pl.when((b < z) & (z < 3))
        def _():
            self.up(b).start()

        @pl.when((b > z) & (z > 0))
        def _():
            self.down(b).start()

    def end(self):
        z = self.at.z
        for b in range(4):

            @pl.when((b <= z) & (z < 3))
            def _():
                self.up(b).wait_send()

            @pl.when((b >= z) & (z > 0))
            def _():
                self.down(b).wait_send()

    @staticmethod
    def semaphores():
        return [pltpu.SemaphoreType.DMA((2, 4)), pltpu.SemaphoreType.DMA((4,))]


class LineSum:
    def __init__(self, at, part, came, sems):
        self.at, self.part, self.came = at, part, came
        self.send, self.recv = sems

    def arrival(self, slot):
        block = self.came.at[slot]
        return remote(block, block, self.send.at[0], self.recv.at[slot], self.at.sibling)

    def copy(self, t):
        z = self.at.z
        up = (t > z).astype(jnp.int32)
        there = z + 2 * up - 1
        slot = jnp.where((t == there) & (up == 0), 4, t)
        return remote(
            self.part.at[t], self.came.at[slot], self.send.at[t], self.recv.at[slot], (self.at.e, there)
        )

    def give(self, t):
        z = self.at.z

        @pl.when(((t > z) & (z > 0)) | ((t < z) & (z < 3)))
        def _():
            self.arrival(t).wait_recv()

            @pl.loop(0, self.part.shape[1] // 32)
            def _(i):
                here = pl.ds(pl.multiple_of(i * 32, 32), 32)
                self.part[t, here] = (
                    self.part[t, here].astype(F32) + self.came[t, here].astype(F32)
                ).astype(BF)

        self.copy(t).start()

    def give_far(self):
        half = self.at.half
        self.give(jnp.where(half == 0, 3, 0))
        self.give(jnp.where(half == 0, 2, 1))

    def give_near(self, early):
        z = self.at.z
        outer = (z == 0) | (z == 3)

        @pl.when(outer if early else jnp.logical_not(outer))
        def _():
            self.give(self.at.partner)

    def wait(self):
        z = self.at.z
        zero = jnp.zeros(self.came.shape[1:], BF)

        @pl.when(z > 0)
        def _():
            self.arrival(z).wait_recv()

        @pl.when(z == 0)
        def _():
            self.came[0] = zero

        @pl.when(z < 3)
        def _():
            self.arrival(4).wait_recv()

        @pl.when(z == 3)
        def _():
            self.came[4] = zero

    def total(self, here):
        return self.came[self.at.z, here].astype(F32) + self.came[4, here].astype(F32)

    def end(self):
        for t in range(4):

            @pl.when(t != self.at.z)
            def _():
                self.copy(t).wait_send()

    @staticmethod
    def semaphores():
        return [pltpu.SemaphoreType.DMA((4,)), pltpu.SemaphoreType.DMA((5,))]


class Gather:
    def __init__(self, at, block, sems, sibling=True):
        self.at, self.block, self.sibling = at, block, sibling
        (self.x_send, self.x_recv, self.y_send, self.y_recv) = sems[:4]
        self.half_send, self.half_recv = sems[4:6]
        if sibling:
            self.sib_send, self.sib_recv = sems[6:8]

    def to_x(self, k):
        block = self.block(k, OWN)
        return remote(block, block, self.x_send.at[k], self.x_recv.at[k], self.at.x_near)

    def to_y(self, k):
        block = self.block(k, OWN)
        return remote(block, block, self.y_send.at[k], self.y_recv.at[k], self.at.y_near)

    def on_y(self, k):
        block = self.block(k, XCOL, 0)
        sem = 2 * k
        return remote(block, block, self.half_send.at[sem], self.half_recv.at[sem], self.at.y_near)

    def on_x(self, k):
        block = self.block(k, YCOL, 1)
        sem = 2 * k + 1
        return remote(block, block, self.half_send.at[sem], self.half_recv.at[sem], self.at.x_near)

    def to_sib(self, k, q):
        block = self.block(k, q)
        sem = 4 * k + q
        return remote(block, block, self.sib_send.at[sem], self.sib_recv.at[sem], self.at.sibling)

    def share(self, k, q):
        if self.sibling:
            self.to_sib(k, q).start()

    def own(self, k):
        self.to_x(k).start()
        self.to_y(k).start()
        self.share(k, OWN)

    def cross(self, k, halves=True):
        self.to_x(k).wait_recv()
        if halves:
            self.on_y(k).start()
        self.share(k, XCOL)
        self.to_y(k).wait_recv()
        if halves:
            self.on_x(k).start()
        self.share(k, YCOL)

    def diag(self, k):
        self.on_y(k).wait_recv()
        self.on_x(k).wait_recv()
        self.share(k, DIAG)

    def ready(self, k, q):
        self.to_sib(k, q).wait_recv()

    def end(self, k, halves=True):
        self.to_x(k).wait_send()
        self.to_y(k).wait_send()
        if halves:
            self.on_x(k).wait_send()
            self.on_y(k).wait_send()
        for q in range(4) if self.sibling else ():
            self.to_sib(k, q).wait_send()

    @staticmethod
    def semaphores(sibling=True):
        dma = pltpu.SemaphoreType.DMA
        return [dma((4,))] * 4 + [dma((8,))] * 2 + [dma((16,))] * 2 * sibling


def expert_kernel(
    second_ref,
    cot_ref,
    gate_ref,
    up_ref,
    down_ref,
    sums_ref,
    gate_grad_ref,
    up_grad_ref,
    down_grad_ref,
    kept_ref,
    held,
    part,
    diag_a,
    diag_b,
    diag_z,
    x_whole,
    y_whole,
    z_part,
    pair_part,
    cot_tile,
    gate_up,
    down,
    acts,
    back,
    gate_tile,
    hidden_tile,
    kept_tile,
    grad_tile,
    widen,
    narrow,
    load_sem,
    gift_send,
    gift_recv,
    cot_sem,
    kept_sem,
    grad_sem,
    reload_sem,
    over_sem,
    red_send,
    red_recv,
    zr_send,
    zr_recv,
    pair_send,
    pair_recv,
    give_send,
    give_recv,
    give_ready,
    *sems,
):
    at = Place()
    rows = second_ref.shape[0]
    pair, quad = 2 * rows, 4 * rows
    total_rows, carried = held.shape
    model = cot_ref.shape[1]
    wide = down.shape[0]
    own_wide = wide // 2
    units = wide // 4
    half = rows // 2
    partner = (at.e, at.partner)
    experts_all = 16
    loads, gifts = [], []
    for i, (ref, held_weights, first) in enumerate(
        ((gate_ref, gate_up, 0), (up_ref, gate_up, wide), (down_ref, down, 0))
    ):
        here = pl.ds(pl.multiple_of(first + at.core * own_wide, own_wide), own_wide)
        loads.append(pltpu.make_async_copy(ref, held_weights.at[here], load_sem.at[i]))
        gifts.append(
            remote(ref, held_weights.at[here], gift_send.at[i], gift_recv.at[i], at.sibling)
        )
    for copy in loads:
        copy.start()

    def named(shape, unit_axis):
        unit = lax.broadcasted_iota(jnp.int32, shape, unit_axis)
        lane = lax.broadcasted_iota(jnp.int32, shape, 1 - unit_axis)
        expert = at.e // 2 * 4
        for i in (1, 2, 3):
            expert = expert + (unit >= i * units).astype(jnp.int32)
        return ((lane == expert) | (lane == expert + experts_all)).astype(F32).astype(BF)

    widen[...] = named((EXTRA, wide), 1)
    narrow[...] = named((wide, EXTRA), 0)
    meet(at.everyone())
    for copy in gifts:
        copy.start()

    def side_first(k, side):
        return (at.plane(k) * 4 + (at.y if side else 1 - at.y) * 2) * rows

    def side_rows(k, side):
        return pl.ds(pl.multiple_of(side_first(k, side), pair), pair)

    def block(k, q, i=None):
        first, count = (0, rows) if i is None else (i * half, half)
        first = (at.plane(k) * 4 + at.column_base(q) // 2) * rows + first
        return held.at[pl.ds(pl.multiple_of(first, half), count)]

    def line_block(b):
        first = (b * 4 + at.column_base(OWN) // 2) * rows
        return held.at[pl.ds(pl.multiple_of(first, rows), rows)]

    line = Line(at, line_block, sems[:2])
    gather = Gather(at, block, sems[2:], sibling=False)
    first_row = (at.z * 4 + at.column_base(OWN) // 2) * rows
    held[pl.ds(pl.multiple_of(first_row, rows), rows)] = second_ref[...]
    line.begin()
    gather.own(0)

    def over_z(k):
        there = block(k, DIAG)
        return remote(there, there, over_sem.at[0], over_sem.at[1], partner)

    def cot_copy(k, side):
        return pltpu.make_async_copy(cot_ref.at[side_rows(k, side)], cot_tile, cot_sem)

    def kept_copy(k, side):
        return pltpu.make_async_copy(kept_tile, kept_ref.at[:, side_rows(k, side)], kept_sem)

    def compute(r, k, side, following):
        here = side_rows(k, side)
        acts[...] = lax.dot_general(
            held[here, :model], gate_up[...], (NT, ((), ())), preferred_element_type=F32
        )
        cot_copy(k, side).wait()
        back[...] = lax.dot_general(
            cot_tile[...], down[...], (NT, ((), ())), preferred_element_type=F32
        )
        following()

        @when(not (isinstance(r, int) and r == 0 and side == 1))
        def _():
            kept_copy(k, side).wait()

        out_first = r * quad + side * pair
        for i in range(pair // rows):
            strip_rows = slice(i * rows, (i + 1) * rows)
            first = side_first(k, side) + i * rows
            share_rows = held[pl.ds(pl.multiple_of(first, rows), rows), model:]
            gate_act, up_act = acts[strip_rows, :wide], acts[strip_rows, wide:]
            raw_back = back[strip_rows]
            share = jnp.dot(share_rows, widen[...], preferred_element_type=F32)
            sigmoid = 1.0 / (1.0 + jnp.exp(-gate_act))
            silu = gate_act * sigmoid
            hidden = silu * up_act
            product = hidden * raw_back
            high = product.astype(BF)
            low = (product - high.astype(F32)).astype(BF)
            share_grad = jnp.dot(high, narrow[...], preferred_element_type=F32) + jnp.dot(
                low, narrow[...], preferred_element_type=F32
            )
            lane = lax.broadcasted_iota(jnp.int32, share_grad.shape, 1)
            rounded = share_grad.astype(BF).astype(F32)
            share_grad = jnp.where(lane < experts_all, rounded, share_grad - rounded)
            hidden_low = (share * hidden).astype(BF)
            hidden_grad = share * raw_back
            gate_grad = (
                hidden_grad * up_act * sigmoid * (1.0 + gate_act * (1.0 - sigmoid))
            ).astype(BF)
            up_grad = (hidden_grad * silu).astype(BF)
            gate_tile[strip_rows, :wide] = gate_grad
            gate_tile[strip_rows, wide:] = up_grad
            hidden_tile[strip_rows] = hidden_low
            kept_tile[:wide, strip_rows] = gate_grad.T
            kept_tile[wide : 2 * wide, strip_rows] = up_grad.T
            kept_tile[2 * wide :, strip_rows] = hidden_low.T
            out_rows = pl.ds(pl.multiple_of(out_first + i * rows, rows), rows)
            part[out_rows, 2 * model :] = share_grad.astype(BF)
        kept_copy(k, side).start()
        there = pl.ds(pl.multiple_of(out_first, pair), pair)
        step = 512
        for start in range(0, model, step):
            part[there, start : start + step] = jnp.dot(
                hidden_tile[...], down[:, start : start + step], preferred_element_type=F32
            ).astype(BF)
            part[there, model + start : model + start + step] = jnp.dot(
                gate_tile[...], gate_up[:, start : start + step], preferred_element_type=F32
            ).astype(BF)

    def part_row(r, q, first=0):
        x = at.x if q in (YCOL, OWN) else 1 - at.x
        return r * quad + (pair if q in (XCOL, OWN) else 0) + x * rows + first

    def part_rows(r, q, first, count):
        return pl.ds(pl.multiple_of(part_row(r, q, first), min(count, half)), count)

    def half_a(r):
        src = part.at[part_rows(r, DIAG, 0, half)]
        return remote(src, diag_a.at[r % 2], red_send.at[0, r], red_recv.at[0, r], at.y_near)

    def half_b(r):
        src = part.at[part_rows(r, DIAG, half, half)]
        return remote(src, diag_b.at[r % 2], red_send.at[1, r], red_recv.at[1, r], at.x_near)

    def x_copy(r):
        src = part.at[part_rows(r, XCOL, 0, rows)]
        return remote(src, x_whole.at[r % 2], red_send.at[2, r], red_recv.at[2, r], at.x_near)

    def y_copy(r):
        src = part.at[part_rows(r, YCOL, 0, rows)]
        return remote(src, y_whole.at[r % 2], red_send.at[3, r], red_recv.at[3, r], at.y_near)

    def diag_over():
        src = part.at[part_rows(0, DIAG, 0, rows)]
        return remote(src, diag_z, red_send.at[0, 0], red_recv.at[0, 0], partner)

    strip = 32

    def by_strips(count, body):
        @pl.loop(0, count // strip)
        def _(i):
            body(pl.multiple_of(i * strip, strip))

    def reduce_diag(r):
        @when(r == 3)
        def _():
            diag_over().wait_recv()

            def body(row):
                here = part_rows(r, DIAG, row, strip)
                part[here] = (
                    part[here].astype(F32) + diag_z[pl.ds(row, strip)].astype(F32)
                ).astype(BF)

            by_strips(rows, body)

        @when(r == 0)
        def _():
            diag_over().start()

        @when(r > 0)
        def _():
            half_a(r).start()
            half_b(r).start()

    def reduce_x(r):
        @when(r > 0)
        def _():
            half_a(r).wait_recv()

            def body(row):
                here = part_rows(r, XCOL, row, strip)
                part[here] = (
                    part[here].astype(F32) + diag_a[r % 2, pl.ds(row, strip)].astype(F32)
                ).astype(BF)

            by_strips(half, body)

        x_copy(r).start()

    def reduce_y(r):
        @when(r > 0)
        def _():
            half_b(r).wait_recv()

            def body(row):
                here = part_rows(r, YCOL, half + row, strip)
                part[here] = (
                    part[here].astype(F32) + diag_b[r % 2, pl.ds(row, strip)].astype(F32)
                ).astype(BF)

            by_strips(half, body)

        y_copy(r).start()

    inner = (at.z == 1) | (at.z == 2)

    def near_copy():
        src = part.at[part_rows(0, OWN, 0, rows)]
        return remote(src, z_part.at[0], zr_send.at[0], zr_recv.at[0], partner)

    def pair_copy(r):
        block = pair_part.at[r - 1]
        return remote(block, block, pair_send.at[r - 1], pair_recv.at[r - 1], partner)

    def far_copy(r):
        there = at.plane(r + 1)
        return remote(
            pair_part.at[r - 1], z_part.at[1], zr_send.at[r], zr_recv.at[1], (at.e, there)
        )

    def pass_on(r):
        @pl.when(inner)
        def _():
            pair_copy(r).wait_recv()

            def body(row):
                here = pl.ds(row, strip)
                pair_part[r - 1, here] = (
                    pair_part[r - 1, here].astype(F32)
                    + part[part_rows(r, OWN, row, strip)].astype(F32)
                ).astype(BF)

            by_strips(rows, body)
            far_copy(r).start()

    def reduce_own(r):
        x_copy(r).wait_recv()
        y_copy(r).wait_recv()

        def total(row):
            here = pl.ds(row, strip)
            return (
                part[part_rows(r, OWN, row, strip)].astype(F32)
                + x_whole[r % 2, here].astype(F32)
                + y_whole[r % 2, here].astype(F32)
            )

        @when(r == 3)
        def _():
            near_copy().wait_recv()
            block = z_part.at[1]
            remote(block, block, zr_send.at[0], zr_recv.at[1], at.sibling).wait_recv()

            def body(row):
                here = pl.ds(row, strip)
                sums_ref[here] = total(row) + (
                    z_part[0, here].astype(F32) + z_part[1, here].astype(F32)
                )

            by_strips(rows, body)

        def keep(row):
            part[part_rows(r, OWN, row, strip)] = total(row).astype(BF)

        def lay_out(row):
            pair_part[r - 1, pl.ds(row, strip)] = total(row).astype(BF)

        @when(r == 0)
        def _():
            by_strips(rows, keep)
            near_copy().start()

        @when(between(r, 1, 2))
        def _():
            @pl.when(inner)
            def _():
                by_strips(rows, keep)

            @pl.when(jnp.logical_not(inner))
            def _():
                by_strips(rows, lay_out)
                pair_copy(r).start()

    def far_rows(k):
        line.arrive(k)
        gather.own(k)

    cot_copy(1, 1).start()
    line.arrive(1)
    gather.own(1)

    @pl.when(inner)
    def _():
        far_rows(2)

    gather.cross(0)
    gather.cross(1, halves=False)

    @pl.when(inner)
    def _():
        far_rows(3)

    for copy in loads + gifts:
        copy.wait()
    compute(0, 1, 1, lambda: cot_copy(1, 0).start())
    reduce_x(0)
    gather.diag(0)
    over_z(0).start()

    @pl.when(jnp.logical_not(inner))
    def _():
        far_rows(2)

    over_z(1).wait_recv()
    compute(0, 1, 0, lambda: cot_copy(2, 0).start())
    reduce_y(0)
    reduce_diag(0)

    @pl.when(jnp.logical_not(inner))
    def _():
        far_rows(3)

    gather.cross(2)
    gather.diag(2)
    compute(1, 2, 0, lambda: cot_copy(2, 1).start())
    reduce_diag(1)
    gather.cross(3)

    @pl.loop(1, 3)
    def _(r):
        k, later = r + 1, lax.rem(r + 2, 4)
        compute(r, k, 1, lambda: cot_copy(later, 0).start())
        reduce_own(r - 1)

        @pl.when(r == 1)
        def _():
            gather.diag(3)

        compute(r + 1, later, 0, lambda: cot_copy(later, 1).start())
        reduce_x(r)
        reduce_y(r)

        @pl.when(r == 2)
        def _():
            pass_on(1)

        reduce_diag(r + 1)

    compute(3, 0, 1, lambda: None)

    line.end()
    over_z(0).wait_send()
    diag_over().wait_send()
    near_copy().wait_send()
    x_copy(0).wait_send()
    y_copy(0).wait_send()
    for copy in (half_a(1), half_b(1), x_copy(1), y_copy(1)):
        copy.wait_send()
    pl.semaphore_signal(give_ready, inc=1, device_id=at.sibling, device_id_type=MESH)
    for k in range(4):
        gather.end(k, halves=k != 1)
    kept_copy(0, 1).wait()
    turned = [
        pltpu.make_async_copy(kept_ref.at[pl.ds(0, 2 * wide)], gate_up, load_sem.at[0]),
        pltpu.make_async_copy(kept_ref.at[pl.ds(2 * wide, wide)], down, load_sem.at[1]),
    ]
    for copy in turned:
        copy.start()
    step = 256
    chunks = model // step
    mine, theirs = at.core * own_wide, (1 - at.core) * own_wide

    def lanes_of(n):
        return pl.ds(pl.multiple_of(n * step, step), step)

    def turned_rows(first):
        return pl.ds(pl.multiple_of(first, own_wide), own_wide)

    def given(i, first, size):
        return part.at[pl.ds(0, own_wide), pl.ds(pl.multiple_of(i * model + first, step), size)]

    def taken(i, first, size):
        return part.at[pl.ds(quad, own_wide), pl.ds(pl.multiple_of(i * model + first, step), size)]

    def give_copies(n):
        first, size = n % 2 * (model // 2), model // 2
        return [
            remote(
                given(i, first, size),
                taken(i, first, size),
                give_send.at[n, i],
                give_recv.at[n, i],
                at.sibling,
            )
            for i in ((0, 1) if n < 2 else (0,))
        ]

    def gate_out(n):
        slot = lax.rem(n, 2)
        return [
            pltpu.make_async_copy(
                grad_tile.at[slot, pl.ds(i * own_wide, own_wide)],
                ref.at[:, lanes_of(n)],
                grad_sem.at[slot, i],
            )
            for i, ref in enumerate((gate_grad_ref, up_grad_ref))
        ]

    def down_out(n):
        slot = lax.rem(n, 2)
        return pltpu.make_async_copy(
            grad_tile.at[slot, pl.ds(0, own_wide)],
            down_grad_ref.at[:, lanes_of(n)],
            grad_sem.at[slot, 0],
        )

    def reload(n):
        return pltpu.make_async_copy(
            cot_ref.at[:, lanes_of(n)], held.at[:, lanes_of(n)], reload_sem.at[n]
        )

    def gate_up_chunk(first, i, n):
        return jnp.dot(
            gate_up[turned_rows(i * wide + first)],
            held[:, lanes_of(n)],
            preferred_element_type=F32,
        )

    def down_chunk(first, n):
        return jnp.dot(
            down[turned_rows(first)], held[:, lanes_of(n)], preferred_element_type=F32
        )

    def in_half(n, body):
        half_chunks = chunks // 2
        pl.loop(n % 2 * half_chunks, (n % 2 + 1) * half_chunks)(body)

    for copy in turned:
        copy.wait()
    for part_of in (0, 1):

        def give_gate_up(n):
            for i in (0, 1):
                given(i, n * step, step)[...] = gate_up_chunk(theirs, i, n).astype(BF)

        in_half(part_of, give_gate_up)
        if part_of == 0:
            pl.semaphore_wait(give_ready, 1)
        for copy in give_copies(part_of):
            copy.start()

    reduce_own(2)
    for part_of in (0, 1):
        for copy in give_copies(part_of):
            copy.wait_recv()

        def own_gate_up(n):
            @pl.when(n >= 2)
            def _():
                for copy in gate_out(n):
                    copy.wait()

            for i in (0, 1):
                grad_tile[lax.rem(n, 2), i * own_wide : (i + 1) * own_wide] = gate_up_chunk(
                    mine, i, n
                ) + taken(i, n * step, step)[...].astype(F32)
            for copy in gate_out(n):
                copy.start()
            reload(n).start()

        in_half(part_of, own_gate_up)

    pl.semaphore_signal(give_ready, inc=1, device_id=at.sibling, device_id_type=MESH)
    reduce_x(3)
    reduce_y(3)
    pass_on(2)
    for part_of in (0, 1):
        for copy in give_copies(part_of):
            copy.wait_send()
    for part_of in (2, 3):

        def give_down(n):
            reload(n).wait()
            given(0, n * step, step)[...] = down_chunk(theirs, n).astype(BF)

        in_half(part_of, give_down)
        if part_of == 2:
            pl.semaphore_wait(give_ready, 1)
        for copy in give_copies(part_of):
            copy.start()

    for n in (0, 1):
        for copy in gate_out(n):
            copy.wait()
    for part_of in (2, 3):
        for copy in give_copies(part_of):
            copy.wait_recv()

        def own_down(n):
            @pl.when(n >= 2)
            def _():
                down_out(n).wait()

            grad_tile[lax.rem(n, 2), :own_wide] = down_chunk(mine, n) + taken(0, n * step, step)[
                ...
            ].astype(F32)
            down_out(n).start()

        in_half(part_of, own_down)

    reduce_own(3)
    for n in (0, 1):
        down_out(n).wait()

    for n in (2, 3):
        for copy in give_copies(n):
            copy.wait_send()
    for r in (2, 3):
        for copy in (half_a(r), half_b(r), x_copy(r), y_copy(r)):
            copy.wait_send()
    for r in (1, 2):

        @pl.when(inner)
        def _():
            far_copy(r).wait_send()

        @pl.when(jnp.logical_not(inner))
        def _():
            pair_copy(r).wait_send()


def experts_in_one(second_wide, cot_all, gate, up, down):
    rows, carried = second_wide.shape
    total_rows, model = cot_all.shape
    wide = 2 * down.shape[0]
    pair, half = 2 * rows, rows // 2
    both = 2 * model + EXTRA
    vmem = pl.BlockSpec(memory_space=pltpu.VMEM)
    hbm = pl.BlockSpec(memory_space=pl.ANY)
    dma = pltpu.SemaphoreType.DMA
    shape = jax.ShapeDtypeStruct
    return pl.pallas_call(
        expert_kernel,
        out_shape=(
            shape((rows, both), F32),
            shape((wide // 2, model), F32),
            shape((wide // 2, model), F32),
            shape((wide // 2, model), F32),
            shape((3 * wide, total_rows), BF),
        ),
        in_specs=[vmem, hbm, hbm, hbm, hbm],
        out_specs=(vmem, hbm, hbm, hbm, hbm),
        scratch_shapes=[
            pltpu.VMEM((total_rows, carried), BF),
            pltpu.VMEM((16 * rows, both), BF),
            pltpu.VMEM((2, half, both), BF),
            pltpu.VMEM((2, half, both), BF),
            pltpu.VMEM((rows, both), BF),
            pltpu.VMEM((2, rows, both), BF),
            pltpu.VMEM((2, rows, both), BF),
            pltpu.VMEM((2, rows, both), BF),
            pltpu.VMEM((2, rows, both), BF),
            pltpu.VMEM((pair, model), BF),
            pltpu.VMEM((2 * wide, model), BF),
            pltpu.VMEM((wide, model), BF),
            pltpu.VMEM((pair, 2 * wide), F32),
            pltpu.VMEM((pair, wide), F32),
            pltpu.VMEM((pair, 2 * wide), BF),
            pltpu.VMEM((pair, wide), BF),
            pltpu.VMEM((3 * wide, pair), BF),
            pltpu.VMEM((2, wide, 256), F32),
            pltpu.VMEM((EXTRA, wide), BF),
            pltpu.VMEM((wide, EXTRA), BF),
            dma((3,)),
            dma((3,)),
            dma((3,)),
            dma,
            dma,
            dma((2, 2)),
            dma((model // 256,)),
            dma((2,)),
            dma((4, 4)),
            dma((4, 4)),
            dma((3,)),
            dma((2,)),
            dma((2,)),
            dma((2,)),
            dma((4, 2)),
            dma((4, 2)),
            pltpu.SemaphoreType.REGULAR,
            *Line.semaphores(),
            *Gather.semaphores(False),
        ],
        compiler_params=pltpu.CompilerParams(
            collective_id=0, has_side_effects=True, vmem_limit_bytes=VMEM_BYTES
        ),
        cost_estimate=pl.CostEstimate(
            flops=2 * total_rows * model * wide * 9,
            bytes_accessed=8 * total_rows * model,
            transcendentals=total_rows * wide,
        ),
    )(second_wide, cot_all, gate, up, down)


def between(r, low, high):
    if isinstance(r, int):
        return low <= r <= high
    return (r >= low) & (r <= high)


class Tree:
    def __init__(self, at, refs, sems):
        (self.part, self.from_sib, self.diag_sum, self.x_sum, self.y_sum) = refs[:5]
        (self.diag_a, self.diag_b, self.x_whole, self.y_whole) = refs[5:]
        self.part_send, self.part_recv, self.send, self.recv = sems
        self.at = at
        self.rows = self.diag_sum.shape[0]
        self.half = self.rows // 2
        self.strip = 32

    def part_copy(self, q):
        return remote(
            self.part.at[q, 1 - self.at.core],
            self.from_sib.at[q],
            self.part_send.at[q],
            self.part_recv.at[q],
            self.at.sibling,
        )

    def half_a(self):
        there = self.diag_sum.at[pl.ds(0, self.half)]
        return remote(there, self.diag_a, self.send.at[0], self.recv.at[0], self.at.y_near)

    def half_b(self):
        there = self.diag_sum.at[pl.ds(self.half, self.half)]
        return remote(there, self.diag_b, self.send.at[1], self.recv.at[1], self.at.x_near)

    def x_copy(self):
        return remote(self.x_sum, self.x_whole, self.send.at[2], self.recv.at[2], self.at.x_near)

    def y_copy(self):
        return remote(self.y_sum, self.y_whole, self.send.at[3], self.recv.at[3], self.at.y_near)

    def strips(self, first, count, body):
        strip = self.strip

        @pl.loop(first // strip, (first + count) // strip)
        def _(i):
            body(pl.ds(pl.multiple_of(i * strip, strip), strip), i)

    def chip_sum(self, q, here):
        return self.part[q, self.at.core, here].astype(F32) + self.from_sib[q, here].astype(F32)

    def do_diag(self):
        self.part_copy(DIAG).wait_recv()

        def body(here, i):
            self.diag_sum[here] = self.chip_sum(DIAG, here).astype(BF)

        self.strips(0, self.rows, body)
        self.half_a().start()
        self.half_b().start()

    def do_x(self):
        self.part_copy(XCOL).wait_recv()
        self.half_a().wait_recv()

        def with_half(here, i):
            self.x_sum[here] = (
                self.chip_sum(XCOL, here) + self.diag_a[here].astype(F32)
            ).astype(BF)

        def alone(here, i):
            self.x_sum[here] = self.chip_sum(XCOL, here).astype(BF)

        self.strips(0, self.half, with_half)
        self.strips(self.half, self.half, alone)
        self.x_copy().start()

    def do_y(self):
        self.part_copy(YCOL).wait_recv()
        self.half_b().wait_recv()

        def alone(here, i):
            self.y_sum[here] = self.chip_sum(YCOL, here).astype(BF)

        def with_half(here, i):
            low = pl.ds(pl.multiple_of(i * self.strip - self.half, self.strip), self.strip)
            self.y_sum[here] = (self.chip_sum(YCOL, here) + self.diag_b[low].astype(F32)).astype(BF)

        self.strips(0, self.half, alone)
        self.strips(self.half, self.half, with_half)
        self.y_copy().start()

    def do_own(self, result):
        self.part_copy(OWN).wait_recv()
        self.x_copy().wait_recv()
        self.y_copy().wait_recv()

        def body(here, i):
            result[here] = (
                self.chip_sum(OWN, here)
                + self.x_whole[here].astype(F32)
                + self.y_whole[here].astype(F32)
            ).astype(BF)

        self.strips(0, self.rows, body)

    def drain(self):
        for q in range(4):
            self.part_copy(q).wait_send()
        for copy in (self.half_a(), self.half_b(), self.x_copy(), self.y_copy()):
            copy.wait_send()

    @staticmethod
    def buffers(rows, width):
        piece = pltpu.VMEM((rows, width), BF)
        half = pltpu.VMEM((rows // 2, width), BF)
        return [
            pltpu.VMEM((4, 2, rows, width), BF),
            pltpu.VMEM((4, rows, width), BF),
            piece,
            piece,
            piece,
            half,
            half,
            piece,
            piece,
        ]

    @staticmethod
    def semaphores():
        return [pltpu.SemaphoreType.DMA((4,))] * 4


class Spread:
    def __init__(self, at, own, out, sems, first=0):
        self.at, self.own, self.out, self.first = at, own, out, first
        self.send, self.recv, self.local = sems
        self.rows = own.shape[0]
        self.stride = out.shape[0] // 8
        self.e_x, self.e_y, self.e_d = at.x_near[0], at.y_near[0], at.diagonal

    def place(self, slot, first=0, rows=None):
        row = slot * self.stride + self.first + first
        rows = rows or self.rows
        return self.out.at[pl.ds(pl.multiple_of(row, rows), rows)]

    def to(self, src, slot, device, sem):
        return remote(src, self.place(slot), self.send.at[sem], self.recv.at[sem], device)

    def own_copies(self):
        e = self.at.e
        return (
            self.to(self.own, e, self.at.x_near, 0),
            self.to(self.own, e, self.at.y_near, 1),
            self.to(self.own, e, self.at.sibling, 2),
        )

    def here(self):
        return pltpu.make_async_copy(self.own, self.place(self.at.e), self.local)

    def half_copy(self, slot, first, device, sem):
        there = self.place(slot, first, self.rows // 2)
        return remote(there, there, self.send.at[sem], self.recv.at[sem], device)

    def cross_copies(self):
        return (
            self.half_copy(self.e_x, 0, self.at.y_near, 3),
            self.half_copy(self.e_y, self.rows // 2, self.at.x_near, 4),
            self.to(self.place(self.e_x), self.e_x, self.at.sibling, 5),
            self.to(self.place(self.e_y), self.e_y, self.at.sibling, 6),
        )

    def diag_copy(self):
        return self.to(self.place(self.e_d), self.e_d, self.at.sibling, 7)

    def begin(self):
        for copy in self.own_copies():
            copy.start()
        self.here().start()

    def cross(self):
        x, y, s = self.own_copies()
        x.wait_recv()
        y.wait_recv()
        for copy in self.cross_copies():
            copy.start()
        s.wait_recv()

    def diag(self):
        a, b, s, t = self.cross_copies()
        a.wait_recv()
        b.wait_recv()
        self.diag_copy().start()
        s.wait_recv()
        t.wait_recv()

    def end(self):
        self.diag_copy().wait()
        for copy in self.own_copies() + self.cross_copies():
            copy.wait_send()
        self.here().wait()

    @staticmethod
    def semaphores():
        dma = pltpu.SemaphoreType.DMA
        return [dma((8,)), dma((8,)), dma]


def swap(v):
    return pltpu.roll(v, v.shape[-1] // 2, v.ndim - 1)


def fold(v):
    return jnp.sum(v.reshape(v.shape[0] // 8, 8, v.shape[1]), axis=0)


def split_rows(v):
    high = v.astype(BF)
    return jnp.concatenate([v, v - high.astype(F32)], axis=0).astype(BF)


def back_kernel(
    middle_ref,
    share_ref,
    cot_ref,
    router_ref,
    small_ref,
    cos_ref,
    sin_ref,
    second_ref,
    place_ref,
    sums_ref,
    w_out_ref,
    w_cols_ref,
    mixed_ref,
    normed_ref,
    raw_ref,
    prob_ref,
    dnormed_ref,
    block_out_ref,
    middle_grad_ref,
    out_grad_ref,
    cols_grad_ref,
    w_out_held,
    w_cols_held,
    mixed_held,
    normed_held,
    raw_held,
    prob_held,
    held,
    raw_grad,
    left,
    right,
    share_sum,
    router_wide,
    rows_out,
    rows_in,
    gain_total,
    head_total,
    out_total,
    *rest,
):
    at = Place()
    rows, model = middle_ref.shape
    quarter = model // 4
    experts_all = router_ref.shape[1]
    own_part = dnormed_ref
    pair = 2 * rows
    width = HEAD_WIDTH
    heads = w_out_ref.shape[0] // width
    q_cols = heads * width
    cols = w_cols_ref.shape[1]
    count = model // 4 // 8
    scale = HEAD_WIDTH ** (-0.5)
    rest = list(rest)

    def grab(count):
        got, rest[:] = rest[:count], rest[count:]
        return got

    cols_totals, cols_alls = grab(2), grab(2)
    out_tree = Tree(at, grab(9), grab(4))
    cols_trees = [Tree(at, grab(9), grab(4)) for _ in (0, 1)]
    out_spread = Spread(at, out_total, out_grad_ref, grab(3))
    cols_spreads = [
        Spread(at, cols_alls[i], cols_grad_ref, grab(3), i * (count // 2)) for i in (0, 1)
    ]

    def line_block(b):
        return held.at[pl.ds(pl.multiple_of(b * rows, rows), rows)]

    line = Line(at, line_block, grab(2))
    sums = LineSum(at, rows_out, rows_in, grab(2))
    outer = (at.z == 0) | (at.z == 3)
    ex_send, ex_recv, ex_local, load_sem, sum_sem = grab(5)
    loads = [
        pltpu.make_async_copy(src, dst, load_sem.at[i])
        for i, (src, dst) in enumerate(
            (
                (w_out_ref, w_out_held),
                (raw_ref, raw_held),
                (w_cols_ref, w_cols_held),
                (normed_ref, normed_held),
                (prob_ref, prob_held),
                (mixed_ref, mixed_held),
            )
        )
    ]

    def sum_copy(j):
        lanes = pl.ds(pl.multiple_of(j * EXTRA, EXTRA), EXTRA)
        return pltpu.make_async_copy(sums_ref.at[:, lanes], prob_held.at[j], sum_sem.at[0])

    greet(at.everyone())
    columns = 2 * model // EXTRA
    share_copy = pltpu.make_async_copy(
        sums_ref.at[:, pl.ds(2 * model, EXTRA)], share_sum, sum_sem.at[1]
    )
    share_copy.start()

    @pl.loop(0, columns)
    def _(j):
        sum_copy(j).start()

    for copy in loads[:4]:
        copy.start()

    row_id = lax.broadcasted_iota(jnp.int32, right.shape, 0)
    lane_id = lax.broadcasted_iota(jnp.int32, right.shape, 1)
    chosen = (lane_id == experts_all) & (row_id >= rows) & (row_id < 2 * rows)
    for i in (0, 1, 2):
        first = 2 * rows + 16 * i
        chosen = chosen | (
            (lane_id == experts_all + 1 + i) & (row_id >= first) & (row_id < first + 16)
        )
    right[...] = chosen.astype(F32).astype(BF)
    router_wide[...] = jnp.zeros_like(router_wide)
    left[pl.ds(0, rows)] = second_ref[:, :model]
    left[pl.ds(2 * rows, rows)] = jnp.zeros((rows, model), BF)
    lane = lax.broadcasted_iota(jnp.int32, (rows, EXTRA), 1)
    share = share_ref[...]
    share_copy.wait()
    dshare = share_sum[...]
    dshare = dshare + pltpu.roll(dshare, EXTRA - experts_all, 1)
    weighed = jnp.where(lane < experts_all, share * dshare, 0.0)
    mean_share = jnp.sum(weighed, axis=-1, keepdims=True)
    logit_grad = jnp.where(lane < experts_all, share * (dshare - mean_share), 0.0).astype(BF)
    right[pl.ds(0, rows)] = logit_grad
    middle = middle_ref[...]
    inverse = lax.rsqrt(jnp.mean(middle * middle, axis=-1, keepdims=True) + epsilon)
    mean = jnp.zeros((rows, 1), F32)

    @pl.loop(0, columns)
    def _(j):
        sum_copy(j).wait()

    for j in range(4):
        router_wide[:experts_all, j * quarter : (j + 1) * quarter] = router_ref[j]
    for j in range(model // EXTRA):
        lanes = slice(j * EXTRA, (j + 1) * EXTRA)
        block_out_ref[:, lanes] = (middle[:, lanes] + prob_held[j]).astype(BF)
        second_grad = prob_held[model // EXTRA + j] + dot(logit_grad, router_wide[:, lanes], NN)
        unit = middle[:, lanes] * inverse
        left[rows : 2 * rows, lanes] = (second_grad * unit).astype(BF)
        of = j * EXTRA % quarter
        scaled = second_grad * small_ref[j * EXTRA // quarter, 1:2, of : of + EXTRA]
        middle_grad_ref[:, lanes] = scaled
        mean += jnp.sum(scaled * unit, axis=-1, keepdims=True)
    loads[4].start()
    loads[5].start()
    mean = mean / model
    middle_grad = cot_ref[...].astype(F32) + inverse * (
        middle_grad_ref[...] - middle * inverse * mean
    )
    middle_grad_ref[...] = middle_grad
    head_gains = small_ref[0, 2:3, :] + small_ref[1, 2:3, :]
    head_gains += small_ref[2, 2:3, :] + small_ref[3, 2:3, :]

    held[pl.ds(pl.multiple_of(at.z * rows, rows), rows)] = middle_grad.astype(BF)
    meet(at.everyone(), greeted=True)
    line.begin()
    gain_total[...] = jnp.zeros_like(gain_total)
    head_total[...] = jnp.zeros_like(head_total)

    def attention(far):
        first = 2 * (1 - at.half if far else at.half)
        both = pl.ds(pl.multiple_of(first * rows, pair), pair)
        mixed_grads = lax.dot_general(
            held[both, :], w_out_held[...], (NT, ((), ())), preferred_element_type=F32
        ).astype(BF)
        for i in (0, 1):
            heads_back(first + i, mixed_grads[i * rows : (i + 1) * rows])
            if not far and i == 0:

                @pl.when(jnp.logical_not(outer))
                def _():
                    line.arrive(3)

            if far and i == 0:
                out_tree.do_x()
                out_tree.do_y()
        step = 512
        for start in range(0, model, step):
            lanes = slice(start, start + step)
            part = lax.dot_general(
                raw_grad[both, :],
                w_cols_held[start : start + step, :],
                (NT, ((), ())),
                preferred_element_type=F32,
            )
            gain_total[:, lanes] += fold(part * normed_held[both, lanes].astype(F32))
            if not far:
                own_part[:, lanes] = jnp.where(at.z % 2 == 0, part[:rows], part[rows:])
            rows_out[first, :, lanes] = part[:rows].astype(BF)
            rows_out[first + 1, :, lanes] = part[rows:].astype(BF)
        if not far:
            sums.give_near(True)
        else:

            @pl.when(outer)
            def _():
                sums.give_far()

    def heads_back(b, mixed_grad):
        here = pl.ds(pl.multiple_of(b * rows, rows), rows)
        cosine, sine = cos_ref[here, :], sin_ref[here, :]

        def unit_of(v):
            inverse = lax.rsqrt(jnp.mean(v * v, axis=-1, keepdims=True) + epsilon)
            return v * inverse, inverse

        def low_of(unit, gain):
            scaled = unit * gain
            return (scaled * cosine + swap(scaled) * sine).astype(BF)

        def back_of(gradient, unit, inverse, gain, slot):
            turned = gradient * cosine - swap(gradient) * sine
            head_total[slot] += fold(turned * unit)
            return norm_back(turned * gain, unit, inverse).astype(BF)

        q_gain, k_gain = head_gains[:, :width], head_gains[:, width : 2 * width]
        k_unit, k_inverse = unit_of(raw_held[here, q_cols : q_cols + width])
        k_low = low_of(k_unit, k_gain)
        v_low = raw_held[here, q_cols + width : q_cols + 2 * width].astype(BF)
        k_grad = jnp.zeros((rows, width), F32)
        v_grad = jnp.zeros((rows, width), F32)
        for h in range(heads):
            lanes = slice(h * width, (h + 1) * width)
            q_unit, q_inverse = unit_of(raw_held[here, lanes])
            q_low = low_of(q_unit, q_gain)
            prob = prob_held[b * heads + h]
            own_grad = mixed_grad[:, lanes]
            v_grad += dot(prob.astype(BF), own_grad, TN)
            prob_grad = dot(own_grad, v_low, NT)
            score_grad = (
                prob * (prob_grad - jnp.sum(prob * prob_grad, axis=-1, keepdims=True))
            ).astype(BF)
            q_grad = dot(score_grad, k_low, NN) * scale
            k_grad += dot(score_grad, q_low, TN)
            raw_grad[here, lanes] = back_of(q_grad, q_unit, q_inverse, q_gain, 0)
        raw_grad[here, q_cols : q_cols + width] = back_of(
            k_grad * scale, k_unit, k_inverse, k_gain, 1
        )
        raw_grad[here, q_cols + width : q_cols + 2 * width] = v_grad.astype(BF)

    def out_piece(q):
        base = at.column_base(q)
        lanes = pl.ds(pl.multiple_of(base * width, 2 * width), 2 * width)
        left_side = mixed_held[:, lanes]
        step = 512
        for start in range(0, model, step):
            total = dot(left_side, held[:, start : start + step], TN)
            for c in (0, 1):
                out_tree.part[q, c, :, start : start + step] = total[
                    c * width : (c + 1) * width
                ].astype(BF)
        out_tree.part_copy(q).start()

    some = count // 2

    def cols_piece(q):
        base = at.column_base(q)
        for there in range(4):
            lanes = pl.ds(
                pl.multiple_of(there * (model // 4) + base * count, 2 * count), 2 * count
            )
            block = dot(normed_held[:, lanes], raw_grad[...], TN)
            small = dot(left[:, lanes], right[...], TN)
            for c in (0, 1):
                for i, tree in enumerate(cols_trees):
                    of = slice(c * count + i * some, c * count + (i + 1) * some)
                    here = pl.ds(there * some, some)
                    tree.part[q, c, here, :cols] = block[of].astype(BF)
                    tree.part[q, c, here, cols:] = small[of].astype(BF)
        cols_trees[0].part_copy(q).start()

    groups = ((0, q_cols), (q_cols, width), (q_cols + width, width), (cols, EXTRA))

    def exchange_refs(i, to, of):
        here = pl.ds(pl.multiple_of(to * some, some), some)
        first = 0
        refs = []
        for start, size in groups:
            lanes = pl.ds(pl.multiple_of(first + of * size, size), size)
            refs.append((cols_totals[i].at[here, pl.ds(start, size)], cols_alls[i].at[:, lanes]))
            first += 4 * size
        return refs

    def exchange(i, k):
        there = at.plane(k)
        turn = at.turn_at(there)
        return [
            remote(src, dst, ex_send.at[i, k - 1, j], ex_recv.at[i, turn - 1, j], (at.e, there))
            for j, (src, dst) in enumerate(exchange_refs(i, there, at.z))
        ]

    def exchange_arrival(i, k):
        return [
            remote(dst, dst, ex_send.at[i, k - 1, j], ex_recv.at[i, k - 1, j], at.sibling)
            for j, (src, dst) in enumerate(exchange_refs(i, at.z, at.plane(k)))
        ]

    def own_exchange(i):
        return [
            pltpu.make_async_copy(src, dst, ex_local.at[i, j])
            for j, (src, dst) in enumerate(exchange_refs(i, at.z, at.z))
        ]

    def begin_exchange(i):
        cols_trees[i].do_own(cols_totals[i])
        for k in (1, 2, 3):
            for copy in exchange(i, k):
                copy.start()
        for copy in own_exchange(i):
            copy.start()

    def end_exchange(i):
        for copy in own_exchange(i):
            copy.wait()
        for k in (1, 2, 3):
            for copy in exchange_arrival(i, k):
                copy.wait_recv()
        cols_spreads[i].begin()

    line.arrive(1)

    @pl.when(jnp.logical_not(outer))
    def _():
        line.arrive(2)

    for copy in loads[:5]:
        copy.wait()
    attention(False)

    @pl.when(outer)
    def _():
        line.arrive(2)
        line.arrive(3)

    loads[5].wait()
    for q in (DIAG, XCOL, YCOL, OWN):
        out_piece(q)
    out_tree.do_diag()
    attention(True)
    out_tree.do_own(out_total)
    out_spread.begin()
    for j in range(4):
        lanes = slice(j * quarter, (j + 1) * quarter)
        left[pl.ds(2 * rows, 16), lanes] = split_rows(
            gain_total[:, lanes] / small_ref[j, 0:1, :]
        )
    for slot in (0, 1):
        placed = jnp.dot(
            split_rows(head_total[slot]), place_ref[...], preferred_element_type=F32
        )
        left[pl.ds(2 * rows + 16 * (slot + 1), 16)] = placed.astype(BF)
    first, last = cols_trees
    for q in (DIAG, XCOL, YCOL, OWN):
        cols_piece(q)
    out_spread.cross()
    for q in (DIAG, XCOL, YCOL, OWN):
        last.part_copy(q).start()
    first.do_diag()
    last.do_diag()
    first.do_x()
    first.do_y()

    @pl.when(jnp.logical_not(outer))
    def _():
        sums.give_far()

    last.do_x()
    last.do_y()
    begin_exchange(0)
    sums.give_near(False)
    begin_exchange(1)
    end_exchange(0)
    out_spread.diag()
    end_exchange(1)
    cols_spreads[0].cross()
    sums.wait()

    @pl.loop(0, rows // 32)
    def _(i):
        here = pl.ds(pl.multiple_of(i * 32, 32), 32)
        dnormed_ref[here] += sums.total(here)

    cols_spreads[1].cross()
    cols_spreads[0].diag()
    cols_spreads[1].diag()
    out_spread.end()
    for spread in cols_spreads:
        spread.end()
    out_tree.drain()
    for tree in cols_trees:
        tree.drain()
    line.end()
    sums.end()
    for i in (0, 1):
        for k in (1, 2, 3):
            for copy in exchange(i, k):
                copy.wait_send()


def back_in_one(resident, sums, loaded):
    w_out, w_cols = loaded[:2]
    rows, model = resident[0].shape
    cols = w_cols.shape[1]
    wide = cols + EXTRA
    count = model // 4 // 8
    vmem = pl.BlockSpec(memory_space=pltpu.VMEM)
    hbm = pl.BlockSpec(memory_space=pl.ANY)
    dma = pltpu.SemaphoreType.DMA
    return pl.pallas_call(
        back_kernel,
        out_shape=(
            jax.ShapeDtypeStruct((rows, model), F32),
            jax.ShapeDtypeStruct((rows, model), BF),
            jax.ShapeDtypeStruct((rows, model), F32),
            jax.ShapeDtypeStruct((8 * HEAD_WIDTH, model), BF),
            jax.ShapeDtypeStruct((8 * count, 4 * wide), BF),
        ),
        in_specs=[vmem] * len(resident) + [hbm] * (1 + len(loaded)),
        out_specs=(vmem, vmem, vmem, hbm, hbm),
        scratch_shapes=[
            *[pltpu.VMEM(v.shape, v.dtype) for v in loaded],
            pltpu.VMEM((4 * rows, model), BF),
            pltpu.VMEM((4 * rows, cols), BF),
            pltpu.VMEM((3 * rows, model), BF),
            pltpu.VMEM((3 * rows, EXTRA), BF),
            pltpu.VMEM((rows, EXTRA), F32),
            pltpu.VMEM((EXTRA, model), BF),
            pltpu.VMEM((4, rows, model), BF),
            pltpu.VMEM((5, rows, model), BF),
            pltpu.VMEM((8, model), F32),
            pltpu.VMEM((2, 8, HEAD_WIDTH), F32),
            pltpu.VMEM((HEAD_WIDTH, model), BF),
            *[pltpu.VMEM((2 * count, wide), BF)] * 2,
            *[pltpu.VMEM((count // 2, 4 * wide), BF)] * 2,
            *Tree.buffers(HEAD_WIDTH, model),
            *Tree.semaphores(),
            *Tree.buffers(2 * count, wide),
            *Tree.semaphores(),
            *Tree.buffers(2 * count, wide),
            *Tree.semaphores(),
            *Spread.semaphores(),
            *Spread.semaphores(),
            *Spread.semaphores(),
            *Line.semaphores(),
            *LineSum.semaphores(),
            dma((2, 3, 4)),
            dma((2, 3, 4)),
            dma((2, 4)),
            dma((6,)),
            dma((2,)),
        ],
        compiler_params=pltpu.CompilerParams(
            collective_id=1, has_side_effects=True, vmem_limit_bytes=VMEM_BYTES
        ),
        cost_estimate=pl.CostEstimate(
            flops=2 * 4 * rows * model * cols * 5,
            bytes_accessed=64 * 1024 * 1024,
            transcendentals=4 * rows * cols,
        ),
    )(*resident, sums, *loaded)


def front_kernel(
    tokens_ref,
    small_ref,
    router_ref,
    w_query_ref,
    w_key_ref,
    w_value_ref,
    w_out_ref,
    table_ref,
    chosen_ref,
    cot_ref,
    second_ref,
    middle_ref,
    share_ref,
    w_cols_out,
    normed_out,
    raw_out,
    prob_out,
    mixed_out,
    cos_ref,
    sin_ref,
    small_all_ref,
    router_all_ref,
    cot_all_ref,
    w_cols_ref,
    normed_ref,
    raw_ref,
    prob_ref,
    mixed_ref,
    own_part,
    router_wide,
    rows_out,
    rows_in,
    small_send,
    small_recv,
    piece_send,
    piece_recv,
    piece_local,
    cot_local,
    store_sem,
    *sems,
):
    at = Place()
    rows, model = tokens_ref.shape
    pair = 2 * rows
    width = HEAD_WIDTH
    q_cols = w_query_ref.shape[1] // 4
    heads = q_cols // width
    cols = q_cols + 2 * width
    quarter = model // 4
    count = quarter // 8
    half = rows // 2
    experts_all = router_ref.shape[0]
    scale = HEAD_WIDTH ** (-0.5)
    meet(at.everyone())

    cot_here = pltpu.make_async_copy(cot_ref, cot_all_ref.at[at.z, at.e // 2], cot_local)
    cot_here.start()

    small_all_ref[at.z] = small_ref[...]
    router_all_ref[at.z] = router_ref[...]

    def small_copies(k):
        there = at.plane(k)
        turn = at.turn_at(there)
        return [
            remote(
                ref,
                ref_all.at[at.z],
                small_send.at[k - 1, i],
                small_recv.at[turn - 1, i],
                (at.e, there),
            )
            for i, (ref, ref_all) in enumerate(
                ((small_ref, small_all_ref), (router_ref, router_all_ref))
            )
        ]

    for k in (1, 2, 3):
        for copy in small_copies(k):
            copy.start()

    def w_block(k, q, i=None):
        first, size = (0, count) if i is None else (i * (count // 2), count // 2)
        row = at.plane(k) * quarter + at.own(q) * count + first
        return w_cols_ref.at[pl.ds(pl.multiple_of(row, count // 2), size)]

    def piece_refs(there):
        own = pl.ds(pl.multiple_of(at.e * count, count), count)
        row = pl.ds(pl.multiple_of(at.z * quarter + at.e * count, count), count)
        narrow = pl.ds(pl.multiple_of(there * width, width), width)
        return (
            (
                w_query_ref.at[own, pl.ds(pl.multiple_of(there * q_cols, q_cols), q_cols)],
                w_cols_ref.at[row, pl.ds(0, q_cols)],
            ),
            (w_key_ref.at[own, narrow], w_cols_ref.at[row, pl.ds(q_cols, width)]),
            (w_value_ref.at[own, narrow], w_cols_ref.at[row, pl.ds(q_cols + width, width)]),
        )

    def piece_copies(k):
        there = at.plane(k)
        turn = at.turn_at(there)
        return [
            remote(
                src, dst, piece_send.at[k - 1, i], piece_recv.at[turn - 1, i], (at.e, there)
            )
            for i, (src, dst) in enumerate(piece_refs(there))
        ]

    def pieces_arrive(k):
        block = w_block(k, OWN)
        for i, (first, size) in enumerate(((0, q_cols), (q_cols, width), (q_cols, width))):
            part = block.at[:, pl.ds(first, size)]
            remote(
                part, part, piece_send.at[k - 1, i], piece_recv.at[k - 1, i], at.sibling
            ).wait_recv()

    own_pieces = [
        pltpu.make_async_copy(src, dst, piece_local.at[i])
        for i, (src, dst) in enumerate(piece_refs(at.z))
    ]
    for copy in own_pieces:
        copy.start()
    for k in (1, 2, 3):
        for copy in piece_copies(k):
            copy.start()
    weights = Gather(at, w_block, sems[2:10])
    for copy in own_pieces:
        copy.wait()
    weights.own(0)

    def normed_block(b):
        return normed_ref.at[pl.ds(pl.multiple_of(b * rows, rows), rows)]

    line = Line(at, normed_block, sems[10:12])
    source = tokens_ref[...].astype(F32)
    inverse = lax.rsqrt(jnp.mean(source * source, axis=-1, keepdims=True) + epsilon)
    for k in (1, 2, 3):
        for i, ref_all in enumerate((small_all_ref, router_all_ref)):
            block = ref_all.at[at.plane(k)]
            remote(
                block, block, small_send.at[k - 1, i], small_recv.at[k - 1, i], at.sibling
            ).wait_recv()
    own_rows = pl.ds(pl.multiple_of(at.z * rows, rows), rows)
    for j in range(4):
        lanes = slice(j * quarter, (j + 1) * quarter)
        normed_ref[own_rows, lanes] = (source[:, lanes] * inverse * small_all_ref[j, 0:1, :]).astype(BF)
        router_wide[0:experts_all, lanes] = router_all_ref[j]
        router_wide[experts_all : 2 * experts_all, lanes] = router_all_ref[j]
    router_wide[2 * experts_all :] = jnp.zeros((EXTRA - 2 * experts_all, model), BF)
    line.begin()

    def cot_block(k, q, i=None):
        block = cot_all_ref.at[at.plane(k), at.column_base(q) // 2]
        return block if i is None else block.at[pl.ds(i * half, half)]

    def cot_line_block(b):
        return cot_all_ref.at[b, at.e // 2]

    cot_line = Line(at, cot_line_block, sems[12:14])
    cot_gather = Gather(at, cot_block, sems[14:], sibling=False)
    outer = (at.z == 0) | (at.z == 3)
    cot_here.wait()

    @pl.when(outer)
    def _():
        cot_line.begin()


    pieces_arrive(1)
    weights.own(1)
    line.arrive(1)
    pieces_arrive(2)
    weights.own(2)
    pieces_arrive(3)
    weights.own(3)

    @pl.when(jnp.logical_not(outer))
    def _():
        line.arrive(2)

    weights.cross(0)
    weights.cross(1)

    @pl.when(jnp.logical_not(outer))
    def _():
        line.arrive(3)
        cot_line.begin()

    cot_gather.own(0)
    weights.diag(0)
    weights.cross(2)
    weights.diag(1)
    weights.cross(3)
    weights.diag(2)
    weights.diag(3)
    stores = [
        pltpu.make_async_copy(src, dst, store_sem.at[i])
        for i, (src, dst) in enumerate(
            (
                (normed_ref, normed_out),
                (w_cols_ref, w_cols_out),
                (raw_ref, raw_out),
                (prob_ref, prob_out),
                (mixed_ref, mixed_out),
            )
        )
    ]
    for k in range(4):
        for q in range(4):
            weights.ready(k, q)
    stores[1].start()
    sums = LineSum(at, rows_out, rows_in, sems[:2])

    def project(far):
        first = 2 * (1 - at.half if far else at.half)
        both = pl.ds(pl.multiple_of(first * rows, pair), pair)
        step = 256
        for start in range(0, cols, step):
            lanes = slice(start, start + step)
            raw_ref[both, lanes] = jnp.dot(
                normed_ref[both, :], w_cols_ref[:, lanes], preferred_element_type=F32
            )

    gains = small_all_ref[0, 2:3, :] + small_all_ref[1, 2:3, :] + small_all_ref[2, 2:3, :] + small_all_ref[3, 2:3, :]
    q_gain, k_gain = gains[:, :width], gains[:, width : 2 * width]
    row_id = lax.broadcasted_iota(jnp.int32, (rows, rows), 0).astype(F32)
    lane_id = lax.broadcasted_iota(jnp.int32, (rows, rows), 1).astype(F32)

    def attention(far):
        first = 2 * (1 - at.half if far else at.half)
        both = pl.ds(pl.multiple_of(first * rows, pair), pair)
        for i in (0, 1):
            heads_of(first + i)
        step = 512
        for start in range(0, model, step):
            lanes = slice(start, start + step)
            part = jnp.dot(mixed_ref[both, :], w_out_ref[:, lanes], preferred_element_type=F32)
            if not far:
                own_part[:, lanes] = jnp.where(at.z % 2 == 0, part[:rows], part[rows:])
            rows_out[first, :, lanes] = part[:rows].astype(BF)
            rows_out[first + 1, :, lanes] = part[rows:].astype(BF)
        if far:
            sums.give_far()
        sums.give_near(not far)

    def heads_of(b):
        here = pl.ds(pl.multiple_of(b * rows, rows), rows)
        segment = jnp.zeros((rows, rows), F32)
        lane_segment = jnp.zeros((rows, rows), F32)
        place = row_id
        end = jnp.zeros((1, 1), F32)
        for i in range(SEQ_SLOTS - 1):
            length = small_all_ref[b, 2:3, 2 * width + i : 2 * width + i + 1]
            end = end + length
            past = (row_id >= end).astype(F32)
            segment += past
            place -= past * length
            lane_segment += (lane_id >= end).astype(F32)
        allowed = (segment == lane_segment) & (lane_id <= row_id)
        named = (lane_id == place).astype(BF)

        def looked_up(first):
            total = jnp.zeros((rows, width), F32)
            for i in range(3):
                part = table_ref[(first + i) * width : (first + i + 1) * width]
                total += jnp.dot(named, part, preferred_element_type=F32)
            return total

        cosine, sine = looked_up(0), looked_up(3)
        cos_ref[here, :] = cosine
        sin_ref[here, :] = sine

        def low_of(v, gain):
            inverse = lax.rsqrt(jnp.mean(v * v, axis=-1, keepdims=True) + epsilon)
            scaled = v * inverse * gain
            return (scaled * cosine + swap(scaled) * sine).astype(BF)

        k_low = low_of(raw_ref[here, q_cols : q_cols + width], k_gain)
        v_low = raw_ref[here, q_cols + width : q_cols + 2 * width].astype(BF)
        for h in range(heads):
            lanes = slice(h * width, (h + 1) * width)
            q_low = low_of(raw_ref[here, lanes], q_gain)
            scores = jnp.where(allowed, dot(q_low, k_low, NT) * scale, masked_score)
            weight = jnp.exp(scores - jnp.max(scores, axis=-1, keepdims=True))
            prob = weight / jnp.sum(weight, axis=-1, keepdims=True)
            prob_ref[b * heads + h] = prob
            mixed_ref[here, lanes] = dot(prob.astype(BF), v_low, NN).astype(BF)

    project(False)
    cot_line.arrive(1)
    cot_gather.own(1)
    attention(False)

    @pl.when(outer)
    def _():
        line.arrive(2)
        line.arrive(3)

    @pl.when(jnp.logical_not(outer))
    def _():
        cot_line.arrive(2)
        cot_gather.own(2)

    cot_gather.cross(0)
    stores[0].start()
    project(True)
    stores[2].start()

    @pl.when(jnp.logical_not(outer))
    def _():
        cot_line.arrive(3)
        cot_gather.own(3)

    cot_gather.cross(1)
    attention(True)
    stores[3].start()
    stores[4].start()

    @pl.when(outer)
    def _():
        cot_line.arrive(2)
        cot_gather.own(2)
        cot_line.arrive(3)
        cot_gather.own(3)

    cot_gather.diag(0)
    cot_gather.diag(1)
    cot_gather.cross(2)
    cot_gather.cross(3)
    sums.wait()
    middle = (
        tokens_ref[...].astype(F32)
        + own_part[...]
        + sums.total(pl.ds(0, rows))
    )
    middle_ref[...] = middle
    inverse = lax.rsqrt(jnp.mean(middle * middle, axis=-1, keepdims=True) + epsilon)
    for j in range(4):
        lanes = slice(j * quarter, (j + 1) * quarter)
        second_ref[:, lanes] = (middle[:, lanes] * inverse * small_all_ref[j, 1:2, :]).astype(BF)
    logits = dot(second_ref[:, :model], router_wide[...], NT)
    chosen = chosen_ref[...] > 0.0
    lane = lax.broadcasted_iota(jnp.int32, (rows, EXTRA), 1)
    top = jnp.max(jnp.where(chosen, logits, masked_score), axis=-1, keepdims=True)
    lifted = jnp.where(chosen, jnp.exp(logits - top), 0.0)
    share = lifted / jnp.sum(jnp.where(lane < experts_all, lifted, 0.0), axis=-1, keepdims=True)
    share_ref[...] = share
    high = share.astype(BF).astype(F32)
    second_ref[:, model:] = jnp.where(lane < experts_all, high, share - high).astype(BF)
    cot_gather.diag(2)
    cot_gather.diag(3)
    for copy in stores:
        copy.wait()
    for k in range(4):
        cot_gather.end(k)
        weights.end(k)
    line.end()
    cot_line.end()
    sums.end()
    for k in (1, 2, 3):
        for copy in small_copies(k):
            copy.wait_send()
        for copy in piece_copies(k):
            copy.wait_send()


def front_in_one(tokens, small, router, w_query, w_key, w_value, w_out, table, chosen, cotangent):
    rows, model = tokens.shape
    q_cols = w_query.shape[1] // 4
    cols = q_cols + 2 * HEAD_WIDTH
    heads = q_cols // HEAD_WIDTH
    experts_all = router.shape[0]
    vmem = pl.BlockSpec(memory_space=pltpu.VMEM)
    hbm = pl.BlockSpec(memory_space=pl.ANY)
    dma = pltpu.SemaphoreType.DMA
    shape = jax.ShapeDtypeStruct
    return pl.pallas_call(
        front_kernel,
        out_shape=(
            shape((rows, model + EXTRA), BF),
            shape((rows, model), F32),
            shape((rows, EXTRA), F32),
            shape((model, cols), BF),
            shape((4 * rows, model), BF),
            shape((4 * rows, cols), F32),
            shape((4 * heads, rows, rows), F32),
            shape((4 * rows, q_cols), BF),
            shape((4 * rows, HEAD_WIDTH), F32),
            shape((4 * rows, HEAD_WIDTH), F32),
            shape((4, 8, model // 4), F32),
            shape((4, experts_all, model // 4), BF),
            shape((4, 4, rows, model), BF),
        ),
        in_specs=[vmem, vmem, vmem, hbm, hbm, hbm, vmem, vmem, vmem, hbm],
        out_specs=(vmem,) * 3 + (hbm,) * 5 + (vmem,) * 4 + (hbm,),
        scratch_shapes=[
            pltpu.VMEM((model, cols), BF),
            pltpu.VMEM((4 * rows, model), BF),
            pltpu.VMEM((4 * rows, cols), F32),
            pltpu.VMEM((4 * heads, rows, rows), F32),
            pltpu.VMEM((4 * rows, q_cols), BF),
            pltpu.VMEM((rows, model), F32),
            pltpu.VMEM((EXTRA, model), BF),
            pltpu.VMEM((4, rows, model), BF),
            pltpu.VMEM((5, rows, model), BF),
            dma((3, 2)),
            dma((3, 2)),
            dma((3, 3)),
            dma((3, 3)),
            dma((3,)),
            dma,
            dma((5,)),
            *LineSum.semaphores(),
            *Gather.semaphores(),
            *Line.semaphores(),
            *Line.semaphores(),
            *Gather.semaphores(False),
        ],
        compiler_params=pltpu.CompilerParams(
            collective_id=2, has_side_effects=True, vmem_limit_bytes=VMEM_BYTES
        ),
        cost_estimate=pl.CostEstimate(
            flops=2 * 4 * rows * model * (cols + q_cols),
            bytes_accessed=64 * 1024 * 1024,
            transcendentals=4 * rows * cols,
        ),
    )(tokens, small, router, w_query, w_key, w_value, w_out, table, chosen, cotangent)


def per_device(
    tokens,
    lengths,
    routes,
    attn_gain,
    w_query,
    key_projection,
    value_projection,
    w_out,
    query_gain,
    key_gain,
    ffn_gain,
    w_router,
    w_gate,
    w_up,
    w_down,
    cotangent,
):
    ring = lax.axis_size("fsdp")
    groups = lax.axis_size("expert")
    plane_rank = lax.axis_index("expert")
    experts_all = w_router.shape[1]
    local_experts = w_gate.shape[0]
    units = w_gate.shape[2]
    wide = local_experts * units
    in_rows = MODEL_WIDTH // ring
    heads = QUERY_HEADS // ring
    kv = KEY_VALUE_HEADS // ring
    group_width = heads // kv
    q_cols = heads * HEAD_WIDTH
    kv_cols = kv * HEAD_WIDTH
    cols = q_cols + 2 * kv_cols
    piece_rows = in_rows // groups
    score_scale = HEAD_WIDTH ** (-0.5)
    both = ("expert", "fsdp")
    one_block = (groups, ring, experts_all) == (8, 4, 16)

    gate_w = w_gate.transpose(0, 2, 1).reshape(wide, MODEL_WIDTH)
    up_w = w_up.transpose(0, 2, 1).reshape(wide, MODEL_WIDTH)
    down_w = w_down.reshape(wide, MODEL_WIDTH)
    line_tokens = ring * DEVICE_TOKENS
    source = tokens.astype(F32)
    expert_ids = jnp.arange(experts_all, dtype=jnp.int32)
    chosen = jnp.any(routes[:, :, None] == expert_ids[None, None, :], axis=1)

    if one_block:
        here = lax.axis_index("fsdp") * (HEAD_WIDTH // ring)
        spread = lambda gain: lax.dynamic_update_slice_in_dim(
            jnp.zeros((HEAD_WIDTH,), F32), gain.astype(F32), here, 0
        )
        third = jnp.concatenate(
            [spread(query_gain), spread(key_gain), lengths.reshape(-1).astype(F32)]
        )
        small = jnp.stack(
            [
                attn_gain.astype(F32),
                ffn_gain.astype(F32),
                jnp.pad(third, (0, in_rows - third.shape[0])),
            ]
        )
        frequency = rope_base ** (-np.arange(0, HEAD_WIDTH, 2) / HEAD_WIDTH)
        angles = np.arange(HEAD_WIDTH)[:, None] * np.tile(frequency, 2)[None, :]
        sine_sign = np.where(np.arange(HEAD_WIDTH) < HEAD_WIDTH // 2, -1.0, 1.0)
        parts = []
        for exact in (np.cos(angles), np.sin(angles) * sine_sign):
            for _ in range(3):
                parts.append(exact.astype(ml_dtypes.bfloat16))
                exact = exact - parts[-1].astype(np.float64)
        wide_chosen = jnp.pad(
            jnp.concatenate([chosen, chosen], axis=1).astype(F32),
            ((0, 0), (0, EXTRA - 2 * experts_all)),
        )
        (
            second_wide,
            middle,
            share,
            w_cols,
            normed_all,
            raw,
            probabilities,
            mixed,
            cosine,
            sine_table,
            small_all,
            router_all,
            cot_all,
        ) = front_in_one(
            tokens,
            jnp.pad(small, ((0, 5), (0, 0))),
            w_router.T,
            w_query,
            key_projection,
            value_projection,
            w_out,
            jnp.asarray(np.concatenate(parts)),
            wide_chosen,
            cotangent,
        )
        cot_all = cot_all.reshape(-1, MODEL_WIDTH)
        attn_gain_f = small_all[:, 0].reshape(-1)
        attn_inverse = lax.rsqrt(jnp.mean(source * source, axis=-1, keepdims=True) + epsilon)
        attn_unit = source * attn_inverse
    else:
        small = jnp.concatenate(
            [
                attn_gain,
                ffn_gain,
                query_gain,
                key_gain,
                w_router.reshape(-1),
                lengths.reshape(-1).astype(BF),
            ]
        )
        small_all = lax.all_gather(small, "fsdp", axis=0, tiled=False)
        at = 0

        def take(count):
            nonlocal at
            part = small_all[:, at : at + count]
            at += count
            return part

        attn_gain_f = take(in_rows).reshape(-1).astype(F32)
        ffn_gain_f = take(in_rows).reshape(-1).astype(F32)
        query_gain_f = take(HEAD_WIDTH // ring).reshape(-1).astype(F32)
        key_gain_f = take(HEAD_WIDTH // ring).reshape(-1).astype(F32)
        router_all = take(in_rows * experts_all).reshape(MODEL_WIDTH, experts_all)
        lengths_all = take(SEQ_SLOTS).astype(jnp.int32)

        by_col = jnp.concatenate(
            [
                w_query.reshape(in_rows, ring, q_cols),
                key_projection.reshape(in_rows, ring, kv_cols),
                value_projection.reshape(in_rows, ring, kv_cols),
            ],
            axis=2,
        )
        piece = lax.dynamic_slice_in_dim(by_col, plane_rank * piece_rows, piece_rows, 0)
        piece = lax.all_to_all(
            piece.transpose(1, 0, 2), "fsdp", split_axis=0, concat_axis=0, tiled=True
        )
        w_cols = lax.all_gather(piece, "expert", axis=1, tiled=True).reshape(MODEL_WIDTH, cols)

        attn_inverse = lax.rsqrt(jnp.mean(source * source, axis=-1, keepdims=True) + epsilon)
        attn_unit = source * attn_inverse
        normed = (attn_unit * attn_gain_f).astype(BF)
        normed_all = lax.all_gather(normed, "fsdp", axis=0, tiled=True)
        raw = dot(normed_all, w_cols, NN)
        query_raw = raw[:, :q_cols].reshape(ring, DEVICE_TOKENS, kv, group_width, HEAD_WIDTH)
        key_raw = raw[:, q_cols : q_cols + kv_cols].reshape(ring, DEVICE_TOKENS, kv, HEAD_WIDTH)
        value_low = raw[:, q_cols + kv_cols :].astype(BF).reshape(ring, DEVICE_TOKENS, kv, HEAD_WIDTH)
        places, segment_ids = jax.vmap(lambda row: layout(row, DEVICE_TOKENS, SEQ_SLOTS))(lengths_all)
        cosine, sine_table = rope_tables(places, HEAD_WIDTH)
        cos_k, sin_k = cosine[:, :, None, :], sine_table[:, :, None, :]
        cos_q, sin_q = cosine[:, :, None, None, :], sine_table[:, :, None, None, :]
        query_inverse = lax.rsqrt(jnp.mean(query_raw * query_raw, axis=-1, keepdims=True) + epsilon)
        query_unit = query_raw * query_inverse
        query_low = rotate(query_unit * query_gain_f, cos_q, sin_q).astype(BF)
        key_inverse = lax.rsqrt(jnp.mean(key_raw * key_raw, axis=-1, keepdims=True) + epsilon)
        key_unit = key_raw * key_inverse
        key_low = rotate(key_unit * key_gain_f, cos_k, sin_k).astype(BF)
        row_ids = jnp.arange(DEVICE_TOKENS, dtype=jnp.int32)
        allowed = (segment_ids[:, :, None] == segment_ids[:, None, :]) & (
            row_ids[None, None, :] <= row_ids[None, :, None]
        )
        scores = (
            jnp.einsum("bqhgd,bkhd->bhgqk", query_low, key_low, preferred_element_type=F32)
            * score_scale
        )
        scores = jnp.where(allowed[:, None, None], scores, masked_score)
        weights = jnp.exp(scores - jnp.max(scores, axis=-1, keepdims=True))
        probabilities = weights / jnp.sum(weights, axis=-1, keepdims=True)
        prob_low = probabilities.astype(BF)
        mixed = (
            jnp.einsum("bhgqk,bkhd->bqhgd", prob_low, value_low, preferred_element_type=F32)
            .astype(BF)
            .reshape(line_tokens, q_cols)
        )
        branch = lax.psum_scatter(
            dot(mixed, w_out, NN).astype(BF), "fsdp", scatter_dimension=0, tiled=True
        ).astype(F32)
        middle = source + branch
        ffn_inverse = lax.rsqrt(jnp.mean(middle * middle, axis=-1, keepdims=True) + epsilon)
        ffn_unit = middle * ffn_inverse
        second = (ffn_unit * ffn_gain_f).astype(BF)

        logits = dot(second, router_all, NN)
        top = jnp.max(jnp.where(chosen, logits, -jnp.inf), axis=1, keepdims=True)
        lifted = jnp.where(chosen, jnp.exp(logits - top), 0.0)
        share = lifted / jnp.sum(lifted, axis=1, keepdims=True)

    def experts(second, share, cotangent):
        second_all = lax.all_gather(second, both, axis=0, tiled=True)
        share_all = lax.all_gather(share, both, axis=0, tiled=True)
        cot_all = lax.all_gather(cotangent, both, axis=0, tiled=True)
        first = plane_rank * local_experts
        own_share = lax.dynamic_slice_in_dim(share_all, first, local_experts, 1)
        share_wide = jnp.repeat(own_share, units, axis=1)
        gate_act = dot(second_all, gate_w, NT)
        up_act = dot(second_all, up_w, NT)
        back = dot(cot_all, down_w, NT)
        sigmoid_gate = jax.nn.sigmoid(gate_act)
        silu_gate = gate_act * sigmoid_gate
        hidden = silu_gate * up_act
        share_grad = jnp.sum((hidden * back).reshape(-1, local_experts, units), axis=2)
        hidden_low = (share_wide * hidden).astype(BF)
        hidden_grad = share_wide * back
        gate_grad = (
            hidden_grad * up_act * sigmoid_gate * (1.0 + gate_act * (1.0 - sigmoid_gate))
        ).astype(BF)
        up_grad = (hidden_grad * silu_gate).astype(BF)
        routed_part = dot(hidden_low, down_w, NN).astype(BF)
        second_part = (dot(gate_grad, gate_w, NN) + dot(up_grad, up_w, NN)).astype(BF)
        spread = jnp.zeros((share_grad.shape[0], experts_all), F32)
        spread = lax.dynamic_update_slice_in_dim(spread, share_grad, first, 1)
        second_grad = lax.psum_scatter(second_part, both, scatter_dimension=0, tiled=True)
        routed = lax.psum_scatter(routed_part, both, scatter_dimension=0, tiled=True)
        dshare = lax.psum_scatter(spread, both, scatter_dimension=0, tiled=True)
        return (
            (second_grad.astype(F32), routed.astype(F32), dshare),
            (
                dot(gate_grad, second_all, TN),
                dot(up_grad, second_all, TN),
                dot(hidden_low, cot_all, TN),
            ),
        )

    chunks = max(1, ring * groups // 32)
    if one_block:
        sums, *weight_grads, _ = experts_in_one(second_wide, cot_all, gate_w, up_w, down_w)
    elif chunks == 1:
        rows_out, weight_grads = experts(second, share, cotangent)
    else:
        def turn(total, rows):
            rows_out, grads = experts(*rows)
            return jax.tree.map(jnp.add, total, grads), rows_out

        start = (
            jnp.zeros((wide, MODEL_WIDTH), F32),
            jnp.zeros((wide, MODEL_WIDTH), F32),
            jnp.zeros((wide, MODEL_WIDTH), F32),
        )
        weight_grads, rows_out = lax.scan(
            turn,
            start,
            [v.reshape(chunks, -1, v.shape[1]) for v in (second, share, cotangent)],
        )
        rows_out = [v.reshape(-1, v.shape[2]) for v in rows_out]
    gate_wgrad, up_wgrad, down_wgrad = weight_grads
    grad_w_gate = gate_wgrad.reshape(local_experts, units, MODEL_WIDTH).transpose(0, 2, 1)
    grad_w_up = up_wgrad.reshape(local_experts, units, MODEL_WIDTH).transpose(0, 2, 1)
    grad_w_down = down_wgrad.reshape(local_experts, units, MODEL_WIDTH)
    if one_block:
        at_gain = experts_all
        part_width = HEAD_WIDTH // ring
        head_lane = np.arange(HEAD_WIDTH)
        place_of = head_lane // part_width * in_rows + head_lane % part_width
        placing = jnp.asarray(place_of[:, None] == np.arange(MODEL_WIDTH)[None, :], BF)
        normed_grad, block_out, middle_grad, out_sum, cols_sum = back_in_one(
            (
                middle,
                share,
                cotangent,
                router_all,
                small_all,
                cosine,
                sine_table,
                second_wide,
                placing,
            ),
            sums,
            (w_out, w_cols, mixed, normed_all, raw, probabilities),
        )
        tokens_grad = middle_grad + norm_back(normed_grad * attn_gain_f, attn_unit, attn_inverse)
        out_grad = out_sum.astype(F32)
        ends = [ring * n for n in (q_cols, q_cols + kv_cols, cols)]
        grad_w_query = cols_sum[:, : ends[0]].astype(F32)
        grad_w_key = cols_sum[:, ends[0] : ends[1]].astype(F32)
        grad_w_value = cols_sum[:, ends[1] : ends[2]].astype(F32)
        small_own = sum(
            cols_sum[:, ends[2] + j * EXTRA : ends[2] + (j + 1) * EXTRA].astype(F32)
            for j in range(ring)
        )
        own_grads = (
            small_own[:, at_gain + 1],
            small_own[:part_width, at_gain + 2],
            small_own[:part_width, at_gain + 3],
            small_own[:, at_gain],
            small_own[:, :experts_all],
        )
    else:
        second_grad, routed, dshare = rows_out
        block_out = (middle + routed).astype(BF)

        mean_grad = jnp.sum(share * dshare, axis=1, keepdims=True)
        logit_grad = (share * (dshare - mean_grad)).astype(BF)
        upstream = cotangent.astype(F32)
        second_grad = second_grad + dot(logit_grad, router_all, NT)
        middle_grad = upstream + norm_back(second_grad * ffn_gain_f, ffn_unit, ffn_inverse)
        router_grad = dot(second, logit_grad, TN)
        ffn_gain_grad = jnp.sum(second_grad * ffn_unit, axis=0)
        branch_all = lax.all_gather(middle_grad.astype(BF), "fsdp", axis=0, tiled=True)
        out_grad = lax.psum(dot(mixed, branch_all, TN).astype(BF), "expert").astype(F32)
        mixed_grad = dot(branch_all, w_out, NT).astype(BF)
        mixed_grad = mixed_grad.reshape(ring, DEVICE_TOKENS, kv, group_width, HEAD_WIDTH)
        value_grad = jnp.einsum("bhgqk,bqhgd->bkhd", prob_low, mixed_grad, preferred_element_type=F32)
        prob_grad = jnp.einsum("bqhgd,bkhd->bhgqk", mixed_grad, value_low, preferred_element_type=F32)
        score_grad = (
            probabilities * (prob_grad - jnp.sum(probabilities * prob_grad, axis=-1, keepdims=True))
        ).astype(BF)
        query_grad = (
            jnp.einsum("bhgqk,bkhd->bqhgd", score_grad, key_low, preferred_element_type=F32)
            * score_scale
        )
        key_grad = (
            jnp.einsum("bhgqk,bqhgd->bkhd", score_grad, query_low, preferred_element_type=F32)
            * score_scale
        )
        query_turned = unrotate(query_grad, cos_q, sin_q)
        query_gain_grad = jnp.sum(query_turned * query_unit, axis=(0, 1, 2, 3))
        query_back = norm_back(query_turned * query_gain_f, query_unit, query_inverse)
        key_turned = unrotate(key_grad, cos_k, sin_k)
        key_gain_grad = jnp.sum(key_turned * key_unit, axis=(0, 1, 2))
        key_back = norm_back(key_turned * key_gain_f, key_unit, key_inverse)
        raw_grad = jnp.concatenate(
            [
                query_back.astype(BF).reshape(line_tokens, q_cols),
                key_back.astype(BF).reshape(line_tokens, kv_cols),
                value_grad.astype(BF).reshape(line_tokens, kv_cols),
            ],
            axis=1,
        )
        cols_grad = dot(normed_all, raw_grad, TN).astype(BF)
        normed_part = dot(raw_grad, w_cols, NT).astype(BF)
        normed_grad = lax.psum_scatter(normed_part, "fsdp", scatter_dimension=0, tiled=True).astype(F32)
        attn_gain_grad = jnp.sum(normed_grad * attn_unit, axis=0)
        tokens_grad = middle_grad + norm_back(normed_grad * attn_gain_f, attn_unit, attn_inverse)

        own = lax.psum_scatter(
            cols_grad.reshape(ring, groups, piece_rows, cols), "expert", scatter_dimension=1, tiled=False
        )
        own = lax.all_to_all(own, "fsdp", split_axis=0, concat_axis=0, tiled=True)
        rows_grad = lax.all_gather(own, "expert", axis=1, tiled=True)
        rows_grad = rows_grad.transpose(1, 0, 2).astype(F32)
        grad_w_query = rows_grad[:, :, :q_cols].reshape(in_rows, QUERY_HEADS * HEAD_WIDTH)
        grad_w_key = rows_grad[:, :, q_cols : q_cols + kv_cols].reshape(in_rows, -1)
        grad_w_value = rows_grad[:, :, q_cols + kv_cols :].reshape(in_rows, -1)

        small_grad = jnp.concatenate(
            [
                attn_gain_grad.reshape(ring, -1),
                ffn_gain_grad.reshape(ring, -1),
                query_gain_grad.reshape(ring, -1),
                key_gain_grad.reshape(ring, -1),
                router_grad.reshape(ring, -1),
            ],
            axis=1,
        )
        small_own = lax.psum(small_grad, both)
        small_own = lax.dynamic_index_in_dim(small_own, lax.axis_index("fsdp"), 0, keepdims=False)
        a, b = in_rows, HEAD_WIDTH // ring
        own_grads = (
            small_own[:a],
            small_own[2 * a : 2 * a + b],
            small_own[2 * a + b : 2 * a + 2 * b],
            small_own[a : 2 * a],
            small_own[2 * a + 2 * b :].reshape(in_rows, experts_all),
        )
    return (
        block_out,
        tokens_grad,
        own_grads[0],
        grad_w_query,
        grad_w_key,
        grad_w_value,
        out_grad,
        own_grads[1],
        own_grads[2],
        own_grads[3],
        own_grads[4],
        grad_w_gate,
        grad_w_up,
        grad_w_down,
    )


def solution(mesh):
    rows = P(("expert", "fsdp"), None)
    return jax.shard_map(
        per_device,
        mesh=mesh,
        in_specs=(
            rows,
            rows,
            rows,
            P("fsdp"),
            P("fsdp", None),
            P("fsdp", None),
            P("fsdp", None),
            P("fsdp", None),
            P("fsdp"),
            P("fsdp"),
            P("fsdp"),
            P("fsdp", None),
            P("expert", None, "fsdp"),
            P("expert", None, "fsdp"),
            P("expert", "fsdp", None),
            rows,
        ),
        out_specs=(
            rows,
            rows,
            P("fsdp"),
            P("fsdp", None),
            P("fsdp", None),
            P("fsdp", None),
            P("fsdp", None),
            P("fsdp"),
            P("fsdp"),
            P("fsdp"),
            P("fsdp", None),
            P("expert", None, "fsdp"),
            P("expert", None, "fsdp"),
            P("expert", "fsdp", None),
        ),
        check_vma=False,
    )
```

```python
import jax
import jax.numpy as jnp
import ml_dtypes
import numpy as np
from jax import lax
from jax.experimental import pallas as pl
from jax.experimental.pallas import tpu as pltpu
from jax.sharding import PartitionSpec as P

MODEL_WIDTH = 2048
QUERY_HEADS = 32
KEY_VALUE_HEADS = 4
HEAD_WIDTH = 128
TOPK = 8
DEVICE_TOKENS = 128
SEQ_SLOTS = 4

epsilon = 1e-06
rope_base = 1000000.0
masked_score = -1e30
BF = jnp.bfloat16
F32 = jnp.float32


def layout(lengths_row, tok_count, slot_count):
    seq_ends = jnp.cumsum(lengths_row)
    starts = seq_ends - lengths_row
    places = jnp.arange(tok_count, dtype=jnp.int32)
    segment = jnp.sum((places[:, None] >= seq_ends[None, :]).astype(jnp.int32), axis=1)
    member = segment[:, None] == jnp.arange(slot_count, dtype=jnp.int32)[None, :]
    start_of = jnp.sum(jnp.where(member, starts[None, :], 0), axis=1)
    return (places - start_of, segment)


def rope_tables(places, head_size):
    frequency = rope_base ** (-jnp.arange(0, head_size, 2, dtype=jnp.float32) / head_size)
    angles = places.astype(jnp.float32)[..., None] * frequency
    angles = jnp.concatenate([angles, angles], axis=-1)
    return (jnp.cos(angles), jnp.sin(angles))


def rotate(values, cosine, sine_table):
    half_width = values.shape[-1] // 2
    turned = jnp.concatenate([-values[..., half_width:], values[..., :half_width]], axis=-1)
    return values * cosine + turned * sine_table


def unrotate(gradient, cosine, sine_table):
    scaled = gradient * sine_table
    half_width = gradient.shape[-1] // 2
    return gradient * cosine + jnp.concatenate(
        [scaled[..., half_width:], -scaled[..., :half_width]], axis=-1
    )


def norm_back(gradient, unit_value, inverse):
    return inverse * (
        gradient - unit_value * jnp.mean(gradient * unit_value, axis=-1, keepdims=True)
    )


def dot(a, b, dims):
    return lax.dot_general(a, b, (dims, ((), ())), preferred_element_type=F32)


NN = ((1,), (0,))
NT = ((1,), (1,))
TN = ((0,), (0,))
VMEM_BYTES = 63 * 1024 * 1024

MESH = pl.DeviceIdType.MESH
EXTRA = 128
DIAG, XCOL, YCOL, OWN = 0, 1, 2, 3


def remote(src, dst, send, recv, device):
    return pltpu.make_async_remote_copy(
        src_ref=src,
        dst_ref=dst,
        send_sem=send,
        recv_sem=recv,
        device_id=device,
        device_id_type=MESH,
    )


class Place:
    def __init__(self):
        e = lax.axis_index("expert")
        z = lax.axis_index("fsdp")
        self.e, self.z = e, z
        self.core = lax.rem(e, 2)
        self.x = lax.rem(lax.div(e, 2), 2)
        self.y = lax.div(e, 4)
        self.x_near = (e + 2 - 4 * self.x, z)
        self.y_near = (e + 4 - 8 * self.y, z)
        self.sibling = (e + 1 - 2 * self.core, z)
        self.diagonal = (1 - self.y) * 4 + (1 - self.x) * 2 + self.core
        self.partner = z + 1 - 2 * lax.rem(z, 2)
        self.half = lax.div(z, 2)

    def plane(self, k):
        far = jnp.where(self.half == 0, k, 3 - k)
        return jnp.where(k == 0, self.z, jnp.where(k == 1, self.partner, far))

    def turn_at(self, z_there):
        far = jnp.where(z_there < 2, self.z, 3 - self.z)
        return jnp.where(z_there == self.partner, 1, far)

    def column_base(self, q):
        x = self.x if q in (YCOL, OWN) else 1 - self.x
        y = self.y if q in (XCOL, OWN) else 1 - self.y
        return (y * 2 + x) * 2

    def own(self, q):
        return self.column_base(q) + self.core

    def everyone(self):
        return [self.x_near, self.y_near, self.sibling] + [(self.e, self.plane(k)) for k in (1, 2, 3)]


def when(condition):
    def run(body):
        if isinstance(condition, bool):
            if condition:
                body()
        else:
            pl.when(condition)(body)

    return run


def greet(devices):
    barrier = pltpu.get_barrier_semaphore()
    for device in devices:
        pl.semaphore_signal(barrier, inc=1, device_id=device, device_id_type=MESH)


def meet(devices, greeted=False):
    if not greeted:
        greet(devices)
    pl.semaphore_wait(pltpu.get_barrier_semaphore(), len(devices))


class Line:
    def __init__(self, at, block, sems):
        self.at, self.block = at, block
        self.send, self.recv = sems

    def up(self, b):
        block = self.block(b)
        return remote(
            block, block, self.send.at[0, b], self.recv.at[b], (self.at.e, self.at.z + 1)
        )

    def down(self, b):
        block = self.block(b)
        return remote(
            block, block, self.send.at[1, b], self.recv.at[b], (self.at.e, self.at.z - 1)
        )

    def begin(self):
        z = self.at.z

        @pl.when(z < 3)
        def _():
            self.up(z).start()

        @pl.when(z > 0)
        def _():
            self.down(z).start()

    def arrive(self, k):
        z = self.at.z
        b = self.at.plane(k)
        block = self.block(b)
        remote(block, block, self.send.at[0, b], self.recv.at[b], self.at.sibling).wait_recv()

        @pl.when((b < z) & (z < 3))
        def _():
            self.up(b).start()

        @pl.when((b > z) & (z > 0))
        def _():
            self.down(b).start()

    def end(self):
        z = self.at.z
        for b in range(4):

            @pl.when((b <= z) & (z < 3))
            def _():
                self.up(b).wait_send()

            @pl.when((b >= z) & (z > 0))
            def _():
                self.down(b).wait_send()

    @staticmethod
    def semaphores():
        return [pltpu.SemaphoreType.DMA((2, 4)), pltpu.SemaphoreType.DMA((4,))]


class LineSum:
    def __init__(self, at, part, came, sems):
        self.at, self.part, self.came = at, part, came
        self.send, self.recv = sems

    def arrival(self, slot):
        block = self.came.at[slot]
        return remote(block, block, self.send.at[0], self.recv.at[slot], self.at.sibling)

    def copy(self, t):
        z = self.at.z
        up = (t > z).astype(jnp.int32)
        there = z + 2 * up - 1
        slot = jnp.where((t == there) & (up == 0), 4, t)
        return remote(
            self.part.at[t], self.came.at[slot], self.send.at[t], self.recv.at[slot], (self.at.e, there)
        )

    def give(self, t):
        z = self.at.z

        @pl.when(((t > z) & (z > 0)) | ((t < z) & (z < 3)))
        def _():
            self.arrival(t).wait_recv()

            @pl.loop(0, self.part.shape[1] // 32)
            def _(i):
                here = pl.ds(pl.multiple_of(i * 32, 32), 32)
                self.part[t, here] = (
                    self.part[t, here].astype(F32) + self.came[t, here].astype(F32)
                ).astype(BF)

        self.copy(t).start()

    def give_far(self):
        half = self.at.half
        self.give(jnp.where(half == 0, 3, 0))
        self.give(jnp.where(half == 0, 2, 1))

    def give_near(self, early):
        z = self.at.z
        outer = (z == 0) | (z == 3)

        @pl.when(outer if early else jnp.logical_not(outer))
        def _():
            self.give(self.at.partner)

    def wait(self):
        z = self.at.z
        zero = jnp.zeros(self.came.shape[1:], BF)

        @pl.when(z > 0)
        def _():
            self.arrival(z).wait_recv()

        @pl.when(z == 0)
        def _():
            self.came[0] = zero

        @pl.when(z < 3)
        def _():
            self.arrival(4).wait_recv()

        @pl.when(z == 3)
        def _():
            self.came[4] = zero

    def total(self, here):
        return self.came[self.at.z, here].astype(F32) + self.came[4, here].astype(F32)

    def end(self):
        for t in range(4):

            @pl.when(t != self.at.z)
            def _():
                self.copy(t).wait_send()

    @staticmethod
    def semaphores():
        return [pltpu.SemaphoreType.DMA((4,)), pltpu.SemaphoreType.DMA((5,))]


class Gather:
    def __init__(self, at, block, sems, sibling=True):
        self.at, self.block, self.sibling = at, block, sibling
        (self.x_send, self.x_recv, self.y_send, self.y_recv) = sems[:4]
        self.half_send, self.half_recv = sems[4:6]
        if sibling:
            self.sib_send, self.sib_recv = sems[6:8]

    def to_x(self, k):
        block = self.block(k, OWN)
        return remote(block, block, self.x_send.at[k], self.x_recv.at[k], self.at.x_near)

    def to_y(self, k):
        block = self.block(k, OWN)
        return remote(block, block, self.y_send.at[k], self.y_recv.at[k], self.at.y_near)

    def on_y(self, k):
        block = self.block(k, XCOL, 0)
        sem = 2 * k
        return remote(block, block, self.half_send.at[sem], self.half_recv.at[sem], self.at.y_near)

    def on_x(self, k):
        block = self.block(k, YCOL, 1)
        sem = 2 * k + 1
        return remote(block, block, self.half_send.at[sem], self.half_recv.at[sem], self.at.x_near)

    def to_sib(self, k, q):
        block = self.block(k, q)
        sem = 4 * k + q
        return remote(block, block, self.sib_send.at[sem], self.sib_recv.at[sem], self.at.sibling)

    def share(self, k, q):
        if self.sibling:
            self.to_sib(k, q).start()

    def own(self, k):
        self.to_x(k).start()
        self.to_y(k).start()
        self.share(k, OWN)

    def cross(self, k, halves=True):
        self.to_x(k).wait_recv()
        if halves:
            self.on_y(k).start()
        self.share(k, XCOL)
        self.to_y(k).wait_recv()
        if halves:
            self.on_x(k).start()
        self.share(k, YCOL)

    def diag(self, k):
        self.on_y(k).wait_recv()
        self.on_x(k).wait_recv()
        self.share(k, DIAG)

    def ready(self, k, q):
        self.to_sib(k, q).wait_recv()

    def end(self, k, halves=True):
        self.to_x(k).wait_send()
        self.to_y(k).wait_send()
        if halves:
            self.on_x(k).wait_send()
            self.on_y(k).wait_send()
        for q in range(4) if self.sibling else ():
            self.to_sib(k, q).wait_send()

    @staticmethod
    def semaphores(sibling=True):
        dma = pltpu.SemaphoreType.DMA
        return [dma((4,))] * 4 + [dma((8,))] * 2 + [dma((16,))] * 2 * sibling


def expert_kernel(
    second_ref,
    cot_ref,
    gate_ref,
    up_ref,
    down_ref,
    sums_ref,
    gate_grad_ref,
    up_grad_ref,
    down_grad_ref,
    kept_ref,
    held,
    part,
    diag_a,
    diag_b,
    diag_z,
    x_whole,
    y_whole,
    z_part,
    pair_part,
    cot_tile,
    gate_up,
    down,
    acts,
    back,
    gate_tile,
    hidden_tile,
    kept_tile,
    grad_tile,
    widen,
    narrow,
    load_sem,
    gift_send,
    gift_recv,
    cot_sem,
    kept_sem,
    grad_sem,
    reload_sem,
    over_sem,
    red_send,
    red_recv,
    zr_send,
    zr_recv,
    pair_send,
    pair_recv,
    give_send,
    give_recv,
    give_ready,
    *sems,
):
    at = Place()
    rows = second_ref.shape[0]
    pair, quad = 2 * rows, 4 * rows
    total_rows, carried = held.shape
    model = cot_ref.shape[1]
    wide = down.shape[0]
    own_wide = wide // 2
    units = wide // 4
    half = rows // 2
    partner = (at.e, at.partner)
    experts_all = 16
    loads, gifts = [], []
    for i, (ref, held_weights, first) in enumerate(
        ((gate_ref, gate_up, 0), (up_ref, gate_up, wide), (down_ref, down, 0))
    ):
        here = pl.ds(pl.multiple_of(first + at.core * own_wide, own_wide), own_wide)
        loads.append(pltpu.make_async_copy(ref, held_weights.at[here], load_sem.at[i]))
        gifts.append(
            remote(ref, held_weights.at[here], gift_send.at[i], gift_recv.at[i], at.sibling)
        )
    for copy in loads:
        copy.start()

    def named(shape, unit_axis):
        unit = lax.broadcasted_iota(jnp.int32, shape, unit_axis)
        lane = lax.broadcasted_iota(jnp.int32, shape, 1 - unit_axis)
        expert = at.e // 2 * 4
        for i in (1, 2, 3):
            expert = expert + (unit >= i * units).astype(jnp.int32)
        return ((lane == expert) | (lane == expert + experts_all)).astype(F32).astype(BF)

    widen[...] = named((EXTRA, wide), 1)
    narrow[...] = named((wide, EXTRA), 0)
    meet(at.everyone())
    for copy in gifts:
        copy.start()

    def side_first(k, side):
        return (at.plane(k) * 4 + (at.y if side else 1 - at.y) * 2) * rows

    def side_rows(k, side):
        return pl.ds(pl.multiple_of(side_first(k, side), pair), pair)

    def block(k, q, i=None):
        first, count = (0, rows) if i is None else (i * half, half)
        first = (at.plane(k) * 4 + at.column_base(q) // 2) * rows + first
        return held.at[pl.ds(pl.multiple_of(first, half), count)]

    def line_block(b):
        first = (b * 4 + at.column_base(OWN) // 2) * rows
        return held.at[pl.ds(pl.multiple_of(first, rows), rows)]

    line = Line(at, line_block, sems[:2])
    gather = Gather(at, block, sems[2:], sibling=False)
    first_row = (at.z * 4 + at.column_base(OWN) // 2) * rows
    held[pl.ds(pl.multiple_of(first_row, rows), rows)] = second_ref[...]
    line.begin()
    gather.own(0)

    def over_z(k):
        there = block(k, DIAG)
        return remote(there, there, over_sem.at[0], over_sem.at[1], partner)

    def cot_copy(k, side):
        return pltpu.make_async_copy(cot_ref.at[side_rows(k, side)], cot_tile, cot_sem)

    def kept_copy(k, side):
        return pltpu.make_async_copy(kept_tile, kept_ref.at[:, side_rows(k, side)], kept_sem)

    def compute(r, k, side, following):
        here = side_rows(k, side)
        acts[...] = lax.dot_general(
            held[here, :model], gate_up[...], (NT, ((), ())), preferred_element_type=F32
        )
        cot_copy(k, side).wait()
        back[...] = lax.dot_general(
            cot_tile[...], down[...], (NT, ((), ())), preferred_element_type=F32
        )
        following()

        @when(not (isinstance(r, int) and r == 0 and side == 1))
        def _():
            kept_copy(k, side).wait()

        out_first = r * quad + side * pair
        for i in range(pair // rows):
            strip_rows = slice(i * rows, (i + 1) * rows)
            first = side_first(k, side) + i * rows
            share_rows = held[pl.ds(pl.multiple_of(first, rows), rows), model:]
            gate_act, up_act = acts[strip_rows, :wide], acts[strip_rows, wide:]
            raw_back = back[strip_rows]
            share = jnp.dot(share_rows, widen[...], preferred_element_type=F32)
            sigmoid = 1.0 / (1.0 + jnp.exp(-gate_act))
            silu = gate_act * sigmoid
            hidden = silu * up_act
            product = hidden * raw_back
            high = product.astype(BF)
            low = (product - high.astype(F32)).astype(BF)
            share_grad = jnp.dot(high, narrow[...], preferred_element_type=F32) + jnp.dot(
                low, narrow[...], preferred_element_type=F32
            )
            lane = lax.broadcasted_iota(jnp.int32, share_grad.shape, 1)
            rounded = share_grad.astype(BF).astype(F32)
            share_grad = jnp.where(lane < experts_all, rounded, share_grad - rounded)
            hidden_low = (share * hidden).astype(BF)
            hidden_grad = share * raw_back
            gate_grad = (
                hidden_grad * up_act * sigmoid * (1.0 + gate_act * (1.0 - sigmoid))
            ).astype(BF)
            up_grad = (hidden_grad * silu).astype(BF)
            gate_tile[strip_rows, :wide] = gate_grad
            gate_tile[strip_rows, wide:] = up_grad
            hidden_tile[strip_rows] = hidden_low
            kept_tile[:wide, strip_rows] = gate_grad.T
            kept_tile[wide : 2 * wide, strip_rows] = up_grad.T
            kept_tile[2 * wide :, strip_rows] = hidden_low.T
            out_rows = pl.ds(pl.multiple_of(out_first + i * rows, rows), rows)
            part[out_rows, 2 * model :] = share_grad.astype(BF)
        kept_copy(k, side).start()
        there = pl.ds(pl.multiple_of(out_first, pair), pair)
        step = 512
        for start in range(0, model, step):
            part[there, start : start + step] = jnp.dot(
                hidden_tile[...], down[:, start : start + step], preferred_element_type=F32
            ).astype(BF)
            part[there, model + start : model + start + step] = jnp.dot(
                gate_tile[...], gate_up[:, start : start + step], preferred_element_type=F32
            ).astype(BF)

    def part_row(r, q, first=0):
        x = at.x if q in (YCOL, OWN) else 1 - at.x
        return r * quad + (pair if q in (XCOL, OWN) else 0) + x * rows + first

    def part_rows(r, q, first, count):
        return pl.ds(pl.multiple_of(part_row(r, q, first), min(count, half)), count)

    def half_a(r):
        src = part.at[part_rows(r, DIAG, 0, half)]
        return remote(src, diag_a.at[r % 2], red_send.at[0, r], red_recv.at[0, r], at.y_near)

    def half_b(r):
        src = part.at[part_rows(r, DIAG, half, half)]
        return remote(src, diag_b.at[r % 2], red_send.at[1, r], red_recv.at[1, r], at.x_near)

    def x_copy(r):
        src = part.at[part_rows(r, XCOL, 0, rows)]
        return remote(src, x_whole.at[r % 2], red_send.at[2, r], red_recv.at[2, r], at.x_near)

    def y_copy(r):
        src = part.at[part_rows(r, YCOL, 0, rows)]
        return remote(src, y_whole.at[r % 2], red_send.at[3, r], red_recv.at[3, r], at.y_near)

    def diag_over():
        src = part.at[part_rows(0, DIAG, 0, rows)]
        return remote(src, diag_z, red_send.at[0, 0], red_recv.at[0, 0], partner)

    strip = 32

    def by_strips(count, body):
        @pl.loop(0, count // strip)
        def _(i):
            body(pl.multiple_of(i * strip, strip))

    def reduce_diag(r):
        @when(r == 3)
        def _():
            diag_over().wait_recv()

            def body(row):
                here = part_rows(r, DIAG, row, strip)
                part[here] = (
                    part[here].astype(F32) + diag_z[pl.ds(row, strip)].astype(F32)
                ).astype(BF)

            by_strips(rows, body)

        @when(r == 0)
        def _():
            diag_over().start()

        @when(r > 0)
        def _():
            half_a(r).start()
            half_b(r).start()

    def reduce_x(r):
        @when(r > 0)
        def _():
            half_a(r).wait_recv()

            def body(row):
                here = part_rows(r, XCOL, row, strip)
                part[here] = (
                    part[here].astype(F32) + diag_a[r % 2, pl.ds(row, strip)].astype(F32)
                ).astype(BF)

            by_strips(half, body)

        x_copy(r).start()

    def reduce_y(r):
        @when(r > 0)
        def _():
            half_b(r).wait_recv()

            def body(row):
                here = part_rows(r, YCOL, half + row, strip)
                part[here] = (
                    part[here].astype(F32) + diag_b[r % 2, pl.ds(row, strip)].astype(F32)
                ).astype(BF)

            by_strips(half, body)

        y_copy(r).start()

    inner = (at.z == 1) | (at.z == 2)

    def near_copy():
        src = part.at[part_rows(0, OWN, 0, rows)]
        return remote(src, z_part.at[0], zr_send.at[0], zr_recv.at[0], partner)

    def pair_copy(r):
        block = pair_part.at[r - 1]
        return remote(block, block, pair_send.at[r - 1], pair_recv.at[r - 1], partner)

    def far_copy(r):
        there = at.plane(r + 1)
        return remote(
            pair_part.at[r - 1], z_part.at[1], zr_send.at[r], zr_recv.at[1], (at.e, there)
        )

    def pass_on(r):
        @pl.when(inner)
        def _():
            pair_copy(r).wait_recv()

            def body(row):
                here = pl.ds(row, strip)
                pair_part[r - 1, here] = (
                    pair_part[r - 1, here].astype(F32)
                    + part[part_rows(r, OWN, row, strip)].astype(F32)
                ).astype(BF)

            by_strips(rows, body)
            far_copy(r).start()

    def reduce_own(r):
        x_copy(r).wait_recv()
        y_copy(r).wait_recv()

        def total(row):
            here = pl.ds(row, strip)
            return (
                part[part_rows(r, OWN, row, strip)].astype(F32)
                + x_whole[r % 2, here].astype(F32)
                + y_whole[r % 2, here].astype(F32)
            )

        @when(r == 3)
        def _():
            near_copy().wait_recv()
            block = z_part.at[1]
            remote(block, block, zr_send.at[0], zr_recv.at[1], at.sibling).wait_recv()

            def body(row):
                here = pl.ds(row, strip)
                sums_ref[here] = total(row) + (
                    z_part[0, here].astype(F32) + z_part[1, here].astype(F32)
                )

            by_strips(rows, body)

        def keep(row):
            part[part_rows(r, OWN, row, strip)] = total(row).astype(BF)

        def lay_out(row):
            pair_part[r - 1, pl.ds(row, strip)] = total(row).astype(BF)

        @when(r == 0)
        def _():
            by_strips(rows, keep)
            near_copy().start()

        @when(between(r, 1, 2))
        def _():
            @pl.when(inner)
            def _():
                by_strips(rows, keep)

            @pl.when(jnp.logical_not(inner))
            def _():
                by_strips(rows, lay_out)
                pair_copy(r).start()

    def far_rows(k):
        line.arrive(k)
        gather.own(k)

    cot_copy(1, 1).start()
    line.arrive(1)
    gather.own(1)

    @pl.when(inner)
    def _():
        far_rows(2)

    gather.cross(0)
    gather.cross(1, halves=False)

    @pl.when(inner)
    def _():
        far_rows(3)

    for copy in loads + gifts:
        copy.wait()
    compute(0, 1, 1, lambda: cot_copy(1, 0).start())
    reduce_x(0)
    gather.diag(0)
    over_z(0).start()

    @pl.when(jnp.logical_not(inner))
    def _():
        far_rows(2)

    over_z(1).wait_recv()
    compute(0, 1, 0, lambda: cot_copy(2, 0).start())
    reduce_y(0)
    reduce_diag(0)

    @pl.when(jnp.logical_not(inner))
    def _():
        far_rows(3)

    gather.cross(2)
    gather.diag(2)
    compute(1, 2, 0, lambda: cot_copy(2, 1).start())
    reduce_diag(1)
    gather.cross(3)

    @pl.loop(1, 3)
    def _(r):
        k, later = r + 1, lax.rem(r + 2, 4)
        compute(r, k, 1, lambda: cot_copy(later, 0).start())
        reduce_own(r - 1)

        @pl.when(r == 1)
        def _():
            gather.diag(3)

        compute(r + 1, later, 0, lambda: cot_copy(later, 1).start())
        reduce_x(r)
        reduce_y(r)

        @pl.when(r == 2)
        def _():
            pass_on(1)

        reduce_diag(r + 1)

    compute(3, 0, 1, lambda: None)

    line.end()
    over_z(0).wait_send()
    diag_over().wait_send()
    near_copy().wait_send()
    x_copy(0).wait_send()
    y_copy(0).wait_send()
    for copy in (half_a(1), half_b(1), x_copy(1), y_copy(1)):
        copy.wait_send()
    pl.semaphore_signal(give_ready, inc=1, device_id=at.sibling, device_id_type=MESH)
    for k in range(4):
        gather.end(k, halves=k != 1)
    kept_copy(0, 1).wait()
    turned = [
        pltpu.make_async_copy(kept_ref.at[pl.ds(0, 2 * wide)], gate_up, load_sem.at[0]),
        pltpu.make_async_copy(kept_ref.at[pl.ds(2 * wide, wide)], down, load_sem.at[1]),
    ]
    for copy in turned:
        copy.start()
    step = 256
    chunks = model // step
    mine, theirs = at.core * own_wide, (1 - at.core) * own_wide

    def lanes_of(n):
        return pl.ds(pl.multiple_of(n * step, step), step)

    def turned_rows(first):
        return pl.ds(pl.multiple_of(first, own_wide), own_wide)

    def given(i, first, size):
        return part.at[pl.ds(0, own_wide), pl.ds(pl.multiple_of(i * model + first, step), size)]

    def taken(i, first, size):
        return part.at[pl.ds(quad, own_wide), pl.ds(pl.multiple_of(i * model + first, step), size)]

    def give_copies(n):
        first, size = n % 2 * (model // 2), model // 2
        return [
            remote(
                given(i, first, size),
                taken(i, first, size),
                give_send.at[n, i],
                give_recv.at[n, i],
                at.sibling,
            )
            for i in ((0, 1) if n < 2 else (0,))
        ]

    def gate_out(n):
        slot = lax.rem(n, 2)
        return [
            pltpu.make_async_copy(
                grad_tile.at[slot, pl.ds(i * own_wide, own_wide)],
                ref.at[:, lanes_of(n)],
                grad_sem.at[slot, i],
            )
            for i, ref in enumerate((gate_grad_ref, up_grad_ref))
        ]

    def down_out(n):
        slot = lax.rem(n, 2)
        return pltpu.make_async_copy(
            grad_tile.at[slot, pl.ds(0, own_wide)],
            down_grad_ref.at[:, lanes_of(n)],
            grad_sem.at[slot, 0],
        )

    def reload(n):
        return pltpu.make_async_copy(
            cot_ref.at[:, lanes_of(n)], held.at[:, lanes_of(n)], reload_sem.at[n]
        )

    def gate_up_chunk(first, i, n):
        return jnp.dot(
            gate_up[turned_rows(i * wide + first)],
            held[:, lanes_of(n)],
            preferred_element_type=F32,
        )

    def down_chunk(first, n):
        return jnp.dot(
            down[turned_rows(first)], held[:, lanes_of(n)], preferred_element_type=F32
        )

    def in_half(n, body):
        half_chunks = chunks // 2
        pl.loop(n % 2 * half_chunks, (n % 2 + 1) * half_chunks)(body)

    for copy in turned:
        copy.wait()
    for part_of in (0, 1):

        def give_gate_up(n):
            for i in (0, 1):
                given(i, n * step, step)[...] = gate_up_chunk(theirs, i, n).astype(BF)

        in_half(part_of, give_gate_up)
        if part_of == 0:
            pl.semaphore_wait(give_ready, 1)
        for copy in give_copies(part_of):
            copy.start()

    reduce_own(2)
    for part_of in (0, 1):
        for copy in give_copies(part_of):
            copy.wait_recv()

        def own_gate_up(n):
            @pl.when(n >= 2)
            def _():
                for copy in gate_out(n):
                    copy.wait()

            for i in (0, 1):
                grad_tile[lax.rem(n, 2), i * own_wide : (i + 1) * own_wide] = gate_up_chunk(
                    mine, i, n
                ) + taken(i, n * step, step)[...].astype(F32)
            for copy in gate_out(n):
                copy.start()
            reload(n).start()

        in_half(part_of, own_gate_up)

    pl.semaphore_signal(give_ready, inc=1, device_id=at.sibling, device_id_type=MESH)
    reduce_x(3)
    reduce_y(3)
    pass_on(2)
    for part_of in (0, 1):
        for copy in give_copies(part_of):
            copy.wait_send()
    for part_of in (2, 3):

        def give_down(n):
            reload(n).wait()
            given(0, n * step, step)[...] = down_chunk(theirs, n).astype(BF)

        in_half(part_of, give_down)
        if part_of == 2:
            pl.semaphore_wait(give_ready, 1)
        for copy in give_copies(part_of):
            copy.start()

    for n in (0, 1):
        for copy in gate_out(n):
            copy.wait()
    for part_of in (2, 3):
        for copy in give_copies(part_of):
            copy.wait_recv()

        def own_down(n):
            @pl.when(n >= 2)
            def _():
                down_out(n).wait()

            grad_tile[lax.rem(n, 2), :own_wide] = down_chunk(mine, n) + taken(0, n * step, step)[
                ...
            ].astype(F32)
            down_out(n).start()

        in_half(part_of, own_down)

    reduce_own(3)
    for n in (0, 1):
        down_out(n).wait()

    for n in (2, 3):
        for copy in give_copies(n):
            copy.wait_send()
    for r in (2, 3):
        for copy in (half_a(r), half_b(r), x_copy(r), y_copy(r)):
            copy.wait_send()
    for r in (1, 2):

        @pl.when(inner)
        def _():
            far_copy(r).wait_send()

        @pl.when(jnp.logical_not(inner))
        def _():
            pair_copy(r).wait_send()


def experts_in_one(second_wide, cot_all, gate, up, down):
    rows, carried = second_wide.shape
    total_rows, model = cot_all.shape
    wide = 2 * down.shape[0]
    pair, half = 2 * rows, rows // 2
    both = 2 * model + EXTRA
    vmem = pl.BlockSpec(memory_space=pltpu.VMEM)
    hbm = pl.BlockSpec(memory_space=pl.ANY)
    dma = pltpu.SemaphoreType.DMA
    shape = jax.ShapeDtypeStruct
    return pl.pallas_call(
        expert_kernel,
        out_shape=(
            shape((rows, both), F32),
            shape((wide // 2, model), F32),
            shape((wide // 2, model), F32),
            shape((wide // 2, model), F32),
            shape((3 * wide, total_rows), BF),
        ),
        in_specs=[vmem, hbm, hbm, hbm, hbm],
        out_specs=(vmem, hbm, hbm, hbm, hbm),
        scratch_shapes=[
            pltpu.VMEM((total_rows, carried), BF),
            pltpu.VMEM((16 * rows, both), BF),
            pltpu.VMEM((2, half, both), BF),
            pltpu.VMEM((2, half, both), BF),
            pltpu.VMEM((rows, both), BF),
            pltpu.VMEM((2, rows, both), BF),
            pltpu.VMEM((2, rows, both), BF),
            pltpu.VMEM((2, rows, both), BF),
            pltpu.VMEM((2, rows, both), BF),
            pltpu.VMEM((pair, model), BF),
            pltpu.VMEM((2 * wide, model), BF),
            pltpu.VMEM((wide, model), BF),
            pltpu.VMEM((pair, 2 * wide), F32),
            pltpu.VMEM((pair, wide), F32),
            pltpu.VMEM((pair, 2 * wide), BF),
            pltpu.VMEM((pair, wide), BF),
            pltpu.VMEM((3 * wide, pair), BF),
            pltpu.VMEM((2, wide, 256), F32),
            pltpu.VMEM((EXTRA, wide), BF),
            pltpu.VMEM((wide, EXTRA), BF),
            dma((3,)),
            dma((3,)),
            dma((3,)),
            dma,
            dma,
            dma((2, 2)),
            dma((model // 256,)),
            dma((2,)),
            dma((4, 4)),
            dma((4, 4)),
            dma((3,)),
            dma((2,)),
            dma((2,)),
            dma((2,)),
            dma((4, 2)),
            dma((4, 2)),
            pltpu.SemaphoreType.REGULAR,
            *Line.semaphores(),
            *Gather.semaphores(False),
        ],
        compiler_params=pltpu.CompilerParams(
            collective_id=0, has_side_effects=True, vmem_limit_bytes=VMEM_BYTES
        ),
        cost_estimate=pl.CostEstimate(
            flops=2 * total_rows * model * wide * 9,
            bytes_accessed=8 * total_rows * model,
            transcendentals=total_rows * wide,
        ),
    )(second_wide, cot_all, gate, up, down)


def between(r, low, high):
    if isinstance(r, int):
        return low <= r <= high
    return (r >= low) & (r <= high)


class Tree:
    def __init__(self, at, refs, sems):
        (self.part, self.from_sib, self.diag_sum, self.x_sum, self.y_sum) = refs[:5]
        (self.diag_a, self.diag_b, self.x_whole, self.y_whole) = refs[5:]
        self.part_send, self.part_recv, self.send, self.recv = sems
        self.at = at
        self.rows = self.diag_sum.shape[0]
        self.half = self.rows // 2
        self.strip = 32

    def part_copy(self, q):
        return remote(
            self.part.at[q, 1 - self.at.core],
            self.from_sib.at[q],
            self.part_send.at[q],
            self.part_recv.at[q],
            self.at.sibling,
        )

    def half_a(self):
        there = self.diag_sum.at[pl.ds(0, self.half)]
        return remote(there, self.diag_a, self.send.at[0], self.recv.at[0], self.at.y_near)

    def half_b(self):
        there = self.diag_sum.at[pl.ds(self.half, self.half)]
        return remote(there, self.diag_b, self.send.at[1], self.recv.at[1], self.at.x_near)

    def x_copy(self):
        return remote(self.x_sum, self.x_whole, self.send.at[2], self.recv.at[2], self.at.x_near)

    def y_copy(self):
        return remote(self.y_sum, self.y_whole, self.send.at[3], self.recv.at[3], self.at.y_near)

    def strips(self, first, count, body):
        strip = self.strip

        @pl.loop(first // strip, (first + count) // strip)
        def _(i):
            body(pl.ds(pl.multiple_of(i * strip, strip), strip), i)

    def chip_sum(self, q, here):
        return self.part[q, self.at.core, here].astype(F32) + self.from_sib[q, here].astype(F32)

    def do_diag(self):
        self.part_copy(DIAG).wait_recv()

        def body(here, i):
            self.diag_sum[here] = self.chip_sum(DIAG, here).astype(BF)

        self.strips(0, self.rows, body)
        self.half_a().start()
        self.half_b().start()

    def do_x(self):
        self.part_copy(XCOL).wait_recv()
        self.half_a().wait_recv()

        def with_half(here, i):
            self.x_sum[here] = (
                self.chip_sum(XCOL, here) + self.diag_a[here].astype(F32)
            ).astype(BF)

        def alone(here, i):
            self.x_sum[here] = self.chip_sum(XCOL, here).astype(BF)

        self.strips(0, self.half, with_half)
        self.strips(self.half, self.half, alone)
        self.x_copy().start()

    def do_y(self):
        self.part_copy(YCOL).wait_recv()
        self.half_b().wait_recv()

        def alone(here, i):
            self.y_sum[here] = self.chip_sum(YCOL, here).astype(BF)

        def with_half(here, i):
            low = pl.ds(pl.multiple_of(i * self.strip - self.half, self.strip), self.strip)
            self.y_sum[here] = (self.chip_sum(YCOL, here) + self.diag_b[low].astype(F32)).astype(BF)

        self.strips(0, self.half, alone)
        self.strips(self.half, self.half, with_half)
        self.y_copy().start()

    def do_own(self, result):
        self.part_copy(OWN).wait_recv()
        self.x_copy().wait_recv()
        self.y_copy().wait_recv()

        def body(here, i):
            result[here] = (
                self.chip_sum(OWN, here)
                + self.x_whole[here].astype(F32)
                + self.y_whole[here].astype(F32)
            ).astype(BF)

        self.strips(0, self.rows, body)

    def drain(self):
        for q in range(4):
            self.part_copy(q).wait_send()
        for copy in (self.half_a(), self.half_b(), self.x_copy(), self.y_copy()):
            copy.wait_send()

    @staticmethod
    def buffers(rows, width):
        piece = pltpu.VMEM((rows, width), BF)
        half = pltpu.VMEM((rows // 2, width), BF)
        return [
            pltpu.VMEM((4, 2, rows, width), BF),
            pltpu.VMEM((4, rows, width), BF),
            piece,
            piece,
            piece,
            half,
            half,
            piece,
            piece,
        ]

    @staticmethod
    def semaphores():
        return [pltpu.SemaphoreType.DMA((4,))] * 4


class Spread:
    def __init__(self, at, own, out, sems, first=0):
        self.at, self.own, self.out, self.first = at, own, out, first
        self.send, self.recv, self.local = sems
        self.rows = own.shape[0]
        self.stride = out.shape[0] // 8
        self.e_x, self.e_y, self.e_d = at.x_near[0], at.y_near[0], at.diagonal

    def place(self, slot, first=0, rows=None):
        row = slot * self.stride + self.first + first
        rows = rows or self.rows
        return self.out.at[pl.ds(pl.multiple_of(row, rows), rows)]

    def to(self, src, slot, device, sem):
        return remote(src, self.place(slot), self.send.at[sem], self.recv.at[sem], device)

    def own_copies(self):
        e = self.at.e
        return (
            self.to(self.own, e, self.at.x_near, 0),
            self.to(self.own, e, self.at.y_near, 1),
            self.to(self.own, e, self.at.sibling, 2),
        )

    def here(self):
        return pltpu.make_async_copy(self.own, self.place(self.at.e), self.local)

    def half_copy(self, slot, first, device, sem):
        there = self.place(slot, first, self.rows // 2)
        return remote(there, there, self.send.at[sem], self.recv.at[sem], device)

    def cross_copies(self):
        return (
            self.half_copy(self.e_x, 0, self.at.y_near, 3),
            self.half_copy(self.e_y, self.rows // 2, self.at.x_near, 4),
            self.to(self.place(self.e_x), self.e_x, self.at.sibling, 5),
            self.to(self.place(self.e_y), self.e_y, self.at.sibling, 6),
        )

    def diag_copy(self):
        return self.to(self.place(self.e_d), self.e_d, self.at.sibling, 7)

    def begin(self):
        for copy in self.own_copies():
            copy.start()
        self.here().start()

    def cross(self):
        x, y, s = self.own_copies()
        x.wait_recv()
        y.wait_recv()
        for copy in self.cross_copies():
            copy.start()
        s.wait_recv()

    def diag(self):
        a, b, s, t = self.cross_copies()
        a.wait_recv()
        b.wait_recv()
        self.diag_copy().start()
        s.wait_recv()
        t.wait_recv()

    def end(self):
        self.diag_copy().wait()
        for copy in self.own_copies() + self.cross_copies():
            copy.wait_send()
        self.here().wait()

    @staticmethod
    def semaphores():
        dma = pltpu.SemaphoreType.DMA
        return [dma((8,)), dma((8,)), dma]


def swap(v):
    return pltpu.roll(v, v.shape[-1] // 2, v.ndim - 1)


def fold(v):
    return jnp.sum(v.reshape(v.shape[0] // 8, 8, v.shape[1]), axis=0)


def split_rows(v):
    high = v.astype(BF)
    return jnp.concatenate([v, v - high.astype(F32)], axis=0).astype(BF)


def back_kernel(
    middle_ref,
    share_ref,
    cot_ref,
    router_ref,
    small_ref,
    cos_ref,
    sin_ref,
    second_ref,
    place_ref,
    sums_ref,
    w_out_ref,
    w_cols_ref,
    mixed_ref,
    normed_ref,
    raw_ref,
    prob_ref,
    dnormed_ref,
    block_out_ref,
    middle_grad_ref,
    out_grad_ref,
    cols_grad_ref,
    w_out_held,
    w_cols_held,
    mixed_held,
    normed_held,
    raw_held,
    prob_held,
    held,
    raw_grad,
    left,
    right,
    share_sum,
    router_wide,
    rows_out,
    rows_in,
    gain_total,
    head_total,
    out_total,
    *rest,
):
    at = Place()
    rows, model = middle_ref.shape
    quarter = model // 4
    experts_all = router_ref.shape[1]
    own_part = dnormed_ref
    pair = 2 * rows
    width = HEAD_WIDTH
    heads = w_out_ref.shape[0] // width
    q_cols = heads * width
    cols = w_cols_ref.shape[1]
    count = model // 4 // 8
    scale = HEAD_WIDTH ** (-0.5)
    rest = list(rest)

    def grab(count):
        got, rest[:] = rest[:count], rest[count:]
        return got

    cols_totals, cols_alls = grab(2), grab(2)
    out_tree = Tree(at, grab(9), grab(4))
    cols_trees = [Tree(at, grab(9), grab(4)) for _ in (0, 1)]
    out_spread = Spread(at, out_total, out_grad_ref, grab(3))
    cols_spreads = [
        Spread(at, cols_alls[i], cols_grad_ref, grab(3), i * (count // 2)) for i in (0, 1)
    ]

    def line_block(b):
        return held.at[pl.ds(pl.multiple_of(b * rows, rows), rows)]

    line = Line(at, line_block, grab(2))
    sums = LineSum(at, rows_out, rows_in, grab(2))
    outer = (at.z == 0) | (at.z == 3)
    ex_send, ex_recv, ex_local, load_sem, sum_sem = grab(5)
    loads = [
        pltpu.make_async_copy(src, dst, load_sem.at[i])
        for i, (src, dst) in enumerate(
            (
                (w_out_ref, w_out_held),
                (raw_ref, raw_held),
                (w_cols_ref, w_cols_held),
                (normed_ref, normed_held),
                (prob_ref, prob_held),
                (mixed_ref, mixed_held),
            )
        )
    ]

    def sum_copy(j):
        lanes = pl.ds(pl.multiple_of(j * EXTRA, EXTRA), EXTRA)
        return pltpu.make_async_copy(sums_ref.at[:, lanes], prob_held.at[j], sum_sem.at[0])

    greet(at.everyone())
    columns = 2 * model // EXTRA
    share_copy = pltpu.make_async_copy(
        sums_ref.at[:, pl.ds(2 * model, EXTRA)], share_sum, sum_sem.at[1]
    )
    share_copy.start()

    @pl.loop(0, columns)
    def _(j):
        sum_copy(j).start()

    for copy in loads[:4]:
        copy.start()

    row_id = lax.broadcasted_iota(jnp.int32, right.shape, 0)
    lane_id = lax.broadcasted_iota(jnp.int32, right.shape, 1)
    chosen = (lane_id == experts_all) & (row_id >= rows) & (row_id < 2 * rows)
    for i in (0, 1, 2):
        first = 2 * rows + 16 * i
        chosen = chosen | (
            (lane_id == experts_all + 1 + i) & (row_id >= first) & (row_id < first + 16)
        )
    right[...] = chosen.astype(F32).astype(BF)
    router_wide[...] = jnp.zeros_like(router_wide)
    left[pl.ds(0, rows)] = second_ref[:, :model]
    left[pl.ds(2 * rows, rows)] = jnp.zeros((rows, model), BF)
    lane = lax.broadcasted_iota(jnp.int32, (rows, EXTRA), 1)
    share = share_ref[...]
    share_copy.wait()
    dshare = share_sum[...]
    dshare = dshare + pltpu.roll(dshare, EXTRA - experts_all, 1)
    weighed = jnp.where(lane < experts_all, share * dshare, 0.0)
    mean_share = jnp.sum(weighed, axis=-1, keepdims=True)
    logit_grad = jnp.where(lane < experts_all, share * (dshare - mean_share), 0.0).astype(BF)
    right[pl.ds(0, rows)] = logit_grad
    middle = middle_ref[...]
    inverse = lax.rsqrt(jnp.mean(middle * middle, axis=-1, keepdims=True) + epsilon)
    mean = jnp.zeros((rows, 1), F32)

    @pl.loop(0, columns)
    def _(j):
        sum_copy(j).wait()

    for j in range(4):
        router_wide[:experts_all, j * quarter : (j + 1) * quarter] = router_ref[j]
    for j in range(model // EXTRA):
        lanes = slice(j * EXTRA, (j + 1) * EXTRA)
        block_out_ref[:, lanes] = (middle[:, lanes] + prob_held[j]).astype(BF)
        second_grad = prob_held[model // EXTRA + j] + dot(logit_grad, router_wide[:, lanes], NN)
        unit = middle[:, lanes] * inverse
        left[rows : 2 * rows, lanes] = (second_grad * unit).astype(BF)
        of = j * EXTRA % quarter
        scaled = second_grad * small_ref[j * EXTRA // quarter, 1:2, of : of + EXTRA]
        middle_grad_ref[:, lanes] = scaled
        mean += jnp.sum(scaled * unit, axis=-1, keepdims=True)
    loads[4].start()
    loads[5].start()
    mean = mean / model
    middle_grad = cot_ref[...].astype(F32) + inverse * (
        middle_grad_ref[...] - middle * inverse * mean
    )
    middle_grad_ref[...] = middle_grad
    head_gains = small_ref[0, 2:3, :] + small_ref[1, 2:3, :]
    head_gains += small_ref[2, 2:3, :] + small_ref[3, 2:3, :]

    held[pl.ds(pl.multiple_of(at.z * rows, rows), rows)] = middle_grad.astype(BF)
    meet(at.everyone(), greeted=True)
    line.begin()
    gain_total[...] = jnp.zeros_like(gain_total)
    head_total[...] = jnp.zeros_like(head_total)

    def attention(far):
        first = 2 * (1 - at.half if far else at.half)
        both = pl.ds(pl.multiple_of(first * rows, pair), pair)
        mixed_grads = lax.dot_general(
            held[both, :], w_out_held[...], (NT, ((), ())), preferred_element_type=F32
        ).astype(BF)
        for i in (0, 1):
            heads_back(first + i, mixed_grads[i * rows : (i + 1) * rows])
            if not far and i == 0:

                @pl.when(jnp.logical_not(outer))
                def _():
                    line.arrive(3)

            if far and i == 0:
                out_tree.do_x()
                out_tree.do_y()
        step = 512
        for start in range(0, model, step):
            lanes = slice(start, start + step)
            part = lax.dot_general(
                raw_grad[both, :],
                w_cols_held[start : start + step, :],
                (NT, ((), ())),
                preferred_element_type=F32,
            )
            gain_total[:, lanes] += fold(part * normed_held[both, lanes].astype(F32))
            if not far:
                own_part[:, lanes] = jnp.where(at.z % 2 == 0, part[:rows], part[rows:])
            rows_out[first, :, lanes] = part[:rows].astype(BF)
            rows_out[first + 1, :, lanes] = part[rows:].astype(BF)
        if not far:
            sums.give_near(True)
        else:

            @pl.when(outer)
            def _():
                sums.give_far()

    def heads_back(b, mixed_grad):
        here = pl.ds(pl.multiple_of(b * rows, rows), rows)
        cosine, sine = cos_ref[here, :], sin_ref[here, :]

        def unit_of(v):
            inverse = lax.rsqrt(jnp.mean(v * v, axis=-1, keepdims=True) + epsilon)
            return v * inverse, inverse

        def low_of(unit, gain):
            scaled = unit * gain
            return (scaled * cosine + swap(scaled) * sine).astype(BF)

        def back_of(gradient, unit, inverse, gain, slot):
            turned = gradient * cosine - swap(gradient) * sine
            head_total[slot] += fold(turned * unit)
            return norm_back(turned * gain, unit, inverse).astype(BF)

        q_gain, k_gain = head_gains[:, :width], head_gains[:, width : 2 * width]
        k_unit, k_inverse = unit_of(raw_held[here, q_cols : q_cols + width])
        k_low = low_of(k_unit, k_gain)
        v_low = raw_held[here, q_cols + width : q_cols + 2 * width].astype(BF)
        k_grad = jnp.zeros((rows, width), F32)
        v_grad = jnp.zeros((rows, width), F32)
        for h in range(heads):
            lanes = slice(h * width, (h + 1) * width)
            q_unit, q_inverse = unit_of(raw_held[here, lanes])
            q_low = low_of(q_unit, q_gain)
            prob = prob_held[b * heads + h]
            own_grad = mixed_grad[:, lanes]
            v_grad += dot(prob.astype(BF), own_grad, TN)
            prob_grad = dot(own_grad, v_low, NT)
            score_grad = (
                prob * (prob_grad - jnp.sum(prob * prob_grad, axis=-1, keepdims=True))
            ).astype(BF)
            q_grad = dot(score_grad, k_low, NN) * scale
            k_grad += dot(score_grad, q_low, TN)
            raw_grad[here, lanes] = back_of(q_grad, q_unit, q_inverse, q_gain, 0)
        raw_grad[here, q_cols : q_cols + width] = back_of(
            k_grad * scale, k_unit, k_inverse, k_gain, 1
        )
        raw_grad[here, q_cols + width : q_cols + 2 * width] = v_grad.astype(BF)

    def out_piece(q):
        base = at.column_base(q)
        lanes = pl.ds(pl.multiple_of(base * width, 2 * width), 2 * width)
        left_side = mixed_held[:, lanes]
        step = 512
        for start in range(0, model, step):
            total = dot(left_side, held[:, start : start + step], TN)
            for c in (0, 1):
                out_tree.part[q, c, :, start : start + step] = total[
                    c * width : (c + 1) * width
                ].astype(BF)
        out_tree.part_copy(q).start()

    some = count // 2

    def cols_piece(q):
        base = at.column_base(q)
        for there in range(4):
            lanes = pl.ds(
                pl.multiple_of(there * (model // 4) + base * count, 2 * count), 2 * count
            )
            block = dot(normed_held[:, lanes], raw_grad[...], TN)
            small = dot(left[:, lanes], right[...], TN)
            for c in (0, 1):
                for i, tree in enumerate(cols_trees):
                    of = slice(c * count + i * some, c * count + (i + 1) * some)
                    here = pl.ds(there * some, some)
                    tree.part[q, c, here, :cols] = block[of].astype(BF)
                    tree.part[q, c, here, cols:] = small[of].astype(BF)
        cols_trees[0].part_copy(q).start()

    groups = ((0, q_cols), (q_cols, width), (q_cols + width, width), (cols, EXTRA))

    def exchange_refs(i, to, of):
        here = pl.ds(pl.multiple_of(to * some, some), some)
        first = 0
        refs = []
        for start, size in groups:
            lanes = pl.ds(pl.multiple_of(first + of * size, size), size)
            refs.append((cols_totals[i].at[here, pl.ds(start, size)], cols_alls[i].at[:, lanes]))
            first += 4 * size
        return refs

    def exchange(i, k):
        there = at.plane(k)
        turn = at.turn_at(there)
        return [
            remote(src, dst, ex_send.at[i, k - 1, j], ex_recv.at[i, turn - 1, j], (at.e, there))
            for j, (src, dst) in enumerate(exchange_refs(i, there, at.z))
        ]

    def exchange_arrival(i, k):
        return [
            remote(dst, dst, ex_send.at[i, k - 1, j], ex_recv.at[i, k - 1, j], at.sibling)
            for j, (src, dst) in enumerate(exchange_refs(i, at.z, at.plane(k)))
        ]

    def own_exchange(i):
        return [
            pltpu.make_async_copy(src, dst, ex_local.at[i, j])
            for j, (src, dst) in enumerate(exchange_refs(i, at.z, at.z))
        ]

    def begin_exchange(i):
        cols_trees[i].do_own(cols_totals[i])
        for k in (1, 2, 3):
            for copy in exchange(i, k):
                copy.start()
        for copy in own_exchange(i):
            copy.start()

    def end_exchange(i):
        for copy in own_exchange(i):
            copy.wait()
        for k in (1, 2, 3):
            for copy in exchange_arrival(i, k):
                copy.wait_recv()
        cols_spreads[i].begin()

    line.arrive(1)

    @pl.when(jnp.logical_not(outer))
    def _():
        line.arrive(2)

    for copy in loads[:5]:
        copy.wait()
    attention(False)

    @pl.when(outer)
    def _():
        line.arrive(2)
        line.arrive(3)

    loads[5].wait()
    for q in (DIAG, XCOL, YCOL, OWN):
        out_piece(q)
    out_tree.do_diag()
    attention(True)
    out_tree.do_own(out_total)
    out_spread.begin()
    for j in range(4):
        lanes = slice(j * quarter, (j + 1) * quarter)
        left[pl.ds(2 * rows, 16), lanes] = split_rows(
            gain_total[:, lanes] / small_ref[j, 0:1, :]
        )
    for slot in (0, 1):
        placed = jnp.dot(
            split_rows(head_total[slot]), place_ref[...], preferred_element_type=F32
        )
        left[pl.ds(2 * rows + 16 * (slot + 1), 16)] = placed.astype(BF)
    first, last = cols_trees
    for q in (DIAG, XCOL, YCOL, OWN):
        cols_piece(q)
    for q in (DIAG, XCOL, YCOL, OWN):
        last.part_copy(q).start()
    first.do_diag()
    last.do_diag()
    out_spread.cross()
    first.do_x()
    first.do_y()

    @pl.when(jnp.logical_not(outer))
    def _():
        sums.give_far()

    last.do_x()
    last.do_y()
    begin_exchange(0)
    sums.give_near(False)
    begin_exchange(1)
    end_exchange(0)
    out_spread.diag()
    end_exchange(1)
    cols_spreads[0].cross()
    sums.wait()

    @pl.loop(0, rows // 32)
    def _(i):
        here = pl.ds(pl.multiple_of(i * 32, 32), 32)
        dnormed_ref[here] += sums.total(here)

    cols_spreads[1].cross()
    cols_spreads[0].diag()
    cols_spreads[1].diag()
    out_spread.end()
    for spread in cols_spreads:
        spread.end()
    out_tree.drain()
    for tree in cols_trees:
        tree.drain()
    line.end()
    sums.end()
    for i in (0, 1):
        for k in (1, 2, 3):
            for copy in exchange(i, k):
                copy.wait_send()


def back_in_one(resident, sums, loaded):
    w_out, w_cols = loaded[:2]
    rows, model = resident[0].shape
    cols = w_cols.shape[1]
    wide = cols + EXTRA
    count = model // 4 // 8
    vmem = pl.BlockSpec(memory_space=pltpu.VMEM)
    hbm = pl.BlockSpec(memory_space=pl.ANY)
    dma = pltpu.SemaphoreType.DMA
    return pl.pallas_call(
        back_kernel,
        out_shape=(
            jax.ShapeDtypeStruct((rows, model), F32),
            jax.ShapeDtypeStruct((rows, model), BF),
            jax.ShapeDtypeStruct((rows, model), F32),
            jax.ShapeDtypeStruct((8 * HEAD_WIDTH, model), BF),
            jax.ShapeDtypeStruct((8 * count, 4 * wide), BF),
        ),
        in_specs=[vmem] * len(resident) + [hbm] * (1 + len(loaded)),
        out_specs=(vmem, vmem, vmem, hbm, hbm),
        scratch_shapes=[
            *[pltpu.VMEM(v.shape, v.dtype) for v in loaded],
            pltpu.VMEM((4 * rows, model), BF),
            pltpu.VMEM((4 * rows, cols), BF),
            pltpu.VMEM((3 * rows, model), BF),
            pltpu.VMEM((3 * rows, EXTRA), BF),
            pltpu.VMEM((rows, EXTRA), F32),
            pltpu.VMEM((EXTRA, model), BF),
            pltpu.VMEM((4, rows, model), BF),
            pltpu.VMEM((5, rows, model), BF),
            pltpu.VMEM((8, model), F32),
            pltpu.VMEM((2, 8, HEAD_WIDTH), F32),
            pltpu.VMEM((HEAD_WIDTH, model), BF),
            *[pltpu.VMEM((2 * count, wide), BF)] * 2,
            *[pltpu.VMEM((count // 2, 4 * wide), BF)] * 2,
            *Tree.buffers(HEAD_WIDTH, model),
            *Tree.semaphores(),
            *Tree.buffers(2 * count, wide),
            *Tree.semaphores(),
            *Tree.buffers(2 * count, wide),
            *Tree.semaphores(),
            *Spread.semaphores(),
            *Spread.semaphores(),
            *Spread.semaphores(),
            *Line.semaphores(),
            *LineSum.semaphores(),
            dma((2, 3, 4)),
            dma((2, 3, 4)),
            dma((2, 4)),
            dma((6,)),
            dma((2,)),
        ],
        compiler_params=pltpu.CompilerParams(
            collective_id=1, has_side_effects=True, vmem_limit_bytes=VMEM_BYTES
        ),
        cost_estimate=pl.CostEstimate(
            flops=2 * 4 * rows * model * cols * 5,
            bytes_accessed=64 * 1024 * 1024,
            transcendentals=4 * rows * cols,
        ),
    )(*resident, sums, *loaded)


def front_kernel(
    tokens_ref,
    small_ref,
    router_ref,
    w_query_ref,
    w_key_ref,
    w_value_ref,
    w_out_ref,
    table_ref,
    chosen_ref,
    cot_ref,
    second_ref,
    middle_ref,
    share_ref,
    w_cols_out,
    normed_out,
    raw_out,
    prob_out,
    mixed_out,
    cos_ref,
    sin_ref,
    small_all_ref,
    router_all_ref,
    cot_all_ref,
    w_cols_ref,
    normed_ref,
    raw_ref,
    prob_ref,
    mixed_ref,
    own_part,
    router_wide,
    rows_out,
    rows_in,
    small_send,
    small_recv,
    piece_send,
    piece_recv,
    piece_local,
    cot_local,
    store_sem,
    *sems,
):
    at = Place()
    rows, model = tokens_ref.shape
    pair = 2 * rows
    width = HEAD_WIDTH
    q_cols = w_query_ref.shape[1] // 4
    heads = q_cols // width
    cols = q_cols + 2 * width
    quarter = model // 4
    count = quarter // 8
    half = rows // 2
    experts_all = router_ref.shape[0]
    scale = HEAD_WIDTH ** (-0.5)
    meet(at.everyone())

    cot_here = pltpu.make_async_copy(cot_ref, cot_all_ref.at[at.z, at.e // 2], cot_local)
    cot_here.start()

    small_all_ref[at.z] = small_ref[...]
    router_all_ref[at.z] = router_ref[...]

    def small_copies(k):
        there = at.plane(k)
        turn = at.turn_at(there)
        return [
            remote(
                ref,
                ref_all.at[at.z],
                small_send.at[k - 1, i],
                small_recv.at[turn - 1, i],
                (at.e, there),
            )
            for i, (ref, ref_all) in enumerate(
                ((small_ref, small_all_ref), (router_ref, router_all_ref))
            )
        ]

    for k in (1, 2, 3):
        for copy in small_copies(k):
            copy.start()

    def w_block(k, q, i=None):
        first, size = (0, count) if i is None else (i * (count // 2), count // 2)
        row = at.plane(k) * quarter + at.own(q) * count + first
        return w_cols_ref.at[pl.ds(pl.multiple_of(row, count // 2), size)]

    def piece_refs(there):
        own = pl.ds(pl.multiple_of(at.e * count, count), count)
        row = pl.ds(pl.multiple_of(at.z * quarter + at.e * count, count), count)
        narrow = pl.ds(pl.multiple_of(there * width, width), width)
        return (
            (
                w_query_ref.at[own, pl.ds(pl.multiple_of(there * q_cols, q_cols), q_cols)],
                w_cols_ref.at[row, pl.ds(0, q_cols)],
            ),
            (w_key_ref.at[own, narrow], w_cols_ref.at[row, pl.ds(q_cols, width)]),
            (w_value_ref.at[own, narrow], w_cols_ref.at[row, pl.ds(q_cols + width, width)]),
        )

    def piece_copies(k):
        there = at.plane(k)
        turn = at.turn_at(there)
        return [
            remote(
                src, dst, piece_send.at[k - 1, i], piece_recv.at[turn - 1, i], (at.e, there)
            )
            for i, (src, dst) in enumerate(piece_refs(there))
        ]

    def pieces_arrive(k):
        block = w_block(k, OWN)
        for i, (first, size) in enumerate(((0, q_cols), (q_cols, width), (q_cols, width))):
            part = block.at[:, pl.ds(first, size)]
            remote(
                part, part, piece_send.at[k - 1, i], piece_recv.at[k - 1, i], at.sibling
            ).wait_recv()

    own_pieces = [
        pltpu.make_async_copy(src, dst, piece_local.at[i])
        for i, (src, dst) in enumerate(piece_refs(at.z))
    ]
    for copy in own_pieces:
        copy.start()
    for k in (1, 2, 3):
        for copy in piece_copies(k):
            copy.start()
    weights = Gather(at, w_block, sems[2:10])
    for copy in own_pieces:
        copy.wait()
    weights.own(0)

    def normed_block(b):
        return normed_ref.at[pl.ds(pl.multiple_of(b * rows, rows), rows)]

    line = Line(at, normed_block, sems[10:12])
    source = tokens_ref[...].astype(F32)
    inverse = lax.rsqrt(jnp.mean(source * source, axis=-1, keepdims=True) + epsilon)
    for k in (1, 2, 3):
        for i, ref_all in enumerate((small_all_ref, router_all_ref)):
            block = ref_all.at[at.plane(k)]
            remote(
                block, block, small_send.at[k - 1, i], small_recv.at[k - 1, i], at.sibling
            ).wait_recv()
    own_rows = pl.ds(pl.multiple_of(at.z * rows, rows), rows)
    for j in range(4):
        lanes = slice(j * quarter, (j + 1) * quarter)
        normed_ref[own_rows, lanes] = (source[:, lanes] * inverse * small_all_ref[j, 0:1, :]).astype(BF)
        router_wide[0:experts_all, lanes] = router_all_ref[j]
        router_wide[experts_all : 2 * experts_all, lanes] = router_all_ref[j]
    router_wide[2 * experts_all :] = jnp.zeros((EXTRA - 2 * experts_all, model), BF)
    line.begin()

    def cot_block(k, q, i=None):
        block = cot_all_ref.at[at.plane(k), at.column_base(q) // 2]
        return block if i is None else block.at[pl.ds(i * half, half)]

    def cot_line_block(b):
        return cot_all_ref.at[b, at.e // 2]

    cot_line = Line(at, cot_line_block, sems[12:14])
    cot_gather = Gather(at, cot_block, sems[14:], sibling=False)
    outer = (at.z == 0) | (at.z == 3)
    cot_here.wait()

    @pl.when(outer)
    def _():
        cot_line.begin()


    pieces_arrive(1)
    weights.own(1)
    line.arrive(1)
    pieces_arrive(2)
    weights.own(2)
    pieces_arrive(3)
    weights.own(3)

    @pl.when(jnp.logical_not(outer))
    def _():
        line.arrive(2)

    weights.cross(0)
    weights.cross(1)

    @pl.when(jnp.logical_not(outer))
    def _():
        line.arrive(3)
        cot_line.begin()

    cot_gather.own(0)
    weights.diag(0)
    weights.cross(2)
    weights.diag(1)
    weights.cross(3)
    weights.diag(2)
    weights.diag(3)
    stores = [
        pltpu.make_async_copy(src, dst, store_sem.at[i])
        for i, (src, dst) in enumerate(
            (
                (normed_ref, normed_out),
                (w_cols_ref, w_cols_out),
                (raw_ref, raw_out),
                (prob_ref, prob_out),
                (mixed_ref, mixed_out),
            )
        )
    ]
    for k in range(4):
        for q in range(4):
            weights.ready(k, q)
    stores[1].start()
    sums = LineSum(at, rows_out, rows_in, sems[:2])

    def is_far(turn):
        return outer if turn == 0 else jnp.logical_not(outer)

    def project(turn):
        first = 2 * jnp.where(is_far(turn), 1 - at.half, at.half)
        both = pl.ds(pl.multiple_of(first * rows, pair), pair)
        step = 256
        for start in range(0, cols, step):
            lanes = slice(start, start + step)
            raw_ref[both, lanes] = jnp.dot(
                normed_ref[both, :], w_cols_ref[:, lanes], preferred_element_type=F32
            )

    gains = small_all_ref[0, 2:3, :] + small_all_ref[1, 2:3, :] + small_all_ref[2, 2:3, :] + small_all_ref[3, 2:3, :]
    q_gain, k_gain = gains[:, :width], gains[:, width : 2 * width]
    row_id = lax.broadcasted_iota(jnp.int32, (rows, rows), 0).astype(F32)
    lane_id = lax.broadcasted_iota(jnp.int32, (rows, rows), 1).astype(F32)

    def attention(turn):
        first = 2 * jnp.where(is_far(turn), 1 - at.half, at.half)
        both = pl.ds(pl.multiple_of(first * rows, pair), pair)
        for i in (0, 1):
            heads_of(first + i)
        step = 512
        for start in range(0, model, step):
            lanes = slice(start, start + step)
            part = jnp.dot(mixed_ref[both, :], w_out_ref[:, lanes], preferred_element_type=F32)

            @pl.when(jnp.logical_not(is_far(turn)))
            def _():
                own_part[:, lanes] = jnp.where(at.z % 2 == 0, part[:rows], part[rows:])

            rows_out[first, :, lanes] = part[:rows].astype(BF)
            rows_out[first + 1, :, lanes] = part[rows:].astype(BF)

        @pl.when(is_far(turn))
        def _():
            sums.give_far()

        if turn == 1:
            sums.give_near(True)
            sums.give_near(False)

    def heads_of(b):
        here = pl.ds(pl.multiple_of(b * rows, rows), rows)
        segment = jnp.zeros((rows, rows), F32)
        lane_segment = jnp.zeros((rows, rows), F32)
        place = row_id
        end = jnp.zeros((1, 1), F32)
        for i in range(SEQ_SLOTS - 1):
            length = small_all_ref[b, 2:3, 2 * width + i : 2 * width + i + 1]
            end = end + length
            past = (row_id >= end).astype(F32)
            segment += past
            place -= past * length
            lane_segment += (lane_id >= end).astype(F32)
        allowed = (segment == lane_segment) & (lane_id <= row_id)
        named = (lane_id == place).astype(BF)

        def looked_up(first):
            total = jnp.zeros((rows, width), F32)
            for i in range(3):
                part = table_ref[(first + i) * width : (first + i + 1) * width]
                total += jnp.dot(named, part, preferred_element_type=F32)
            return total

        cosine, sine = looked_up(0), looked_up(3)
        cos_ref[here, :] = cosine
        sin_ref[here, :] = sine

        def low_of(v, gain):
            inverse = lax.rsqrt(jnp.mean(v * v, axis=-1, keepdims=True) + epsilon)
            scaled = v * inverse * gain
            return (scaled * cosine + swap(scaled) * sine).astype(BF)

        k_low = low_of(raw_ref[here, q_cols : q_cols + width], k_gain)
        v_low = raw_ref[here, q_cols + width : q_cols + 2 * width].astype(BF)
        for h in range(heads):
            lanes = slice(h * width, (h + 1) * width)
            q_low = low_of(raw_ref[here, lanes], q_gain)
            scores = jnp.where(allowed, dot(q_low, k_low, NT) * scale, masked_score)
            weight = jnp.exp(scores - jnp.max(scores, axis=-1, keepdims=True))
            prob = weight / jnp.sum(weight, axis=-1, keepdims=True)
            prob_ref[b * heads + h] = prob
            mixed_ref[here, lanes] = dot(prob.astype(BF), v_low, NN).astype(BF)

    @pl.when(outer)
    def _():
        line.arrive(2)
        line.arrive(3)

    project(0)
    cot_line.arrive(1)
    cot_gather.own(1)
    attention(0)

    @pl.when(jnp.logical_not(outer))
    def _():
        cot_line.arrive(2)
        cot_gather.own(2)

    cot_gather.cross(0)
    stores[0].start()
    project(1)
    stores[2].start()

    @pl.when(jnp.logical_not(outer))
    def _():
        cot_line.arrive(3)
        cot_gather.own(3)

    cot_gather.cross(1)
    attention(1)
    stores[3].start()
    stores[4].start()

    @pl.when(outer)
    def _():
        cot_line.arrive(2)
        cot_gather.own(2)
        cot_line.arrive(3)
        cot_gather.own(3)

    cot_gather.diag(0)
    cot_gather.diag(1)
    cot_gather.cross(2)
    cot_gather.cross(3)
    sums.wait()
    middle = (
        tokens_ref[...].astype(F32)
        + own_part[...]
        + sums.total(pl.ds(0, rows))
    )
    middle_ref[...] = middle
    inverse = lax.rsqrt(jnp.mean(middle * middle, axis=-1, keepdims=True) + epsilon)
    for j in range(4):
        lanes = slice(j * quarter, (j + 1) * quarter)
        second_ref[:, lanes] = (middle[:, lanes] * inverse * small_all_ref[j, 1:2, :]).astype(BF)
    logits = dot(second_ref[:, :model], router_wide[...], NT)
    chosen = chosen_ref[...] > 0.0
    lane = lax.broadcasted_iota(jnp.int32, (rows, EXTRA), 1)
    top = jnp.max(jnp.where(chosen, logits, masked_score), axis=-1, keepdims=True)
    lifted = jnp.where(chosen, jnp.exp(logits - top), 0.0)
    share = lifted / jnp.sum(jnp.where(lane < experts_all, lifted, 0.0), axis=-1, keepdims=True)
    share_ref[...] = share
    high = share.astype(BF).astype(F32)
    second_ref[:, model:] = jnp.where(lane < experts_all, high, share - high).astype(BF)
    cot_gather.diag(2)
    cot_gather.diag(3)
    for copy in stores:
        copy.wait()
    for k in range(4):
        cot_gather.end(k)
        weights.end(k)
    line.end()
    cot_line.end()
    sums.end()
    for k in (1, 2, 3):
        for copy in small_copies(k):
            copy.wait_send()
        for copy in piece_copies(k):
            copy.wait_send()


def front_in_one(tokens, small, router, w_query, w_key, w_value, w_out, table, chosen, cotangent):
    rows, model = tokens.shape
    q_cols = w_query.shape[1] // 4
    cols = q_cols + 2 * HEAD_WIDTH
    heads = q_cols // HEAD_WIDTH
    experts_all = router.shape[0]
    vmem = pl.BlockSpec(memory_space=pltpu.VMEM)
    hbm = pl.BlockSpec(memory_space=pl.ANY)
    dma = pltpu.SemaphoreType.DMA
    shape = jax.ShapeDtypeStruct
    return pl.pallas_call(
        front_kernel,
        out_shape=(
            shape((rows, model + EXTRA), BF),
            shape((rows, model), F32),
            shape((rows, EXTRA), F32),
            shape((model, cols), BF),
            shape((4 * rows, model), BF),
            shape((4 * rows, cols), F32),
            shape((4 * heads, rows, rows), F32),
            shape((4 * rows, q_cols), BF),
            shape((4 * rows, HEAD_WIDTH), F32),
            shape((4 * rows, HEAD_WIDTH), F32),
            shape((4, 8, model // 4), F32),
            shape((4, experts_all, model // 4), BF),
            shape((4, 4, rows, model), BF),
        ),
        in_specs=[vmem, vmem, vmem, hbm, hbm, hbm, vmem, vmem, vmem, hbm],
        out_specs=(vmem,) * 3 + (hbm,) * 5 + (vmem,) * 4 + (hbm,),
        scratch_shapes=[
            pltpu.VMEM((model, cols), BF),
            pltpu.VMEM((4 * rows, model), BF),
            pltpu.VMEM((4 * rows, cols), F32),
            pltpu.VMEM((4 * heads, rows, rows), F32),
            pltpu.VMEM((4 * rows, q_cols), BF),
            pltpu.VMEM((rows, model), F32),
            pltpu.VMEM((EXTRA, model), BF),
            pltpu.VMEM((4, rows, model), BF),
            pltpu.VMEM((5, rows, model), BF),
            dma((3, 2)),
            dma((3, 2)),
            dma((3, 3)),
            dma((3, 3)),
            dma((3,)),
            dma,
            dma((5,)),
            *LineSum.semaphores(),
            *Gather.semaphores(),
            *Line.semaphores(),
            *Line.semaphores(),
            *Gather.semaphores(False),
        ],
        compiler_params=pltpu.CompilerParams(
            collective_id=2, has_side_effects=True, vmem_limit_bytes=VMEM_BYTES
        ),
        cost_estimate=pl.CostEstimate(
            flops=2 * 4 * rows * model * (cols + q_cols),
            bytes_accessed=64 * 1024 * 1024,
            transcendentals=4 * rows * cols,
        ),
    )(tokens, small, router, w_query, w_key, w_value, w_out, table, chosen, cotangent)


def per_device(
    tokens,
    lengths,
    routes,
    attn_gain,
    w_query,
    key_projection,
    value_projection,
    w_out,
    query_gain,
    key_gain,
    ffn_gain,
    w_router,
    w_gate,
    w_up,
    w_down,
    cotangent,
):
    ring = lax.axis_size("fsdp")
    groups = lax.axis_size("expert")
    plane_rank = lax.axis_index("expert")
    experts_all = w_router.shape[1]
    local_experts = w_gate.shape[0]
    units = w_gate.shape[2]
    wide = local_experts * units
    in_rows = MODEL_WIDTH // ring
    heads = QUERY_HEADS // ring
    kv = KEY_VALUE_HEADS // ring
    group_width = heads // kv
    q_cols = heads * HEAD_WIDTH
    kv_cols = kv * HEAD_WIDTH
    cols = q_cols + 2 * kv_cols
    piece_rows = in_rows // groups
    score_scale = HEAD_WIDTH ** (-0.5)
    both = ("expert", "fsdp")
    one_block = (groups, ring, experts_all) == (8, 4, 16)

    gate_w = w_gate.transpose(0, 2, 1).reshape(wide, MODEL_WIDTH)
    up_w = w_up.transpose(0, 2, 1).reshape(wide, MODEL_WIDTH)
    down_w = w_down.reshape(wide, MODEL_WIDTH)
    line_tokens = ring * DEVICE_TOKENS
    source = tokens.astype(F32)
    expert_ids = jnp.arange(experts_all, dtype=jnp.int32)
    chosen = jnp.any(routes[:, :, None] == expert_ids[None, None, :], axis=1)

    if one_block:
        here = lax.axis_index("fsdp") * (HEAD_WIDTH // ring)
        spread = lambda gain: lax.dynamic_update_slice_in_dim(
            jnp.zeros((HEAD_WIDTH,), F32), gain.astype(F32), here, 0
        )
        third = jnp.concatenate(
            [spread(query_gain), spread(key_gain), lengths.reshape(-1).astype(F32)]
        )
        small = jnp.stack(
            [
                attn_gain.astype(F32),
                ffn_gain.astype(F32),
                jnp.pad(third, (0, in_rows - third.shape[0])),
            ]
        )
        frequency = rope_base ** (-np.arange(0, HEAD_WIDTH, 2) / HEAD_WIDTH)
        angles = np.arange(HEAD_WIDTH)[:, None] * np.tile(frequency, 2)[None, :]
        sine_sign = np.where(np.arange(HEAD_WIDTH) < HEAD_WIDTH // 2, -1.0, 1.0)
        parts = []
        for exact in (np.cos(angles), np.sin(angles) * sine_sign):
            for _ in range(3):
                parts.append(exact.astype(ml_dtypes.bfloat16))
                exact = exact - parts[-1].astype(np.float64)
        wide_chosen = jnp.pad(
            jnp.concatenate([chosen, chosen], axis=1).astype(F32),
            ((0, 0), (0, EXTRA - 2 * experts_all)),
        )
        (
            second_wide,
            middle,
            share,
            w_cols,
            normed_all,
            raw,
            probabilities,
            mixed,
            cosine,
            sine_table,
            small_all,
            router_all,
            cot_all,
        ) = front_in_one(
            tokens,
            jnp.pad(small, ((0, 5), (0, 0))),
            w_router.T,
            w_query,
            key_projection,
            value_projection,
            w_out,
            jnp.asarray(np.concatenate(parts)),
            wide_chosen,
            cotangent,
        )
        cot_all = cot_all.reshape(-1, MODEL_WIDTH)
        attn_gain_f = small_all[:, 0].reshape(-1)
        attn_inverse = lax.rsqrt(jnp.mean(source * source, axis=-1, keepdims=True) + epsilon)
        attn_unit = source * attn_inverse
    else:
        small = jnp.concatenate(
            [
                attn_gain,
                ffn_gain,
                query_gain,
                key_gain,
                w_router.reshape(-1),
                lengths.reshape(-1).astype(BF),
            ]
        )
        small_all = lax.all_gather(small, "fsdp", axis=0, tiled=False)
        at = 0

        def take(count):
            nonlocal at
            part = small_all[:, at : at + count]
            at += count
            return part

        attn_gain_f = take(in_rows).reshape(-1).astype(F32)
        ffn_gain_f = take(in_rows).reshape(-1).astype(F32)
        query_gain_f = take(HEAD_WIDTH // ring).reshape(-1).astype(F32)
        key_gain_f = take(HEAD_WIDTH // ring).reshape(-1).astype(F32)
        router_all = take(in_rows * experts_all).reshape(MODEL_WIDTH, experts_all)
        lengths_all = take(SEQ_SLOTS).astype(jnp.int32)

        by_col = jnp.concatenate(
            [
                w_query.reshape(in_rows, ring, q_cols),
                key_projection.reshape(in_rows, ring, kv_cols),
                value_projection.reshape(in_rows, ring, kv_cols),
            ],
            axis=2,
        )
        piece = lax.dynamic_slice_in_dim(by_col, plane_rank * piece_rows, piece_rows, 0)
        piece = lax.all_to_all(
            piece.transpose(1, 0, 2), "fsdp", split_axis=0, concat_axis=0, tiled=True
        )
        w_cols = lax.all_gather(piece, "expert", axis=1, tiled=True).reshape(MODEL_WIDTH, cols)

        attn_inverse = lax.rsqrt(jnp.mean(source * source, axis=-1, keepdims=True) + epsilon)
        attn_unit = source * attn_inverse
        normed = (attn_unit * attn_gain_f).astype(BF)
        normed_all = lax.all_gather(normed, "fsdp", axis=0, tiled=True)
        raw = dot(normed_all, w_cols, NN)
        query_raw = raw[:, :q_cols].reshape(ring, DEVICE_TOKENS, kv, group_width, HEAD_WIDTH)
        key_raw = raw[:, q_cols : q_cols + kv_cols].reshape(ring, DEVICE_TOKENS, kv, HEAD_WIDTH)
        value_low = raw[:, q_cols + kv_cols :].astype(BF).reshape(ring, DEVICE_TOKENS, kv, HEAD_WIDTH)
        places, segment_ids = jax.vmap(lambda row: layout(row, DEVICE_TOKENS, SEQ_SLOTS))(lengths_all)
        cosine, sine_table = rope_tables(places, HEAD_WIDTH)
        cos_k, sin_k = cosine[:, :, None, :], sine_table[:, :, None, :]
        cos_q, sin_q = cosine[:, :, None, None, :], sine_table[:, :, None, None, :]
        query_inverse = lax.rsqrt(jnp.mean(query_raw * query_raw, axis=-1, keepdims=True) + epsilon)
        query_unit = query_raw * query_inverse
        query_low = rotate(query_unit * query_gain_f, cos_q, sin_q).astype(BF)
        key_inverse = lax.rsqrt(jnp.mean(key_raw * key_raw, axis=-1, keepdims=True) + epsilon)
        key_unit = key_raw * key_inverse
        key_low = rotate(key_unit * key_gain_f, cos_k, sin_k).astype(BF)
        row_ids = jnp.arange(DEVICE_TOKENS, dtype=jnp.int32)
        allowed = (segment_ids[:, :, None] == segment_ids[:, None, :]) & (
            row_ids[None, None, :] <= row_ids[None, :, None]
        )
        scores = (
            jnp.einsum("bqhgd,bkhd->bhgqk", query_low, key_low, preferred_element_type=F32)
            * score_scale
        )
        scores = jnp.where(allowed[:, None, None], scores, masked_score)
        weights = jnp.exp(scores - jnp.max(scores, axis=-1, keepdims=True))
        probabilities = weights / jnp.sum(weights, axis=-1, keepdims=True)
        prob_low = probabilities.astype(BF)
        mixed = (
            jnp.einsum("bhgqk,bkhd->bqhgd", prob_low, value_low, preferred_element_type=F32)
            .astype(BF)
            .reshape(line_tokens, q_cols)
        )
        branch = lax.psum_scatter(
            dot(mixed, w_out, NN).astype(BF), "fsdp", scatter_dimension=0, tiled=True
        ).astype(F32)
        middle = source + branch
        ffn_inverse = lax.rsqrt(jnp.mean(middle * middle, axis=-1, keepdims=True) + epsilon)
        ffn_unit = middle * ffn_inverse
        second = (ffn_unit * ffn_gain_f).astype(BF)

        logits = dot(second, router_all, NN)
        top = jnp.max(jnp.where(chosen, logits, -jnp.inf), axis=1, keepdims=True)
        lifted = jnp.where(chosen, jnp.exp(logits - top), 0.0)
        share = lifted / jnp.sum(lifted, axis=1, keepdims=True)

    def experts(second, share, cotangent):
        second_all = lax.all_gather(second, both, axis=0, tiled=True)
        share_all = lax.all_gather(share, both, axis=0, tiled=True)
        cot_all = lax.all_gather(cotangent, both, axis=0, tiled=True)
        first = plane_rank * local_experts
        own_share = lax.dynamic_slice_in_dim(share_all, first, local_experts, 1)
        share_wide = jnp.repeat(own_share, units, axis=1)
        gate_act = dot(second_all, gate_w, NT)
        up_act = dot(second_all, up_w, NT)
        back = dot(cot_all, down_w, NT)
        sigmoid_gate = jax.nn.sigmoid(gate_act)
        silu_gate = gate_act * sigmoid_gate
        hidden = silu_gate * up_act
        share_grad = jnp.sum((hidden * back).reshape(-1, local_experts, units), axis=2)
        hidden_low = (share_wide * hidden).astype(BF)
        hidden_grad = share_wide * back
        gate_grad = (
            hidden_grad * up_act * sigmoid_gate * (1.0 + gate_act * (1.0 - sigmoid_gate))
        ).astype(BF)
        up_grad = (hidden_grad * silu_gate).astype(BF)
        routed_part = dot(hidden_low, down_w, NN).astype(BF)
        second_part = (dot(gate_grad, gate_w, NN) + dot(up_grad, up_w, NN)).astype(BF)
        spread = jnp.zeros((share_grad.shape[0], experts_all), F32)
        spread = lax.dynamic_update_slice_in_dim(spread, share_grad, first, 1)
        second_grad = lax.psum_scatter(second_part, both, scatter_dimension=0, tiled=True)
        routed = lax.psum_scatter(routed_part, both, scatter_dimension=0, tiled=True)
        dshare = lax.psum_scatter(spread, both, scatter_dimension=0, tiled=True)
        return (
            (second_grad.astype(F32), routed.astype(F32), dshare),
            (
                dot(gate_grad, second_all, TN),
                dot(up_grad, second_all, TN),
                dot(hidden_low, cot_all, TN),
            ),
        )

    chunks = max(1, ring * groups // 32)
    if one_block:
        sums, *weight_grads, _ = experts_in_one(second_wide, cot_all, gate_w, up_w, down_w)
    elif chunks == 1:
        rows_out, weight_grads = experts(second, share, cotangent)
    else:
        def turn(total, rows):
            rows_out, grads = experts(*rows)
            return jax.tree.map(jnp.add, total, grads), rows_out

        start = (
            jnp.zeros((wide, MODEL_WIDTH), F32),
            jnp.zeros((wide, MODEL_WIDTH), F32),
            jnp.zeros((wide, MODEL_WIDTH), F32),
        )
        weight_grads, rows_out = lax.scan(
            turn,
            start,
            [v.reshape(chunks, -1, v.shape[1]) for v in (second, share, cotangent)],
        )
        rows_out = [v.reshape(-1, v.shape[2]) for v in rows_out]
    gate_wgrad, up_wgrad, down_wgrad = weight_grads
    grad_w_gate = gate_wgrad.reshape(local_experts, units, MODEL_WIDTH).transpose(0, 2, 1)
    grad_w_up = up_wgrad.reshape(local_experts, units, MODEL_WIDTH).transpose(0, 2, 1)
    grad_w_down = down_wgrad.reshape(local_experts, units, MODEL_WIDTH)
    if one_block:
        at_gain = experts_all
        part_width = HEAD_WIDTH // ring
        head_lane = np.arange(HEAD_WIDTH)
        place_of = head_lane // part_width * in_rows + head_lane % part_width
        placing = jnp.asarray(place_of[:, None] == np.arange(MODEL_WIDTH)[None, :], BF)
        normed_grad, block_out, middle_grad, out_sum, cols_sum = back_in_one(
            (
                middle,
                share,
                cotangent,
                router_all,
                small_all,
                cosine,
                sine_table,
                second_wide,
                placing,
            ),
            sums,
            (w_out, w_cols, mixed, normed_all, raw, probabilities),
        )
        tokens_grad = middle_grad + norm_back(normed_grad * attn_gain_f, attn_unit, attn_inverse)
        out_grad = out_sum.astype(F32)
        ends = [ring * n for n in (q_cols, q_cols + kv_cols, cols)]
        grad_w_query = cols_sum[:, : ends[0]].astype(F32)
        grad_w_key = cols_sum[:, ends[0] : ends[1]].astype(F32)
        grad_w_value = cols_sum[:, ends[1] : ends[2]].astype(F32)
        small_own = sum(
            cols_sum[:, ends[2] + j * EXTRA : ends[2] + (j + 1) * EXTRA].astype(F32)
            for j in range(ring)
        )
        own_grads = (
            small_own[:, at_gain + 1],
            small_own[:part_width, at_gain + 2],
            small_own[:part_width, at_gain + 3],
            small_own[:, at_gain],
            small_own[:, :experts_all],
        )
    else:
        second_grad, routed, dshare = rows_out
        block_out = (middle + routed).astype(BF)

        mean_grad = jnp.sum(share * dshare, axis=1, keepdims=True)
        logit_grad = (share * (dshare - mean_grad)).astype(BF)
        upstream = cotangent.astype(F32)
        second_grad = second_grad + dot(logit_grad, router_all, NT)
        middle_grad = upstream + norm_back(second_grad * ffn_gain_f, ffn_unit, ffn_inverse)
        router_grad = dot(second, logit_grad, TN)
        ffn_gain_grad = jnp.sum(second_grad * ffn_unit, axis=0)
        branch_all = lax.all_gather(middle_grad.astype(BF), "fsdp", axis=0, tiled=True)
        out_grad = lax.psum(dot(mixed, branch_all, TN).astype(BF), "expert").astype(F32)
        mixed_grad = dot(branch_all, w_out, NT).astype(BF)
        mixed_grad = mixed_grad.reshape(ring, DEVICE_TOKENS, kv, group_width, HEAD_WIDTH)
        value_grad = jnp.einsum("bhgqk,bqhgd->bkhd", prob_low, mixed_grad, preferred_element_type=F32)
        prob_grad = jnp.einsum("bqhgd,bkhd->bhgqk", mixed_grad, value_low, preferred_element_type=F32)
        score_grad = (
            probabilities * (prob_grad - jnp.sum(probabilities * prob_grad, axis=-1, keepdims=True))
        ).astype(BF)
        query_grad = (
            jnp.einsum("bhgqk,bkhd->bqhgd", score_grad, key_low, preferred_element_type=F32)
            * score_scale
        )
        key_grad = (
            jnp.einsum("bhgqk,bqhgd->bkhd", score_grad, query_low, preferred_element_type=F32)
            * score_scale
        )
        query_turned = unrotate(query_grad, cos_q, sin_q)
        query_gain_grad = jnp.sum(query_turned * query_unit, axis=(0, 1, 2, 3))
        query_back = norm_back(query_turned * query_gain_f, query_unit, query_inverse)
        key_turned = unrotate(key_grad, cos_k, sin_k)
        key_gain_grad = jnp.sum(key_turned * key_unit, axis=(0, 1, 2))
        key_back = norm_back(key_turned * key_gain_f, key_unit, key_inverse)
        raw_grad = jnp.concatenate(
            [
                query_back.astype(BF).reshape(line_tokens, q_cols),
                key_back.astype(BF).reshape(line_tokens, kv_cols),
                value_grad.astype(BF).reshape(line_tokens, kv_cols),
            ],
            axis=1,
        )
        cols_grad = dot(normed_all, raw_grad, TN).astype(BF)
        normed_part = dot(raw_grad, w_cols, NT).astype(BF)
        normed_grad = lax.psum_scatter(normed_part, "fsdp", scatter_dimension=0, tiled=True).astype(F32)
        attn_gain_grad = jnp.sum(normed_grad * attn_unit, axis=0)
        tokens_grad = middle_grad + norm_back(normed_grad * attn_gain_f, attn_unit, attn_inverse)

        own = lax.psum_scatter(
            cols_grad.reshape(ring, groups, piece_rows, cols), "expert", scatter_dimension=1, tiled=False
        )
        own = lax.all_to_all(own, "fsdp", split_axis=0, concat_axis=0, tiled=True)
        rows_grad = lax.all_gather(own, "expert", axis=1, tiled=True)
        rows_grad = rows_grad.transpose(1, 0, 2).astype(F32)
        grad_w_query = rows_grad[:, :, :q_cols].reshape(in_rows, QUERY_HEADS * HEAD_WIDTH)
        grad_w_key = rows_grad[:, :, q_cols : q_cols + kv_cols].reshape(in_rows, -1)
        grad_w_value = rows_grad[:, :, q_cols + kv_cols :].reshape(in_rows, -1)

        small_grad = jnp.concatenate(
            [
                attn_gain_grad.reshape(ring, -1),
                ffn_gain_grad.reshape(ring, -1),
                query_gain_grad.reshape(ring, -1),
                key_gain_grad.reshape(ring, -1),
                router_grad.reshape(ring, -1),
            ],
            axis=1,
        )
        small_own = lax.psum(small_grad, both)
        small_own = lax.dynamic_index_in_dim(small_own, lax.axis_index("fsdp"), 0, keepdims=False)
        a, b = in_rows, HEAD_WIDTH // ring
        own_grads = (
            small_own[:a],
            small_own[2 * a : 2 * a + b],
            small_own[2 * a + b : 2 * a + 2 * b],
            small_own[a : 2 * a],
            small_own[2 * a + 2 * b :].reshape(in_rows, experts_all),
        )
    return (
        block_out,
        tokens_grad,
        own_grads[0],
        grad_w_query,
        grad_w_key,
        grad_w_value,
        out_grad,
        own_grads[1],
        own_grads[2],
        own_grads[3],
        own_grads[4],
        grad_w_gate,
        grad_w_up,
        grad_w_down,
    )


def solution(mesh):
    rows = P(("expert", "fsdp"), None)
    return jax.shard_map(
        per_device,
        mesh=mesh,
        in_specs=(
            rows,
            rows,
            rows,
            P("fsdp"),
            P("fsdp", None),
            P("fsdp", None),
            P("fsdp", None),
            P("fsdp", None),
            P("fsdp"),
            P("fsdp"),
            P("fsdp"),
            P("fsdp", None),
            P("expert", None, "fsdp"),
            P("expert", None, "fsdp"),
            P("expert", "fsdp", None),
            rows,
        ),
        out_specs=(
            rows,
            rows,
            P("fsdp"),
            P("fsdp", None),
            P("fsdp", None),
            P("fsdp", None),
            P("fsdp", None),
            P("fsdp"),
            P("fsdp"),
            P("fsdp"),
            P("fsdp", None),
            P("expert", None, "fsdp"),
            P("expert", None, "fsdp"),
            P("expert", "fsdp", None),
        ),
        check_vma=False,
    )
```

```python
import jax
import jax.numpy as jnp
import ml_dtypes
import numpy as np
from jax import lax
from jax.experimental import pallas as pl
from jax.experimental.pallas import tpu as pltpu
from jax.sharding import PartitionSpec as P

MODEL_WIDTH = 2048
QUERY_HEADS = 32
KEY_VALUE_HEADS = 4
HEAD_WIDTH = 128
TOPK = 8
DEVICE_TOKENS = 128
SEQ_SLOTS = 4

epsilon = 1e-06
rope_base = 1000000.0
masked_score = -1e30
BF = jnp.bfloat16
F32 = jnp.float32


def layout(lengths_row, tok_count, slot_count):
    seq_ends = jnp.cumsum(lengths_row)
    starts = seq_ends - lengths_row
    places = jnp.arange(tok_count, dtype=jnp.int32)
    segment = jnp.sum((places[:, None] >= seq_ends[None, :]).astype(jnp.int32), axis=1)
    member = segment[:, None] == jnp.arange(slot_count, dtype=jnp.int32)[None, :]
    start_of = jnp.sum(jnp.where(member, starts[None, :], 0), axis=1)
    return (places - start_of, segment)


def rope_tables(places, head_size):
    frequency = rope_base ** (-jnp.arange(0, head_size, 2, dtype=jnp.float32) / head_size)
    angles = places.astype(jnp.float32)[..., None] * frequency
    angles = jnp.concatenate([angles, angles], axis=-1)
    return (jnp.cos(angles), jnp.sin(angles))


def rotate(values, cosine, sine_table):
    half_width = values.shape[-1] // 2
    turned = jnp.concatenate([-values[..., half_width:], values[..., :half_width]], axis=-1)
    return values * cosine + turned * sine_table


def unrotate(gradient, cosine, sine_table):
    scaled = gradient * sine_table
    half_width = gradient.shape[-1] // 2
    return gradient * cosine + jnp.concatenate(
        [scaled[..., half_width:], -scaled[..., :half_width]], axis=-1
    )


def norm_back(gradient, unit_value, inverse):
    return inverse * (
        gradient - unit_value * jnp.mean(gradient * unit_value, axis=-1, keepdims=True)
    )


def dot(a, b, dims):
    return lax.dot_general(a, b, (dims, ((), ())), preferred_element_type=F32)


NN = ((1,), (0,))
NT = ((1,), (1,))
TN = ((0,), (0,))
VMEM_BYTES = 63 * 1024 * 1024

MESH = pl.DeviceIdType.MESH
EXTRA = 128
DIAG, XCOL, YCOL, OWN = 0, 1, 2, 3


def remote(src, dst, send, recv, device):
    return pltpu.make_async_remote_copy(
        src_ref=src,
        dst_ref=dst,
        send_sem=send,
        recv_sem=recv,
        device_id=device,
        device_id_type=MESH,
    )


class Place:
    def __init__(self):
        e = lax.axis_index("expert")
        z = lax.axis_index("fsdp")
        self.e, self.z = e, z
        self.core = lax.rem(e, 2)
        self.x = lax.rem(lax.div(e, 2), 2)
        self.y = lax.div(e, 4)
        self.x_near = (e + 2 - 4 * self.x, z)
        self.y_near = (e + 4 - 8 * self.y, z)
        self.sibling = (e + 1 - 2 * self.core, z)
        self.diagonal = (1 - self.y) * 4 + (1 - self.x) * 2 + self.core
        self.partner = z + 1 - 2 * lax.rem(z, 2)
        self.half = lax.div(z, 2)

    def plane(self, k):
        far = jnp.where(self.half == 0, k, 3 - k)
        return jnp.where(k == 0, self.z, jnp.where(k == 1, self.partner, far))

    def turn_at(self, z_there):
        far = jnp.where(z_there < 2, self.z, 3 - self.z)
        return jnp.where(z_there == self.partner, 1, far)

    def column_base(self, q):
        x = self.x if q in (YCOL, OWN) else 1 - self.x
        y = self.y if q in (XCOL, OWN) else 1 - self.y
        return (y * 2 + x) * 2

    def own(self, q):
        return self.column_base(q) + self.core

    def everyone(self):
        return [self.x_near, self.y_near, self.sibling] + [(self.e, self.plane(k)) for k in (1, 2, 3)]


def when(condition):
    def run(body):
        if isinstance(condition, bool):
            if condition:
                body()
        else:
            pl.when(condition)(body)

    return run


def greet(devices):
    barrier = pltpu.get_barrier_semaphore()
    for device in devices:
        pl.semaphore_signal(barrier, inc=1, device_id=device, device_id_type=MESH)


def meet(devices, greeted=False):
    if not greeted:
        greet(devices)
    pl.semaphore_wait(pltpu.get_barrier_semaphore(), len(devices))


class Line:
    def __init__(self, at, block, sems):
        self.at, self.block = at, block
        self.send, self.recv = sems

    def up(self, b):
        block = self.block(b)
        return remote(
            block, block, self.send.at[0, b], self.recv.at[b], (self.at.e, self.at.z + 1)
        )

    def down(self, b):
        block = self.block(b)
        return remote(
            block, block, self.send.at[1, b], self.recv.at[b], (self.at.e, self.at.z - 1)
        )

    def begin(self):
        z = self.at.z

        @pl.when(z < 3)
        def _():
            self.up(z).start()

        @pl.when(z > 0)
        def _():
            self.down(z).start()

    def arrive(self, k):
        z = self.at.z
        b = self.at.plane(k)
        block = self.block(b)
        remote(block, block, self.send.at[0, b], self.recv.at[b], self.at.sibling).wait_recv()

        @pl.when((b < z) & (z < 3))
        def _():
            self.up(b).start()

        @pl.when((b > z) & (z > 0))
        def _():
            self.down(b).start()

    def end(self):
        z = self.at.z
        for b in range(4):

            @pl.when((b <= z) & (z < 3))
            def _():
                self.up(b).wait_send()

            @pl.when((b >= z) & (z > 0))
            def _():
                self.down(b).wait_send()

    @staticmethod
    def semaphores():
        return [pltpu.SemaphoreType.DMA((2, 4)), pltpu.SemaphoreType.DMA((4,))]


class LineSum:
    def __init__(self, at, part, came, sems):
        self.at, self.part, self.came = at, part, came
        self.send, self.recv = sems

    def arrival(self, slot):
        block = self.came.at[slot]
        return remote(block, block, self.send.at[0], self.recv.at[slot], self.at.sibling)

    def copy(self, t):
        z = self.at.z
        up = (t > z).astype(jnp.int32)
        there = z + 2 * up - 1
        slot = jnp.where((t == there) & (up == 0), 4, t)
        return remote(
            self.part.at[t], self.came.at[slot], self.send.at[t], self.recv.at[slot], (self.at.e, there)
        )

    def give(self, t):
        z = self.at.z

        @pl.when(((t > z) & (z > 0)) | ((t < z) & (z < 3)))
        def _():
            self.arrival(t).wait_recv()

            @pl.loop(0, self.part.shape[1] // 32)
            def _(i):
                here = pl.ds(pl.multiple_of(i * 32, 32), 32)
                self.part[t, here] = (
                    self.part[t, here].astype(F32) + self.came[t, here].astype(F32)
                ).astype(BF)

        self.copy(t).start()

    def give_far(self):
        half = self.at.half
        self.give(jnp.where(half == 0, 3, 0))
        self.give(jnp.where(half == 0, 2, 1))

    def give_near(self, early):
        z = self.at.z
        outer = (z == 0) | (z == 3)

        @pl.when(outer if early else jnp.logical_not(outer))
        def _():
            self.give(self.at.partner)

    def wait(self):
        z = self.at.z
        zero = jnp.zeros(self.came.shape[1:], BF)

        @pl.when(z > 0)
        def _():
            self.arrival(z).wait_recv()

        @pl.when(z == 0)
        def _():
            self.came[0] = zero

        @pl.when(z < 3)
        def _():
            self.arrival(4).wait_recv()

        @pl.when(z == 3)
        def _():
            self.came[4] = zero

    def total(self, here):
        return self.came[self.at.z, here].astype(F32) + self.came[4, here].astype(F32)

    def end(self):
        for t in range(4):

            @pl.when(t != self.at.z)
            def _():
                self.copy(t).wait_send()

    @staticmethod
    def semaphores():
        return [pltpu.SemaphoreType.DMA((4,)), pltpu.SemaphoreType.DMA((5,))]


class Gather:
    def __init__(self, at, block, sems, sibling=True):
        self.at, self.block, self.sibling = at, block, sibling
        (self.x_send, self.x_recv, self.y_send, self.y_recv) = sems[:4]
        self.half_send, self.half_recv = sems[4:6]
        if sibling:
            self.sib_send, self.sib_recv = sems[6:8]

    def to_x(self, k):
        block = self.block(k, OWN)
        return remote(block, block, self.x_send.at[k], self.x_recv.at[k], self.at.x_near)

    def to_y(self, k):
        block = self.block(k, OWN)
        return remote(block, block, self.y_send.at[k], self.y_recv.at[k], self.at.y_near)

    def on_y(self, k):
        block = self.block(k, XCOL, 0)
        sem = 2 * k
        return remote(block, block, self.half_send.at[sem], self.half_recv.at[sem], self.at.y_near)

    def on_x(self, k):
        block = self.block(k, YCOL, 1)
        sem = 2 * k + 1
        return remote(block, block, self.half_send.at[sem], self.half_recv.at[sem], self.at.x_near)

    def to_sib(self, k, q):
        block = self.block(k, q)
        sem = 4 * k + q
        return remote(block, block, self.sib_send.at[sem], self.sib_recv.at[sem], self.at.sibling)

    def share(self, k, q):
        if self.sibling:
            self.to_sib(k, q).start()

    def own(self, k):
        self.to_x(k).start()
        self.to_y(k).start()
        self.share(k, OWN)

    def cross(self, k, halves=True):
        self.to_x(k).wait_recv()
        if halves:
            self.on_y(k).start()
        self.share(k, XCOL)
        self.to_y(k).wait_recv()
        if halves:
            self.on_x(k).start()
        self.share(k, YCOL)

    def diag(self, k):
        self.on_y(k).wait_recv()
        self.on_x(k).wait_recv()
        self.share(k, DIAG)

    def ready(self, k, q):
        self.to_sib(k, q).wait_recv()

    def end(self, k, halves=True):
        self.to_x(k).wait_send()
        self.to_y(k).wait_send()
        if halves:
            self.on_x(k).wait_send()
            self.on_y(k).wait_send()
        for q in range(4) if self.sibling else ():
            self.to_sib(k, q).wait_send()

    @staticmethod
    def semaphores(sibling=True):
        dma = pltpu.SemaphoreType.DMA
        return [dma((4,))] * 4 + [dma((8,))] * 2 + [dma((16,))] * 2 * sibling


def expert_kernel(
    second_ref,
    cot_ref,
    gate_ref,
    up_ref,
    down_ref,
    sums_ref,
    gate_grad_ref,
    up_grad_ref,
    down_grad_ref,
    kept_ref,
    held,
    part,
    diag_a,
    diag_b,
    diag_z,
    x_whole,
    y_whole,
    z_part,
    pair_part,
    cot_tile,
    gate_up,
    down,
    acts,
    back,
    gate_tile,
    hidden_tile,
    kept_tile,
    grad_tile,
    widen,
    narrow,
    load_sem,
    gift_send,
    gift_recv,
    cot_sem,
    kept_sem,
    grad_sem,
    reload_sem,
    over_sem,
    red_send,
    red_recv,
    zr_send,
    zr_recv,
    pair_send,
    pair_recv,
    give_send,
    give_recv,
    give_ready,
    *sems,
):
    at = Place()
    rows = second_ref.shape[0]
    pair, quad = 2 * rows, 4 * rows
    total_rows, carried = held.shape
    model = cot_ref.shape[1]
    wide = down.shape[0]
    own_wide = wide // 2
    units = wide // 4
    half = rows // 2
    partner = (at.e, at.partner)
    experts_all = 16
    loads, gifts = [], []
    for i, (ref, held_weights, first) in enumerate(
        ((gate_ref, gate_up, 0), (up_ref, gate_up, wide), (down_ref, down, 0))
    ):
        here = pl.ds(pl.multiple_of(first + at.core * own_wide, own_wide), own_wide)
        loads.append(pltpu.make_async_copy(ref, held_weights.at[here], load_sem.at[i]))
        gifts.append(
            remote(ref, held_weights.at[here], gift_send.at[i], gift_recv.at[i], at.sibling)
        )
    for copy in loads:
        copy.start()

    def named(shape, unit_axis):
        unit = lax.broadcasted_iota(jnp.int32, shape, unit_axis)
        lane = lax.broadcasted_iota(jnp.int32, shape, 1 - unit_axis)
        expert = at.e // 2 * 4
        for i in (1, 2, 3):
            expert = expert + (unit >= i * units).astype(jnp.int32)
        return ((lane == expert) | (lane == expert + experts_all)).astype(F32).astype(BF)

    widen[...] = named((EXTRA, wide), 1)
    narrow[...] = named((wide, EXTRA), 0)
    meet(at.everyone())
    for copy in gifts:
        copy.start()

    def side_first(k, side):
        return (at.plane(k) * 4 + (at.y if side else 1 - at.y) * 2) * rows

    def side_rows(k, side):
        return pl.ds(pl.multiple_of(side_first(k, side), pair), pair)

    def block(k, q, i=None):
        first, count = (0, rows) if i is None else (i * half, half)
        first = (at.plane(k) * 4 + at.column_base(q) // 2) * rows + first
        return held.at[pl.ds(pl.multiple_of(first, half), count)]

    def line_block(b):
        first = (b * 4 + at.column_base(OWN) // 2) * rows
        return held.at[pl.ds(pl.multiple_of(first, rows), rows)]

    line = Line(at, line_block, sems[:2])
    gather = Gather(at, block, sems[2:], sibling=False)
    first_row = (at.z * 4 + at.column_base(OWN) // 2) * rows
    held[pl.ds(pl.multiple_of(first_row, rows), rows)] = second_ref[...]
    line.begin()
    gather.own(0)

    def over_z(k):
        there = block(k, DIAG)
        return remote(there, there, over_sem.at[0], over_sem.at[1], partner)

    def cot_copy(k, side):
        return pltpu.make_async_copy(cot_ref.at[side_rows(k, side)], cot_tile, cot_sem)

    def kept_copy(k, side):
        return pltpu.make_async_copy(kept_tile, kept_ref.at[:, side_rows(k, side)], kept_sem)

    def compute(r, k, side, following):
        here = side_rows(k, side)
        acts[...] = lax.dot_general(
            held[here, :model], gate_up[...], (NT, ((), ())), preferred_element_type=F32
        )
        cot_copy(k, side).wait()
        back[...] = lax.dot_general(
            cot_tile[...], down[...], (NT, ((), ())), preferred_element_type=F32
        )
        following()

        @when(not (isinstance(r, int) and r == 0 and side == 1))
        def _():
            kept_copy(k, side).wait()

        out_first = r * quad + side * pair
        for i in range(pair // rows):
            strip_rows = slice(i * rows, (i + 1) * rows)
            first = side_first(k, side) + i * rows
            share_rows = held[pl.ds(pl.multiple_of(first, rows), rows), model:]
            gate_act, up_act = acts[strip_rows, :wide], acts[strip_rows, wide:]
            raw_back = back[strip_rows]
            share = jnp.dot(share_rows, widen[...], preferred_element_type=F32)
            sigmoid = 1.0 / (1.0 + jnp.exp(-gate_act))
            silu = gate_act * sigmoid
            hidden = silu * up_act
            product = hidden * raw_back
            high = product.astype(BF)
            low = (product - high.astype(F32)).astype(BF)
            share_grad = jnp.dot(high, narrow[...], preferred_element_type=F32) + jnp.dot(
                low, narrow[...], preferred_element_type=F32
            )
            lane = lax.broadcasted_iota(jnp.int32, share_grad.shape, 1)
            rounded = share_grad.astype(BF).astype(F32)
            share_grad = jnp.where(lane < experts_all, rounded, share_grad - rounded)
            hidden_low = (share * hidden).astype(BF)
            hidden_grad = share * raw_back
            gate_grad = (
                hidden_grad * up_act * sigmoid * (1.0 + gate_act * (1.0 - sigmoid))
            ).astype(BF)
            up_grad = (hidden_grad * silu).astype(BF)
            gate_tile[strip_rows, :wide] = gate_grad
            gate_tile[strip_rows, wide:] = up_grad
            hidden_tile[strip_rows] = hidden_low
            kept_tile[:wide, strip_rows] = gate_grad.T
            kept_tile[wide : 2 * wide, strip_rows] = up_grad.T
            kept_tile[2 * wide :, strip_rows] = hidden_low.T
            out_rows = pl.ds(pl.multiple_of(out_first + i * rows, rows), rows)
            part[out_rows, 2 * model :] = share_grad.astype(BF)
        kept_copy(k, side).start()
        there = pl.ds(pl.multiple_of(out_first, pair), pair)
        step = 512
        for start in range(0, model, step):
            part[there, start : start + step] = jnp.dot(
                hidden_tile[...], down[:, start : start + step], preferred_element_type=F32
            ).astype(BF)
            part[there, model + start : model + start + step] = jnp.dot(
                gate_tile[...], gate_up[:, start : start + step], preferred_element_type=F32
            ).astype(BF)

    def part_row(r, q, first=0):
        x = at.x if q in (YCOL, OWN) else 1 - at.x
        return r * quad + (pair if q in (XCOL, OWN) else 0) + x * rows + first

    def part_rows(r, q, first, count):
        return pl.ds(pl.multiple_of(part_row(r, q, first), min(count, half)), count)

    def half_a(r):
        src = part.at[part_rows(r, DIAG, 0, half)]
        return remote(src, diag_a.at[r % 2], red_send.at[0, r], red_recv.at[0, r], at.y_near)

    def half_b(r):
        src = part.at[part_rows(r, DIAG, half, half)]
        return remote(src, diag_b.at[r % 2], red_send.at[1, r], red_recv.at[1, r], at.x_near)

    def x_copy(r):
        src = part.at[part_rows(r, XCOL, 0, rows)]
        return remote(src, x_whole.at[r % 2], red_send.at[2, r], red_recv.at[2, r], at.x_near)

    def y_copy(r):
        src = part.at[part_rows(r, YCOL, 0, rows)]
        return remote(src, y_whole.at[r % 2], red_send.at[3, r], red_recv.at[3, r], at.y_near)

    def diag_over():
        src = part.at[part_rows(0, DIAG, 0, rows)]
        return remote(src, diag_z, red_send.at[0, 0], red_recv.at[0, 0], partner)

    strip = 32

    def by_strips(count, body):
        @pl.loop(0, count // strip)
        def _(i):
            body(pl.multiple_of(i * strip, strip))

    def reduce_diag(r):
        @when(r == 3)
        def _():
            diag_over().wait_recv()

            def body(row):
                here = part_rows(r, DIAG, row, strip)
                part[here] = (
                    part[here].astype(F32) + diag_z[pl.ds(row, strip)].astype(F32)
                ).astype(BF)

            by_strips(rows, body)

        @when(r == 0)
        def _():
            diag_over().start()

        @when(r > 0)
        def _():
            half_a(r).start()
            half_b(r).start()

    def reduce_x(r):
        @when(r > 0)
        def _():
            half_a(r).wait_recv()

            def body(row):
                here = part_rows(r, XCOL, row, strip)
                part[here] = (
                    part[here].astype(F32) + diag_a[r % 2, pl.ds(row, strip)].astype(F32)
                ).astype(BF)

            by_strips(half, body)

        x_copy(r).start()

    def reduce_y(r):
        @when(r > 0)
        def _():
            half_b(r).wait_recv()

            def body(row):
                here = part_rows(r, YCOL, half + row, strip)
                part[here] = (
                    part[here].astype(F32) + diag_b[r % 2, pl.ds(row, strip)].astype(F32)
                ).astype(BF)

            by_strips(half, body)

        y_copy(r).start()

    inner = (at.z == 1) | (at.z == 2)

    def near_copy():
        src = part.at[part_rows(0, OWN, 0, rows)]
        return remote(src, z_part.at[0], zr_send.at[0], zr_recv.at[0], partner)

    def pair_copy(r):
        block = pair_part.at[r - 1]
        return remote(block, block, pair_send.at[r - 1], pair_recv.at[r - 1], partner)

    def far_copy(r):
        there = at.plane(r + 1)
        return remote(
            pair_part.at[r - 1], z_part.at[1], zr_send.at[r], zr_recv.at[1], (at.e, there)
        )

    def pass_on(r):
        @pl.when(inner)
        def _():
            pair_copy(r).wait_recv()

            def body(row):
                here = pl.ds(row, strip)
                pair_part[r - 1, here] = (
                    pair_part[r - 1, here].astype(F32)
                    + part[part_rows(r, OWN, row, strip)].astype(F32)
                ).astype(BF)

            by_strips(rows, body)
            far_copy(r).start()

    def reduce_own(r):
        x_copy(r).wait_recv()
        y_copy(r).wait_recv()

        def total(row):
            here = pl.ds(row, strip)
            return (
                part[part_rows(r, OWN, row, strip)].astype(F32)
                + x_whole[r % 2, here].astype(F32)
                + y_whole[r % 2, here].astype(F32)
            )

        @when(r == 3)
        def _():
            near_copy().wait_recv()
            block = z_part.at[1]
            remote(block, block, zr_send.at[0], zr_recv.at[1], at.sibling).wait_recv()

            def body(row):
                here = pl.ds(row, strip)
                sums_ref[here] = total(row) + (
                    z_part[0, here].astype(F32) + z_part[1, here].astype(F32)
                )

            by_strips(rows, body)

        def keep(row):
            part[part_rows(r, OWN, row, strip)] = total(row).astype(BF)

        def lay_out(row):
            pair_part[r - 1, pl.ds(row, strip)] = total(row).astype(BF)

        @when(r == 0)
        def _():
            by_strips(rows, keep)
            near_copy().start()

        @when(between(r, 1, 2))
        def _():
            @pl.when(inner)
            def _():
                by_strips(rows, keep)

            @pl.when(jnp.logical_not(inner))
            def _():
                by_strips(rows, lay_out)
                pair_copy(r).start()

    def far_rows(k):
        line.arrive(k)
        gather.own(k)

    cot_copy(1, 1).start()
    line.arrive(1)
    gather.own(1)

    @pl.when(inner)
    def _():
        far_rows(2)

    gather.cross(0)
    gather.cross(1, halves=False)

    @pl.when(inner)
    def _():
        far_rows(3)

    for copy in loads + gifts:
        copy.wait()
    compute(0, 1, 1, lambda: cot_copy(1, 0).start())
    reduce_x(0)
    gather.diag(0)
    over_z(0).start()

    @pl.when(jnp.logical_not(inner))
    def _():
        far_rows(2)

    over_z(1).wait_recv()
    compute(0, 1, 0, lambda: cot_copy(2, 0).start())
    reduce_y(0)
    reduce_diag(0)

    @pl.when(jnp.logical_not(inner))
    def _():
        far_rows(3)

    gather.cross(2)
    gather.diag(2)
    compute(1, 2, 0, lambda: cot_copy(2, 1).start())
    reduce_diag(1)
    gather.cross(3)

    @pl.loop(1, 3)
    def _(r):
        k, later = r + 1, lax.rem(r + 2, 4)
        compute(r, k, 1, lambda: cot_copy(later, 0).start())
        reduce_own(r - 1)

        @pl.when(r == 1)
        def _():
            gather.diag(3)

        compute(r + 1, later, 0, lambda: cot_copy(later, 1).start())
        reduce_x(r)
        reduce_y(r)

        @pl.when(r == 2)
        def _():
            pass_on(1)

        reduce_diag(r + 1)

    compute(3, 0, 1, lambda: None)

    line.end()
    over_z(0).wait_send()
    diag_over().wait_send()
    near_copy().wait_send()
    x_copy(0).wait_send()
    y_copy(0).wait_send()
    for copy in (half_a(1), half_b(1), x_copy(1), y_copy(1)):
        copy.wait_send()
    pl.semaphore_signal(give_ready, inc=1, device_id=at.sibling, device_id_type=MESH)
    for k in range(4):
        gather.end(k, halves=k != 1)
    kept_copy(0, 1).wait()
    turned = [
        pltpu.make_async_copy(kept_ref.at[pl.ds(0, 2 * wide)], gate_up, load_sem.at[0]),
        pltpu.make_async_copy(kept_ref.at[pl.ds(2 * wide, wide)], down, load_sem.at[1]),
    ]
    for copy in turned:
        copy.start()
    step = 256
    chunks = model // step
    mine, theirs = at.core * own_wide, (1 - at.core) * own_wide

    def lanes_of(n):
        return pl.ds(pl.multiple_of(n * step, step), step)

    def turned_rows(first):
        return pl.ds(pl.multiple_of(first, own_wide), own_wide)

    def given(i, first, size):
        return part.at[pl.ds(0, own_wide), pl.ds(pl.multiple_of(i * model + first, step), size)]

    def taken(i, first, size):
        return part.at[pl.ds(quad, own_wide), pl.ds(pl.multiple_of(i * model + first, step), size)]

    def give_copies(n):
        first, size = n % 2 * (model // 2), model // 2
        return [
            remote(
                given(i, first, size),
                taken(i, first, size),
                give_send.at[n, i],
                give_recv.at[n, i],
                at.sibling,
            )
            for i in ((0, 1) if n < 2 else (0,))
        ]

    def gate_out(n):
        slot = lax.rem(n, 2)
        return [
            pltpu.make_async_copy(
                grad_tile.at[slot, pl.ds(i * own_wide, own_wide)],
                ref.at[:, lanes_of(n)],
                grad_sem.at[slot, i],
            )
            for i, ref in enumerate((gate_grad_ref, up_grad_ref))
        ]

    def down_out(n):
        slot = lax.rem(n, 2)
        return pltpu.make_async_copy(
            grad_tile.at[slot, pl.ds(0, own_wide)],
            down_grad_ref.at[:, lanes_of(n)],
            grad_sem.at[slot, 0],
        )

    def reload(n):
        return pltpu.make_async_copy(
            cot_ref.at[:, lanes_of(n)], held.at[:, lanes_of(n)], reload_sem.at[n]
        )

    def gate_up_chunk(first, i, n):
        return jnp.dot(
            gate_up[turned_rows(i * wide + first)],
            held[:, lanes_of(n)],
            preferred_element_type=F32,
        )

    def down_chunk(first, n):
        return jnp.dot(
            down[turned_rows(first)], held[:, lanes_of(n)], preferred_element_type=F32
        )

    def in_half(n, body):
        half_chunks = chunks // 2
        pl.loop(n % 2 * half_chunks, (n % 2 + 1) * half_chunks)(body)

    for copy in turned:
        copy.wait()
    for part_of in (0, 1):

        def give_gate_up(n):
            for i in (0, 1):
                given(i, n * step, step)[...] = gate_up_chunk(theirs, i, n).astype(BF)

        in_half(part_of, give_gate_up)
        if part_of == 0:
            pl.semaphore_wait(give_ready, 1)
        for copy in give_copies(part_of):
            copy.start()

    reduce_own(2)
    for part_of in (0, 1):
        for copy in give_copies(part_of):
            copy.wait_recv()

        def own_gate_up(n):
            @pl.when(n >= 2)
            def _():
                for copy in gate_out(n):
                    copy.wait()

            for i in (0, 1):
                grad_tile[lax.rem(n, 2), i * own_wide : (i + 1) * own_wide] = (
                    gate_up_chunk(mine, i, n) + taken(i, n * step, step)[...].astype(F32)
                ).astype(BF)
            for copy in gate_out(n):
                copy.start()
            reload(n).start()

        in_half(part_of, own_gate_up)

    pl.semaphore_signal(give_ready, inc=1, device_id=at.sibling, device_id_type=MESH)
    reduce_x(3)
    reduce_y(3)
    pass_on(2)
    for part_of in (0, 1):
        for copy in give_copies(part_of):
            copy.wait_send()
    for part_of in (2, 3):

        def give_down(n):
            reload(n).wait()
            given(0, n * step, step)[...] = down_chunk(theirs, n).astype(BF)

        in_half(part_of, give_down)
        if part_of == 2:
            pl.semaphore_wait(give_ready, 1)
        for copy in give_copies(part_of):
            copy.start()

    for n in (0, 1):
        for copy in gate_out(n):
            copy.wait()
    for part_of in (2, 3):
        for copy in give_copies(part_of):
            copy.wait_recv()

        def own_down(n):
            @pl.when(n >= 2)
            def _():
                down_out(n).wait()

            grad_tile[lax.rem(n, 2), :own_wide] = (
                down_chunk(mine, n) + taken(0, n * step, step)[...].astype(F32)
            ).astype(BF)
            down_out(n).start()

        in_half(part_of, own_down)

    reduce_own(3)
    for n in (0, 1):
        down_out(n).wait()

    for n in (2, 3):
        for copy in give_copies(n):
            copy.wait_send()
    for r in (2, 3):
        for copy in (half_a(r), half_b(r), x_copy(r), y_copy(r)):
            copy.wait_send()
    for r in (1, 2):

        @pl.when(inner)
        def _():
            far_copy(r).wait_send()

        @pl.when(jnp.logical_not(inner))
        def _():
            pair_copy(r).wait_send()


def experts_in_one(second_wide, cot_all, gate, up, down):
    rows, carried = second_wide.shape
    total_rows, model = cot_all.shape
    wide = 2 * down.shape[0]
    pair, half = 2 * rows, rows // 2
    both = 2 * model + EXTRA
    vmem = pl.BlockSpec(memory_space=pltpu.VMEM)
    hbm = pl.BlockSpec(memory_space=pl.ANY)
    dma = pltpu.SemaphoreType.DMA
    shape = jax.ShapeDtypeStruct
    return pl.pallas_call(
        expert_kernel,
        out_shape=(
            shape((rows, both), F32),
            shape((wide // 2, model), BF),
            shape((wide // 2, model), BF),
            shape((wide // 2, model), BF),
            shape((3 * wide, total_rows), BF),
        ),
        in_specs=[vmem, hbm, hbm, hbm, hbm],
        out_specs=(vmem, hbm, hbm, hbm, hbm),
        scratch_shapes=[
            pltpu.VMEM((total_rows, carried), BF),
            pltpu.VMEM((16 * rows, both), BF),
            pltpu.VMEM((2, half, both), BF),
            pltpu.VMEM((2, half, both), BF),
            pltpu.VMEM((rows, both), BF),
            pltpu.VMEM((2, rows, both), BF),
            pltpu.VMEM((2, rows, both), BF),
            pltpu.VMEM((2, rows, both), BF),
            pltpu.VMEM((2, rows, both), BF),
            pltpu.VMEM((pair, model), BF),
            pltpu.VMEM((2 * wide, model), BF),
            pltpu.VMEM((wide, model), BF),
            pltpu.VMEM((pair, 2 * wide), F32),
            pltpu.VMEM((pair, wide), F32),
            pltpu.VMEM((pair, 2 * wide), BF),
            pltpu.VMEM((pair, wide), BF),
            pltpu.VMEM((3 * wide, pair), BF),
            pltpu.VMEM((2, wide, 256), BF),
            pltpu.VMEM((EXTRA, wide), BF),
            pltpu.VMEM((wide, EXTRA), BF),
            dma((3,)),
            dma((3,)),
            dma((3,)),
            dma,
            dma,
            dma((2, 2)),
            dma((model // 256,)),
            dma((2,)),
            dma((4, 4)),
            dma((4, 4)),
            dma((3,)),
            dma((2,)),
            dma((2,)),
            dma((2,)),
            dma((4, 2)),
            dma((4, 2)),
            pltpu.SemaphoreType.REGULAR,
            *Line.semaphores(),
            *Gather.semaphores(False),
        ],
        compiler_params=pltpu.CompilerParams(
            collective_id=0, has_side_effects=True, vmem_limit_bytes=VMEM_BYTES
        ),
        cost_estimate=pl.CostEstimate(
            flops=2 * total_rows * model * wide * 9,
            bytes_accessed=8 * total_rows * model,
            transcendentals=total_rows * wide,
        ),
    )(second_wide, cot_all, gate, up, down)


def between(r, low, high):
    if isinstance(r, int):
        return low <= r <= high
    return (r >= low) & (r <= high)


class Tree:
    def __init__(self, at, refs, sems):
        (self.part, self.from_sib, self.diag_sum, self.x_sum, self.y_sum) = refs[:5]
        (self.diag_a, self.diag_b, self.x_whole, self.y_whole) = refs[5:]
        self.part_send, self.part_recv, self.send, self.recv = sems
        self.at = at
        self.rows = self.diag_sum.shape[0]
        self.half = self.rows // 2
        self.strip = 32

    def part_copy(self, q):
        return remote(
            self.part.at[q, 1 - self.at.core],
            self.from_sib.at[q],
            self.part_send.at[q],
            self.part_recv.at[q],
            self.at.sibling,
        )

    def half_a(self):
        there = self.diag_sum.at[pl.ds(0, self.half)]
        return remote(there, self.diag_a, self.send.at[0], self.recv.at[0], self.at.y_near)

    def half_b(self):
        there = self.diag_sum.at[pl.ds(self.half, self.half)]
        return remote(there, self.diag_b, self.send.at[1], self.recv.at[1], self.at.x_near)

    def x_copy(self):
        return remote(self.x_sum, self.x_whole, self.send.at[2], self.recv.at[2], self.at.x_near)

    def y_copy(self):
        return remote(self.y_sum, self.y_whole, self.send.at[3], self.recv.at[3], self.at.y_near)

    def strips(self, first, count, body):
        strip = self.strip

        @pl.loop(first // strip, (first + count) // strip)
        def _(i):
            body(pl.ds(pl.multiple_of(i * strip, strip), strip), i)

    def chip_sum(self, q, here):
        return self.part[q, self.at.core, here].astype(F32) + self.from_sib[q, here].astype(F32)

    def do_diag(self):
        self.part_copy(DIAG).wait_recv()

        def body(here, i):
            self.diag_sum[here] = self.chip_sum(DIAG, here).astype(BF)

        self.strips(0, self.rows, body)
        self.half_a().start()
        self.half_b().start()

    def do_x(self):
        self.part_copy(XCOL).wait_recv()
        self.half_a().wait_recv()

        def with_half(here, i):
            self.x_sum[here] = (
                self.chip_sum(XCOL, here) + self.diag_a[here].astype(F32)
            ).astype(BF)

        def alone(here, i):
            self.x_sum[here] = self.chip_sum(XCOL, here).astype(BF)

        self.strips(0, self.half, with_half)
        self.strips(self.half, self.half, alone)
        self.x_copy().start()

    def do_y(self):
        self.part_copy(YCOL).wait_recv()
        self.half_b().wait_recv()

        def alone(here, i):
            self.y_sum[here] = self.chip_sum(YCOL, here).astype(BF)

        def with_half(here, i):
            low = pl.ds(pl.multiple_of(i * self.strip - self.half, self.strip), self.strip)
            self.y_sum[here] = (self.chip_sum(YCOL, here) + self.diag_b[low].astype(F32)).astype(BF)

        self.strips(0, self.half, alone)
        self.strips(self.half, self.half, with_half)
        self.y_copy().start()

    def do_own(self, result):
        self.part_copy(OWN).wait_recv()
        self.x_copy().wait_recv()
        self.y_copy().wait_recv()

        def body(here, i):
            result[here] = (
                self.chip_sum(OWN, here)
                + self.x_whole[here].astype(F32)
                + self.y_whole[here].astype(F32)
            ).astype(BF)

        self.strips(0, self.rows, body)

    def drain(self):
        for q in range(4):
            self.part_copy(q).wait_send()
        for copy in (self.half_a(), self.half_b(), self.x_copy(), self.y_copy()):
            copy.wait_send()

    @staticmethod
    def buffers(rows, width):
        piece = pltpu.VMEM((rows, width), BF)
        half = pltpu.VMEM((rows // 2, width), BF)
        return [
            pltpu.VMEM((4, 2, rows, width), BF),
            pltpu.VMEM((4, rows, width), BF),
            piece,
            piece,
            piece,
            half,
            half,
            piece,
            piece,
        ]

    @staticmethod
    def semaphores():
        return [pltpu.SemaphoreType.DMA((4,))] * 4


class Spread:
    def __init__(self, at, own, out, sems, first=0):
        self.at, self.own, self.out, self.first = at, own, out, first
        self.send, self.recv, self.local = sems
        self.rows = own.shape[0]
        self.stride = out.shape[0] // 8
        self.e_x, self.e_y, self.e_d = at.x_near[0], at.y_near[0], at.diagonal

    def place(self, slot, first=0, rows=None):
        row = slot * self.stride + self.first + first
        rows = rows or self.rows
        return self.out.at[pl.ds(pl.multiple_of(row, rows), rows)]

    def to(self, src, slot, device, sem):
        return remote(src, self.place(slot), self.send.at[sem], self.recv.at[sem], device)

    def own_copies(self):
        e = self.at.e
        return (
            self.to(self.own, e, self.at.x_near, 0),
            self.to(self.own, e, self.at.y_near, 1),
            self.to(self.own, e, self.at.sibling, 2),
        )

    def here(self):
        return pltpu.make_async_copy(self.own, self.place(self.at.e), self.local)

    def half_copy(self, slot, first, device, sem):
        there = self.place(slot, first, self.rows // 2)
        return remote(there, there, self.send.at[sem], self.recv.at[sem], device)

    def cross_copies(self):
        return (
            self.half_copy(self.e_x, 0, self.at.y_near, 3),
            self.half_copy(self.e_y, self.rows // 2, self.at.x_near, 4),
            self.to(self.place(self.e_x), self.e_x, self.at.sibling, 5),
            self.to(self.place(self.e_y), self.e_y, self.at.sibling, 6),
        )

    def diag_copy(self):
        return self.to(self.place(self.e_d), self.e_d, self.at.sibling, 7)

    def begin(self):
        for copy in self.own_copies():
            copy.start()
        self.here().start()

    def cross(self):
        x, y, s = self.own_copies()
        x.wait_recv()
        y.wait_recv()
        for copy in self.cross_copies():
            copy.start()
        s.wait_recv()

    def diag(self):
        a, b, s, t = self.cross_copies()
        a.wait_recv()
        b.wait_recv()
        self.diag_copy().start()
        s.wait_recv()
        t.wait_recv()

    def end(self):
        self.diag_copy().wait()
        for copy in self.own_copies() + self.cross_copies():
            copy.wait_send()
        self.here().wait()

    @staticmethod
    def semaphores():
        dma = pltpu.SemaphoreType.DMA
        return [dma((8,)), dma((8,)), dma]


def swap(v):
    return pltpu.roll(v, v.shape[-1] // 2, v.ndim - 1)


def fold(v):
    return jnp.sum(v.reshape(v.shape[0] // 8, 8, v.shape[1]), axis=0)


def split_rows(v):
    high = v.astype(BF)
    return jnp.concatenate([v, v - high.astype(F32)], axis=0).astype(BF)


def back_kernel(
    middle_ref,
    share_ref,
    cot_ref,
    router_ref,
    small_ref,
    cos_ref,
    sin_ref,
    second_ref,
    place_ref,
    sums_ref,
    w_out_ref,
    w_cols_ref,
    mixed_ref,
    normed_ref,
    raw_ref,
    prob_ref,
    dnormed_ref,
    block_out_ref,
    middle_grad_ref,
    out_grad_ref,
    cols_grad_ref,
    w_out_held,
    w_cols_held,
    mixed_held,
    normed_held,
    raw_held,
    prob_held,
    held,
    raw_grad,
    left,
    right,
    share_sum,
    router_wide,
    rows_out,
    rows_in,
    gain_total,
    head_total,
    out_total,
    *rest,
):
    at = Place()
    rows, model = middle_ref.shape
    quarter = model // 4
    experts_all = router_ref.shape[1]
    own_part = dnormed_ref
    pair = 2 * rows
    width = HEAD_WIDTH
    heads = w_out_ref.shape[0] // width
    q_cols = heads * width
    cols = w_cols_ref.shape[1]
    count = model // 4 // 8
    scale = HEAD_WIDTH ** (-0.5)
    rest = list(rest)

    def grab(count):
        got, rest[:] = rest[:count], rest[count:]
        return got

    cols_totals, cols_alls = grab(2), grab(2)
    out_tree = Tree(at, grab(9), grab(4))
    cols_trees = [Tree(at, grab(9), grab(4)) for _ in (0, 1)]
    out_spread = Spread(at, out_total, out_grad_ref, grab(3))
    cols_spreads = [
        Spread(at, cols_alls[i], cols_grad_ref, grab(3), i * (count // 2)) for i in (0, 1)
    ]

    def line_block(b):
        return held.at[pl.ds(pl.multiple_of(b * rows, rows), rows)]

    line = Line(at, line_block, grab(2))
    sums = LineSum(at, rows_out, rows_in, grab(2))
    outer = (at.z == 0) | (at.z == 3)
    ex_send, ex_recv, ex_local, load_sem, sum_sem = grab(5)
    loads = [
        pltpu.make_async_copy(src, dst, load_sem.at[i])
        for i, (src, dst) in enumerate(
            (
                (w_out_ref, w_out_held),
                (raw_ref, raw_held),
                (w_cols_ref, w_cols_held),
                (normed_ref, normed_held),
                (prob_ref, prob_held),
                (mixed_ref, mixed_held),
            )
        )
    ]

    def sum_copy(j):
        lanes = pl.ds(pl.multiple_of(j * EXTRA, EXTRA), EXTRA)
        return pltpu.make_async_copy(sums_ref.at[:, lanes], prob_held.at[j], sum_sem.at[0])

    greet(at.everyone())
    columns = 2 * model // EXTRA
    share_copy = pltpu.make_async_copy(
        sums_ref.at[:, pl.ds(2 * model, EXTRA)], share_sum, sum_sem.at[1]
    )
    share_copy.start()

    @pl.loop(0, columns)
    def _(j):
        sum_copy(j).start()

    for copy in loads[:4]:
        copy.start()

    row_id = lax.broadcasted_iota(jnp.int32, right.shape, 0)
    lane_id = lax.broadcasted_iota(jnp.int32, right.shape, 1)
    chosen = (lane_id == experts_all) & (row_id >= rows) & (row_id < 2 * rows)
    for i in (0, 1, 2):
        first = 2 * rows + 16 * i
        chosen = chosen | (
            (lane_id == experts_all + 1 + i) & (row_id >= first) & (row_id < first + 16)
        )
    right[...] = chosen.astype(F32).astype(BF)
    router_wide[...] = jnp.zeros_like(router_wide)
    left[pl.ds(0, rows)] = second_ref[:, :model]
    left[pl.ds(2 * rows, rows)] = jnp.zeros((rows, model), BF)
    lane = lax.broadcasted_iota(jnp.int32, (rows, EXTRA), 1)
    share = share_ref[...]
    share_copy.wait()
    dshare = share_sum[...]
    dshare = dshare + pltpu.roll(dshare, EXTRA - experts_all, 1)
    weighed = jnp.where(lane < experts_all, share * dshare, 0.0)
    mean_share = jnp.sum(weighed, axis=-1, keepdims=True)
    logit_grad = jnp.where(lane < experts_all, share * (dshare - mean_share), 0.0).astype(BF)
    right[pl.ds(0, rows)] = logit_grad
    middle = middle_ref[...]
    inverse = lax.rsqrt(jnp.mean(middle * middle, axis=-1, keepdims=True) + epsilon)
    mean = jnp.zeros((rows, 1), F32)

    @pl.loop(0, columns)
    def _(j):
        sum_copy(j).wait()

    for j in range(4):
        router_wide[:experts_all, j * quarter : (j + 1) * quarter] = router_ref[j]
    for j in range(model // EXTRA):
        lanes = slice(j * EXTRA, (j + 1) * EXTRA)
        block_out_ref[:, lanes] = (middle[:, lanes] + prob_held[j]).astype(BF)
        second_grad = prob_held[model // EXTRA + j] + dot(logit_grad, router_wide[:, lanes], NN)
        unit = middle[:, lanes] * inverse
        left[rows : 2 * rows, lanes] = (second_grad * unit).astype(BF)
        of = j * EXTRA % quarter
        scaled = second_grad * small_ref[j * EXTRA // quarter, 1:2, of : of + EXTRA]
        middle_grad_ref[:, lanes] = scaled
        mean += jnp.sum(scaled * unit, axis=-1, keepdims=True)
    loads[4].start()
    loads[5].start()
    mean = mean / model
    middle_grad = cot_ref[...].astype(F32) + inverse * (
        middle_grad_ref[...] - middle * inverse * mean
    )
    middle_grad_ref[...] = middle_grad
    head_gains = small_ref[0, 2:3, :] + small_ref[1, 2:3, :]
    head_gains += small_ref[2, 2:3, :] + small_ref[3, 2:3, :]

    held[pl.ds(pl.multiple_of(at.z * rows, rows), rows)] = middle_grad.astype(BF)
    meet(at.everyone(), greeted=True)
    line.begin()
    gain_total[...] = jnp.zeros_like(gain_total)
    head_total[...] = jnp.zeros_like(head_total)

    def attention(far):
        first = 2 * (1 - at.half if far else at.half)
        both = pl.ds(pl.multiple_of(first * rows, pair), pair)
        mixed_grads = lax.dot_general(
            held[both, :], w_out_held[...], (NT, ((), ())), preferred_element_type=F32
        ).astype(BF)
        for i in (0, 1):
            heads_back(first + i, mixed_grads[i * rows : (i + 1) * rows])
            if not far and i == 0:

                @pl.when(jnp.logical_not(outer))
                def _():
                    line.arrive(3)

            if far and i == 0:
                out_tree.do_x()
                out_tree.do_y()
        step = 512
        for start in range(0, model, step):
            lanes = slice(start, start + step)
            part = lax.dot_general(
                raw_grad[both, :],
                w_cols_held[start : start + step, :],
                (NT, ((), ())),
                preferred_element_type=F32,
            )
            gain_total[:, lanes] += fold(part * normed_held[both, lanes].astype(F32))
            if not far:
                own_part[:, lanes] = jnp.where(at.z % 2 == 0, part[:rows], part[rows:])
            rows_out[first, :, lanes] = part[:rows].astype(BF)
            rows_out[first + 1, :, lanes] = part[rows:].astype(BF)
        if not far:
            sums.give_near(True)
        else:

            @pl.when(outer)
            def _():
                sums.give_far()

    def heads_back(b, mixed_grad):
        here = pl.ds(pl.multiple_of(b * rows, rows), rows)
        cosine, sine = cos_ref[here, :], sin_ref[here, :]

        def unit_of(v):
            inverse = lax.rsqrt(jnp.mean(v * v, axis=-1, keepdims=True) + epsilon)
            return v * inverse, inverse

        def low_of(unit, gain):
            scaled = unit * gain
            return (scaled * cosine + swap(scaled) * sine).astype(BF)

        def back_of(gradient, unit, inverse, gain, slot):
            turned = gradient * cosine - swap(gradient) * sine
            head_total[slot] += fold(turned * unit)
            return norm_back(turned * gain, unit, inverse).astype(BF)

        q_gain, k_gain = head_gains[:, :width], head_gains[:, width : 2 * width]
        k_unit, k_inverse = unit_of(raw_held[here, q_cols : q_cols + width])
        k_low = low_of(k_unit, k_gain)
        v_low = raw_held[here, q_cols + width : q_cols + 2 * width].astype(BF)
        k_grad = jnp.zeros((rows, width), F32)
        v_grad = jnp.zeros((rows, width), F32)
        for h in range(heads):
            lanes = slice(h * width, (h + 1) * width)
            q_unit, q_inverse = unit_of(raw_held[here, lanes])
            q_low = low_of(q_unit, q_gain)
            prob = prob_held[b * heads + h]
            own_grad = mixed_grad[:, lanes]
            v_grad += dot(prob.astype(BF), own_grad, TN)
            prob_grad = dot(own_grad, v_low, NT)
            score_grad = (
                prob * (prob_grad - jnp.sum(prob * prob_grad, axis=-1, keepdims=True))
            ).astype(BF)
            q_grad = dot(score_grad, k_low, NN) * scale
            k_grad += dot(score_grad, q_low, TN)
            raw_grad[here, lanes] = back_of(q_grad, q_unit, q_inverse, q_gain, 0)
        raw_grad[here, q_cols : q_cols + width] = back_of(
            k_grad * scale, k_unit, k_inverse, k_gain, 1
        )
        raw_grad[here, q_cols + width : q_cols + 2 * width] = v_grad.astype(BF)

    def out_piece(q):
        base = at.column_base(q)
        lanes = pl.ds(pl.multiple_of(base * width, 2 * width), 2 * width)
        left_side = mixed_held[:, lanes]
        step = 512
        for start in range(0, model, step):
            total = dot(left_side, held[:, start : start + step], TN)
            for c in (0, 1):
                out_tree.part[q, c, :, start : start + step] = total[
                    c * width : (c + 1) * width
                ].astype(BF)
        out_tree.part_copy(q).start()

    some = count // 2

    def cols_piece(q):
        base = at.column_base(q)
        for there in range(4):
            lanes = pl.ds(
                pl.multiple_of(there * (model // 4) + base * count, 2 * count), 2 * count
            )
            block = dot(normed_held[:, lanes], raw_grad[...], TN)
            small = dot(left[:, lanes], right[...], TN)
            for c in (0, 1):
                for i, tree in enumerate(cols_trees):
                    of = slice(c * count + i * some, c * count + (i + 1) * some)
                    here = pl.ds(there * some, some)
                    tree.part[q, c, here, :cols] = block[of].astype(BF)
                    tree.part[q, c, here, cols:] = small[of].astype(BF)
        cols_trees[0].part_copy(q).start()

    groups = ((0, q_cols), (q_cols, width), (q_cols + width, width), (cols, EXTRA))

    def exchange_refs(i, to, of):
        here = pl.ds(pl.multiple_of(to * some, some), some)
        first = 0
        refs = []
        for start, size in groups:
            lanes = pl.ds(pl.multiple_of(first + of * size, size), size)
            refs.append((cols_totals[i].at[here, pl.ds(start, size)], cols_alls[i].at[:, lanes]))
            first += 4 * size
        return refs

    def exchange(i, k):
        there = at.plane(k)
        turn = at.turn_at(there)
        return [
            remote(src, dst, ex_send.at[i, k - 1, j], ex_recv.at[i, turn - 1, j], (at.e, there))
            for j, (src, dst) in enumerate(exchange_refs(i, there, at.z))
        ]

    def exchange_arrival(i, k):
        return [
            remote(dst, dst, ex_send.at[i, k - 1, j], ex_recv.at[i, k - 1, j], at.sibling)
            for j, (src, dst) in enumerate(exchange_refs(i, at.z, at.plane(k)))
        ]

    def own_exchange(i):
        return [
            pltpu.make_async_copy(src, dst, ex_local.at[i, j])
            for j, (src, dst) in enumerate(exchange_refs(i, at.z, at.z))
        ]

    def begin_exchange(i):
        cols_trees[i].do_own(cols_totals[i])
        for k in (1, 2, 3):
            for copy in exchange(i, k):
                copy.start()
        for copy in own_exchange(i):
            copy.start()

    def end_exchange(i):
        for copy in own_exchange(i):
            copy.wait()
        for k in (1, 2, 3):
            for copy in exchange_arrival(i, k):
                copy.wait_recv()
        cols_spreads[i].begin()

    line.arrive(1)

    @pl.when(jnp.logical_not(outer))
    def _():
        line.arrive(2)

    for copy in loads[:5]:
        copy.wait()
    attention(False)

    @pl.when(outer)
    def _():
        line.arrive(2)
        line.arrive(3)

    loads[5].wait()
    for q in (DIAG, XCOL, YCOL, OWN):
        out_piece(q)
    out_tree.do_diag()
    attention(True)
    out_tree.do_own(out_total)
    out_spread.begin()
    for j in range(4):
        lanes = slice(j * quarter, (j + 1) * quarter)
        left[pl.ds(2 * rows, 16), lanes] = split_rows(
            gain_total[:, lanes] / small_ref[j, 0:1, :]
        )
    for slot in (0, 1):
        placed = jnp.dot(
            split_rows(head_total[slot]), place_ref[...], preferred_element_type=F32
        )
        left[pl.ds(2 * rows + 16 * (slot + 1), 16)] = placed.astype(BF)
    first, last = cols_trees
    for q in (DIAG, XCOL, YCOL, OWN):
        cols_piece(q)
    for q in (DIAG, XCOL, YCOL, OWN):
        last.part_copy(q).start()
    first.do_diag()
    last.do_diag()
    out_spread.cross()
    first.do_x()
    first.do_y()

    @pl.when(jnp.logical_not(outer))
    def _():
        sums.give_far()

    last.do_x()
    last.do_y()
    begin_exchange(0)
    sums.give_near(False)
    begin_exchange(1)
    end_exchange(0)
    out_spread.diag()
    end_exchange(1)
    cols_spreads[0].cross()
    sums.wait()

    @pl.loop(0, rows // 32)
    def _(i):
        here = pl.ds(pl.multiple_of(i * 32, 32), 32)
        dnormed_ref[here] += sums.total(here)

    cols_spreads[1].cross()
    cols_spreads[0].diag()
    cols_spreads[1].diag()
    out_spread.end()
    for spread in cols_spreads:
        spread.end()
    out_tree.drain()
    for tree in cols_trees:
        tree.drain()
    line.end()
    sums.end()
    for i in (0, 1):
        for k in (1, 2, 3):
            for copy in exchange(i, k):
                copy.wait_send()


def back_in_one(resident, sums, loaded):
    w_out, w_cols = loaded[:2]
    rows, model = resident[0].shape
    cols = w_cols.shape[1]
    wide = cols + EXTRA
    count = model // 4 // 8
    vmem = pl.BlockSpec(memory_space=pltpu.VMEM)
    hbm = pl.BlockSpec(memory_space=pl.ANY)
    dma = pltpu.SemaphoreType.DMA
    return pl.pallas_call(
        back_kernel,
        out_shape=(
            jax.ShapeDtypeStruct((rows, model), F32),
            jax.ShapeDtypeStruct((rows, model), BF),
            jax.ShapeDtypeStruct((rows, model), F32),
            jax.ShapeDtypeStruct((8 * HEAD_WIDTH, model), BF),
            jax.ShapeDtypeStruct((8 * count, 4 * wide), BF),
        ),
        in_specs=[vmem] * len(resident) + [hbm] * (1 + len(loaded)),
        out_specs=(vmem, vmem, vmem, hbm, hbm),
        scratch_shapes=[
            *[pltpu.VMEM(v.shape, v.dtype) for v in loaded],
            pltpu.VMEM((4 * rows, model), BF),
            pltpu.VMEM((4 * rows, cols), BF),
            pltpu.VMEM((3 * rows, model), BF),
            pltpu.VMEM((3 * rows, EXTRA), BF),
            pltpu.VMEM((rows, EXTRA), F32),
            pltpu.VMEM((EXTRA, model), BF),
            pltpu.VMEM((4, rows, model), BF),
            pltpu.VMEM((5, rows, model), BF),
            pltpu.VMEM((8, model), F32),
            pltpu.VMEM((2, 8, HEAD_WIDTH), F32),
            pltpu.VMEM((HEAD_WIDTH, model), BF),
            *[pltpu.VMEM((2 * count, wide), BF)] * 2,
            *[pltpu.VMEM((count // 2, 4 * wide), BF)] * 2,
            *Tree.buffers(HEAD_WIDTH, model),
            *Tree.semaphores(),
            *Tree.buffers(2 * count, wide),
            *Tree.semaphores(),
            *Tree.buffers(2 * count, wide),
            *Tree.semaphores(),
            *Spread.semaphores(),
            *Spread.semaphores(),
            *Spread.semaphores(),
            *Line.semaphores(),
            *LineSum.semaphores(),
            dma((2, 3, 4)),
            dma((2, 3, 4)),
            dma((2, 4)),
            dma((6,)),
            dma((2,)),
        ],
        compiler_params=pltpu.CompilerParams(
            collective_id=1, has_side_effects=True, vmem_limit_bytes=VMEM_BYTES
        ),
        cost_estimate=pl.CostEstimate(
            flops=2 * 4 * rows * model * cols * 5,
            bytes_accessed=64 * 1024 * 1024,
            transcendentals=4 * rows * cols,
        ),
    )(*resident, sums, *loaded)


def front_kernel(
    tokens_ref,
    small_ref,
    router_ref,
    w_query_ref,
    w_key_ref,
    w_value_ref,
    w_out_ref,
    table_ref,
    chosen_ref,
    cot_ref,
    second_ref,
    middle_ref,
    share_ref,
    w_cols_out,
    normed_out,
    raw_out,
    prob_out,
    mixed_out,
    cos_ref,
    sin_ref,
    small_all_ref,
    router_all_ref,
    cot_all_ref,
    w_cols_ref,
    normed_ref,
    raw_ref,
    prob_ref,
    mixed_ref,
    own_part,
    router_wide,
    rows_out,
    rows_in,
    small_send,
    small_recv,
    piece_send,
    piece_recv,
    piece_local,
    cot_local,
    store_sem,
    *sems,
):
    at = Place()
    rows, model = tokens_ref.shape
    pair = 2 * rows
    width = HEAD_WIDTH
    q_cols = w_query_ref.shape[1] // 4
    heads = q_cols // width
    cols = q_cols + 2 * width
    quarter = model // 4
    count = quarter // 8
    half = rows // 2
    experts_all = router_ref.shape[0]
    scale = HEAD_WIDTH ** (-0.5)
    meet(at.everyone())

    cot_here = pltpu.make_async_copy(cot_ref, cot_all_ref.at[at.z, at.e // 2], cot_local)
    cot_here.start()

    small_all_ref[at.z] = small_ref[...]
    router_all_ref[at.z] = router_ref[...]

    def small_copies(k):
        there = at.plane(k)
        turn = at.turn_at(there)
        return [
            remote(
                ref,
                ref_all.at[at.z],
                small_send.at[k - 1, i],
                small_recv.at[turn - 1, i],
                (at.e, there),
            )
            for i, (ref, ref_all) in enumerate(
                ((small_ref, small_all_ref), (router_ref, router_all_ref))
            )
        ]

    for k in (1, 2, 3):
        for copy in small_copies(k):
            copy.start()

    def w_block(k, q, i=None):
        first, size = (0, count) if i is None else (i * (count // 2), count // 2)
        row = at.plane(k) * quarter + at.own(q) * count + first
        return w_cols_ref.at[pl.ds(pl.multiple_of(row, count // 2), size)]

    def piece_refs(there):
        own = pl.ds(pl.multiple_of(at.e * count, count), count)
        row = pl.ds(pl.multiple_of(at.z * quarter + at.e * count, count), count)
        narrow = pl.ds(pl.multiple_of(there * width, width), width)
        return (
            (
                w_query_ref.at[own, pl.ds(pl.multiple_of(there * q_cols, q_cols), q_cols)],
                w_cols_ref.at[row, pl.ds(0, q_cols)],
            ),
            (w_key_ref.at[own, narrow], w_cols_ref.at[row, pl.ds(q_cols, width)]),
            (w_value_ref.at[own, narrow], w_cols_ref.at[row, pl.ds(q_cols + width, width)]),
        )

    def piece_copies(k):
        there = at.plane(k)
        turn = at.turn_at(there)
        return [
            remote(
                src, dst, piece_send.at[k - 1, i], piece_recv.at[turn - 1, i], (at.e, there)
            )
            for i, (src, dst) in enumerate(piece_refs(there))
        ]

    def pieces_arrive(k):
        block = w_block(k, OWN)
        for i, (first, size) in enumerate(((0, q_cols), (q_cols, width), (q_cols, width))):
            part = block.at[:, pl.ds(first, size)]
            remote(
                part, part, piece_send.at[k - 1, i], piece_recv.at[k - 1, i], at.sibling
            ).wait_recv()

    own_pieces = [
        pltpu.make_async_copy(src, dst, piece_local.at[i])
        for i, (src, dst) in enumerate(piece_refs(at.z))
    ]
    for copy in own_pieces:
        copy.start()
    for k in (1, 2, 3):
        for copy in piece_copies(k):
            copy.start()
    weights = Gather(at, w_block, sems[2:10])
    for copy in own_pieces:
        copy.wait()
    weights.own(0)

    def normed_block(b):
        return normed_ref.at[pl.ds(pl.multiple_of(b * rows, rows), rows)]

    line = Line(at, normed_block, sems[10:12])
    source = tokens_ref[...].astype(F32)
    inverse = lax.rsqrt(jnp.mean(source * source, axis=-1, keepdims=True) + epsilon)
    for k in (1, 2, 3):
        for i, ref_all in enumerate((small_all_ref, router_all_ref)):
            block = ref_all.at[at.plane(k)]
            remote(
                block, block, small_send.at[k - 1, i], small_recv.at[k - 1, i], at.sibling
            ).wait_recv()
    own_rows = pl.ds(pl.multiple_of(at.z * rows, rows), rows)
    for j in range(4):
        lanes = slice(j * quarter, (j + 1) * quarter)
        normed_ref[own_rows, lanes] = (source[:, lanes] * inverse * small_all_ref[j, 0:1, :]).astype(BF)
        router_wide[0:experts_all, lanes] = router_all_ref[j]
        router_wide[experts_all : 2 * experts_all, lanes] = router_all_ref[j]
    router_wide[2 * experts_all :] = jnp.zeros((EXTRA - 2 * experts_all, model), BF)
    line.begin()

    def cot_block(k, q, i=None):
        block = cot_all_ref.at[at.plane(k), at.column_base(q) // 2]
        return block if i is None else block.at[pl.ds(i * half, half)]

    def cot_line_block(b):
        return cot_all_ref.at[b, at.e // 2]

    cot_line = Line(at, cot_line_block, sems[12:14])
    cot_gather = Gather(at, cot_block, sems[14:], sibling=False)
    outer = (at.z == 0) | (at.z == 3)
    cot_here.wait()

    @pl.when(outer)
    def _():
        cot_line.begin()


    pieces_arrive(1)
    weights.own(1)
    line.arrive(1)
    pieces_arrive(2)
    weights.own(2)
    pieces_arrive(3)
    weights.own(3)

    @pl.when(jnp.logical_not(outer))
    def _():
        line.arrive(2)

    weights.cross(0)
    weights.cross(1)

    @pl.when(jnp.logical_not(outer))
    def _():
        line.arrive(3)
        cot_line.begin()

    cot_gather.own(0)
    weights.diag(0)
    weights.cross(2)
    weights.diag(1)
    weights.cross(3)
    weights.diag(2)
    weights.diag(3)
    stores = [
        pltpu.make_async_copy(src, dst, store_sem.at[i])
        for i, (src, dst) in enumerate(
            (
                (normed_ref, normed_out),
                (w_cols_ref, w_cols_out),
                (raw_ref, raw_out),
                (prob_ref, prob_out),
                (mixed_ref, mixed_out),
            )
        )
    ]
    for k in range(4):
        for q in range(4):
            weights.ready(k, q)
    stores[1].start()
    sums = LineSum(at, rows_out, rows_in, sems[:2])

    def is_far(turn):
        return outer if turn == 0 else jnp.logical_not(outer)

    def project(turn):
        first = 2 * jnp.where(is_far(turn), 1 - at.half, at.half)
        both = pl.ds(pl.multiple_of(first * rows, pair), pair)
        step = 256
        for start in range(0, cols, step):
            lanes = slice(start, start + step)
            raw_ref[both, lanes] = jnp.dot(
                normed_ref[both, :], w_cols_ref[:, lanes], preferred_element_type=F32
            )

    gains = small_all_ref[0, 2:3, :] + small_all_ref[1, 2:3, :] + small_all_ref[2, 2:3, :] + small_all_ref[3, 2:3, :]
    q_gain, k_gain = gains[:, :width], gains[:, width : 2 * width]
    row_id = lax.broadcasted_iota(jnp.int32, (rows, rows), 0).astype(F32)
    lane_id = lax.broadcasted_iota(jnp.int32, (rows, rows), 1).astype(F32)

    def attention(turn):
        first = 2 * jnp.where(is_far(turn), 1 - at.half, at.half)
        both = pl.ds(pl.multiple_of(first * rows, pair), pair)
        heads_of(first)
        if turn == 1:

            @pl.when(outer)
            def _():
                cot_line.arrive(2)
                cot_gather.own(2)

            @pl.when(jnp.logical_not(outer))
            def _():
                cot_gather.cross(2)

        heads_of(first + 1)
        step = 512
        for start in range(0, model, step):
            lanes = slice(start, start + step)
            part = jnp.dot(mixed_ref[both, :], w_out_ref[:, lanes], preferred_element_type=F32)

            @pl.when(jnp.logical_not(is_far(turn)))
            def _():
                own_part[:, lanes] = jnp.where(at.z % 2 == 0, part[:rows], part[rows:])

            rows_out[first, :, lanes] = part[:rows].astype(BF)
            rows_out[first + 1, :, lanes] = part[rows:].astype(BF)

        @pl.when(is_far(turn))
        def _():
            sums.give_far()

        if turn == 1:
            sums.give_near(True)
            sums.give_near(False)

    def heads_of(b):
        here = pl.ds(pl.multiple_of(b * rows, rows), rows)
        segment = jnp.zeros((rows, rows), F32)
        lane_segment = jnp.zeros((rows, rows), F32)
        place = row_id
        end = jnp.zeros((1, 1), F32)
        for i in range(SEQ_SLOTS - 1):
            length = small_all_ref[b, 2:3, 2 * width + i : 2 * width + i + 1]
            end = end + length
            past = (row_id >= end).astype(F32)
            segment += past
            place -= past * length
            lane_segment += (lane_id >= end).astype(F32)
        allowed = (segment == lane_segment) & (lane_id <= row_id)
        named = (lane_id == place).astype(BF)

        def looked_up(first):
            total = jnp.zeros((rows, width), F32)
            for i in range(3):
                part = table_ref[(first + i) * width : (first + i + 1) * width]
                total += jnp.dot(named, part, preferred_element_type=F32)
            return total

        cosine, sine = looked_up(0), looked_up(3)
        cos_ref[here, :] = cosine
        sin_ref[here, :] = sine

        def low_of(v, gain):
            inverse = lax.rsqrt(jnp.mean(v * v, axis=-1, keepdims=True) + epsilon)
            scaled = v * inverse * gain
            return (scaled * cosine + swap(scaled) * sine).astype(BF)

        k_low = low_of(raw_ref[here, q_cols : q_cols + width], k_gain)
        v_low = raw_ref[here, q_cols + width : q_cols + 2 * width].astype(BF)
        for h in range(heads):
            lanes = slice(h * width, (h + 1) * width)
            q_low = low_of(raw_ref[here, lanes], q_gain)
            scores = jnp.where(allowed, dot(q_low, k_low, NT) * scale, masked_score)
            weight = jnp.exp(scores - jnp.max(scores, axis=-1, keepdims=True))
            prob = weight / jnp.sum(weight, axis=-1, keepdims=True)
            prob_ref[b * heads + h] = prob
            mixed_ref[here, lanes] = dot(prob.astype(BF), v_low, NN).astype(BF)

    @pl.when(outer)
    def _():
        line.arrive(2)
        line.arrive(3)

    project(0)
    cot_line.arrive(1)
    cot_gather.own(1)
    attention(0)

    @pl.when(jnp.logical_not(outer))
    def _():
        cot_line.arrive(2)
        cot_gather.own(2)

    cot_gather.cross(0)
    stores[0].start()
    project(1)
    stores[2].start()

    @pl.when(jnp.logical_not(outer))
    def _():
        cot_line.arrive(3)
        cot_gather.own(3)

    cot_gather.cross(1)
    attention(1)
    stores[3].start()
    stores[4].start()

    @pl.when(outer)
    def _():
        cot_line.arrive(3)
        cot_gather.own(3)
        cot_gather.cross(2)

    cot_gather.diag(0)
    cot_gather.diag(1)
    cot_gather.cross(3)
    sums.wait()
    middle = (
        tokens_ref[...].astype(F32)
        + own_part[...]
        + sums.total(pl.ds(0, rows))
    )
    middle_ref[...] = middle
    inverse = lax.rsqrt(jnp.mean(middle * middle, axis=-1, keepdims=True) + epsilon)
    for j in range(4):
        lanes = slice(j * quarter, (j + 1) * quarter)
        second_ref[:, lanes] = (middle[:, lanes] * inverse * small_all_ref[j, 1:2, :]).astype(BF)
    logits = dot(second_ref[:, :model], router_wide[...], NT)
    chosen = chosen_ref[...] > 0.0
    lane = lax.broadcasted_iota(jnp.int32, (rows, EXTRA), 1)
    top = jnp.max(jnp.where(chosen, logits, masked_score), axis=-1, keepdims=True)
    lifted = jnp.where(chosen, jnp.exp(logits - top), 0.0)
    share = lifted / jnp.sum(jnp.where(lane < experts_all, lifted, 0.0), axis=-1, keepdims=True)
    share_ref[...] = share
    high = share.astype(BF).astype(F32)
    second_ref[:, model:] = jnp.where(lane < experts_all, high, share - high).astype(BF)
    cot_gather.diag(2)
    cot_gather.diag(3)
    for copy in stores:
        copy.wait()
    for k in range(4):
        cot_gather.end(k)
        weights.end(k)
    line.end()
    cot_line.end()
    sums.end()
    for k in (1, 2, 3):
        for copy in small_copies(k):
            copy.wait_send()
        for copy in piece_copies(k):
            copy.wait_send()


def front_in_one(tokens, small, router, w_query, w_key, w_value, w_out, table, chosen, cotangent):
    rows, model = tokens.shape
    q_cols = w_query.shape[1] // 4
    cols = q_cols + 2 * HEAD_WIDTH
    heads = q_cols // HEAD_WIDTH
    experts_all = router.shape[0]
    vmem = pl.BlockSpec(memory_space=pltpu.VMEM)
    hbm = pl.BlockSpec(memory_space=pl.ANY)
    dma = pltpu.SemaphoreType.DMA
    shape = jax.ShapeDtypeStruct
    return pl.pallas_call(
        front_kernel,
        out_shape=(
            shape((rows, model + EXTRA), BF),
            shape((rows, model), F32),
            shape((rows, EXTRA), F32),
            shape((model, cols), BF),
            shape((4 * rows, model), BF),
            shape((4 * rows, cols), F32),
            shape((4 * heads, rows, rows), F32),
            shape((4 * rows, q_cols), BF),
            shape((4 * rows, HEAD_WIDTH), F32),
            shape((4 * rows, HEAD_WIDTH), F32),
            shape((4, 8, model // 4), F32),
            shape((4, experts_all, model // 4), BF),
            shape((4, 4, rows, model), BF),
        ),
        in_specs=[vmem, vmem, vmem, hbm, hbm, hbm, vmem, vmem, vmem, hbm],
        out_specs=(vmem,) * 3 + (hbm,) * 5 + (vmem,) * 4 + (hbm,),
        scratch_shapes=[
            pltpu.VMEM((model, cols), BF),
            pltpu.VMEM((4 * rows, model), BF),
            pltpu.VMEM((4 * rows, cols), F32),
            pltpu.VMEM((4 * heads, rows, rows), F32),
            pltpu.VMEM((4 * rows, q_cols), BF),
            pltpu.VMEM((rows, model), F32),
            pltpu.VMEM((EXTRA, model), BF),
            pltpu.VMEM((4, rows, model), BF),
            pltpu.VMEM((5, rows, model), BF),
            dma((3, 2)),
            dma((3, 2)),
            dma((3, 3)),
            dma((3, 3)),
            dma((3,)),
            dma,
            dma((5,)),
            *LineSum.semaphores(),
            *Gather.semaphores(),
            *Line.semaphores(),
            *Line.semaphores(),
            *Gather.semaphores(False),
        ],
        compiler_params=pltpu.CompilerParams(
            collective_id=2, has_side_effects=True, vmem_limit_bytes=VMEM_BYTES
        ),
        cost_estimate=pl.CostEstimate(
            flops=2 * 4 * rows * model * (cols + q_cols),
            bytes_accessed=64 * 1024 * 1024,
            transcendentals=4 * rows * cols,
        ),
    )(tokens, small, router, w_query, w_key, w_value, w_out, table, chosen, cotangent)


def per_device(
    tokens,
    lengths,
    routes,
    attn_gain,
    w_query,
    key_projection,
    value_projection,
    w_out,
    query_gain,
    key_gain,
    ffn_gain,
    w_router,
    w_gate,
    w_up,
    w_down,
    cotangent,
):
    ring = lax.axis_size("fsdp")
    groups = lax.axis_size("expert")
    plane_rank = lax.axis_index("expert")
    experts_all = w_router.shape[1]
    local_experts = w_gate.shape[0]
    units = w_gate.shape[2]
    wide = local_experts * units
    in_rows = MODEL_WIDTH // ring
    heads = QUERY_HEADS // ring
    kv = KEY_VALUE_HEADS // ring
    group_width = heads // kv
    q_cols = heads * HEAD_WIDTH
    kv_cols = kv * HEAD_WIDTH
    cols = q_cols + 2 * kv_cols
    piece_rows = in_rows // groups
    score_scale = HEAD_WIDTH ** (-0.5)
    both = ("expert", "fsdp")
    one_block = (groups, ring, experts_all) == (8, 4, 16)

    gate_w = w_gate.transpose(0, 2, 1).reshape(wide, MODEL_WIDTH)
    up_w = w_up.transpose(0, 2, 1).reshape(wide, MODEL_WIDTH)
    down_w = w_down.reshape(wide, MODEL_WIDTH)
    line_tokens = ring * DEVICE_TOKENS
    source = tokens.astype(F32)
    expert_ids = jnp.arange(experts_all, dtype=jnp.int32)
    chosen = jnp.any(routes[:, :, None] == expert_ids[None, None, :], axis=1)

    if one_block:
        here = lax.axis_index("fsdp") * (HEAD_WIDTH // ring)
        spread = lambda gain: lax.dynamic_update_slice_in_dim(
            jnp.zeros((HEAD_WIDTH,), F32), gain.astype(F32), here, 0
        )
        third = jnp.concatenate(
            [spread(query_gain), spread(key_gain), lengths.reshape(-1).astype(F32)]
        )
        small = jnp.stack(
            [
                attn_gain.astype(F32),
                ffn_gain.astype(F32),
                jnp.pad(third, (0, in_rows - third.shape[0])),
            ]
        )
        frequency = rope_base ** (-np.arange(0, HEAD_WIDTH, 2) / HEAD_WIDTH)
        angles = np.arange(HEAD_WIDTH)[:, None] * np.tile(frequency, 2)[None, :]
        sine_sign = np.where(np.arange(HEAD_WIDTH) < HEAD_WIDTH // 2, -1.0, 1.0)
        parts = []
        for exact in (np.cos(angles), np.sin(angles) * sine_sign):
            for _ in range(3):
                parts.append(exact.astype(ml_dtypes.bfloat16))
                exact = exact - parts[-1].astype(np.float64)
        wide_chosen = jnp.pad(
            jnp.concatenate([chosen, chosen], axis=1).astype(F32),
            ((0, 0), (0, EXTRA - 2 * experts_all)),
        )
        (
            second_wide,
            middle,
            share,
            w_cols,
            normed_all,
            raw,
            probabilities,
            mixed,
            cosine,
            sine_table,
            small_all,
            router_all,
            cot_all,
        ) = front_in_one(
            tokens,
            jnp.pad(small, ((0, 5), (0, 0))),
            w_router.T,
            w_query,
            key_projection,
            value_projection,
            w_out,
            jnp.asarray(np.concatenate(parts)),
            wide_chosen,
            cotangent,
        )
        cot_all = cot_all.reshape(-1, MODEL_WIDTH)
        attn_gain_f = small_all[:, 0].reshape(-1)
        attn_inverse = lax.rsqrt(jnp.mean(source * source, axis=-1, keepdims=True) + epsilon)
        attn_unit = source * attn_inverse
    else:
        small = jnp.concatenate(
            [
                attn_gain,
                ffn_gain,
                query_gain,
                key_gain,
                w_router.reshape(-1),
                lengths.reshape(-1).astype(BF),
            ]
        )
        small_all = lax.all_gather(small, "fsdp", axis=0, tiled=False)
        at = 0

        def take(count):
            nonlocal at
            part = small_all[:, at : at + count]
            at += count
            return part

        attn_gain_f = take(in_rows).reshape(-1).astype(F32)
        ffn_gain_f = take(in_rows).reshape(-1).astype(F32)
        query_gain_f = take(HEAD_WIDTH // ring).reshape(-1).astype(F32)
        key_gain_f = take(HEAD_WIDTH // ring).reshape(-1).astype(F32)
        router_all = take(in_rows * experts_all).reshape(MODEL_WIDTH, experts_all)
        lengths_all = take(SEQ_SLOTS).astype(jnp.int32)

        by_col = jnp.concatenate(
            [
                w_query.reshape(in_rows, ring, q_cols),
                key_projection.reshape(in_rows, ring, kv_cols),
                value_projection.reshape(in_rows, ring, kv_cols),
            ],
            axis=2,
        )
        piece = lax.dynamic_slice_in_dim(by_col, plane_rank * piece_rows, piece_rows, 0)
        piece = lax.all_to_all(
            piece.transpose(1, 0, 2), "fsdp", split_axis=0, concat_axis=0, tiled=True
        )
        w_cols = lax.all_gather(piece, "expert", axis=1, tiled=True).reshape(MODEL_WIDTH, cols)

        attn_inverse = lax.rsqrt(jnp.mean(source * source, axis=-1, keepdims=True) + epsilon)
        attn_unit = source * attn_inverse
        normed = (attn_unit * attn_gain_f).astype(BF)
        normed_all = lax.all_gather(normed, "fsdp", axis=0, tiled=True)
        raw = dot(normed_all, w_cols, NN)
        query_raw = raw[:, :q_cols].reshape(ring, DEVICE_TOKENS, kv, group_width, HEAD_WIDTH)
        key_raw = raw[:, q_cols : q_cols + kv_cols].reshape(ring, DEVICE_TOKENS, kv, HEAD_WIDTH)
        value_low = raw[:, q_cols + kv_cols :].astype(BF).reshape(ring, DEVICE_TOKENS, kv, HEAD_WIDTH)
        places, segment_ids = jax.vmap(lambda row: layout(row, DEVICE_TOKENS, SEQ_SLOTS))(lengths_all)
        cosine, sine_table = rope_tables(places, HEAD_WIDTH)
        cos_k, sin_k = cosine[:, :, None, :], sine_table[:, :, None, :]
        cos_q, sin_q = cosine[:, :, None, None, :], sine_table[:, :, None, None, :]
        query_inverse = lax.rsqrt(jnp.mean(query_raw * query_raw, axis=-1, keepdims=True) + epsilon)
        query_unit = query_raw * query_inverse
        query_low = rotate(query_unit * query_gain_f, cos_q, sin_q).astype(BF)
        key_inverse = lax.rsqrt(jnp.mean(key_raw * key_raw, axis=-1, keepdims=True) + epsilon)
        key_unit = key_raw * key_inverse
        key_low = rotate(key_unit * key_gain_f, cos_k, sin_k).astype(BF)
        row_ids = jnp.arange(DEVICE_TOKENS, dtype=jnp.int32)
        allowed = (segment_ids[:, :, None] == segment_ids[:, None, :]) & (
            row_ids[None, None, :] <= row_ids[None, :, None]
        )
        scores = (
            jnp.einsum("bqhgd,bkhd->bhgqk", query_low, key_low, preferred_element_type=F32)
            * score_scale
        )
        scores = jnp.where(allowed[:, None, None], scores, masked_score)
        weights = jnp.exp(scores - jnp.max(scores, axis=-1, keepdims=True))
        probabilities = weights / jnp.sum(weights, axis=-1, keepdims=True)
        prob_low = probabilities.astype(BF)
        mixed = (
            jnp.einsum("bhgqk,bkhd->bqhgd", prob_low, value_low, preferred_element_type=F32)
            .astype(BF)
            .reshape(line_tokens, q_cols)
        )
        branch = lax.psum_scatter(
            dot(mixed, w_out, NN).astype(BF), "fsdp", scatter_dimension=0, tiled=True
        ).astype(F32)
        middle = source + branch
        ffn_inverse = lax.rsqrt(jnp.mean(middle * middle, axis=-1, keepdims=True) + epsilon)
        ffn_unit = middle * ffn_inverse
        second = (ffn_unit * ffn_gain_f).astype(BF)

        logits = dot(second, router_all, NN)
        top = jnp.max(jnp.where(chosen, logits, -jnp.inf), axis=1, keepdims=True)
        lifted = jnp.where(chosen, jnp.exp(logits - top), 0.0)
        share = lifted / jnp.sum(lifted, axis=1, keepdims=True)

    def experts(second, share, cotangent):
        second_all = lax.all_gather(second, both, axis=0, tiled=True)
        share_all = lax.all_gather(share, both, axis=0, tiled=True)
        cot_all = lax.all_gather(cotangent, both, axis=0, tiled=True)
        first = plane_rank * local_experts
        own_share = lax.dynamic_slice_in_dim(share_all, first, local_experts, 1)
        share_wide = jnp.repeat(own_share, units, axis=1)
        gate_act = dot(second_all, gate_w, NT)
        up_act = dot(second_all, up_w, NT)
        back = dot(cot_all, down_w, NT)
        sigmoid_gate = jax.nn.sigmoid(gate_act)
        silu_gate = gate_act * sigmoid_gate
        hidden = silu_gate * up_act
        share_grad = jnp.sum((hidden * back).reshape(-1, local_experts, units), axis=2)
        hidden_low = (share_wide * hidden).astype(BF)
        hidden_grad = share_wide * back
        gate_grad = (
            hidden_grad * up_act * sigmoid_gate * (1.0 + gate_act * (1.0 - sigmoid_gate))
        ).astype(BF)
        up_grad = (hidden_grad * silu_gate).astype(BF)
        routed_part = dot(hidden_low, down_w, NN).astype(BF)
        second_part = (dot(gate_grad, gate_w, NN) + dot(up_grad, up_w, NN)).astype(BF)
        spread = jnp.zeros((share_grad.shape[0], experts_all), F32)
        spread = lax.dynamic_update_slice_in_dim(spread, share_grad, first, 1)
        second_grad = lax.psum_scatter(second_part, both, scatter_dimension=0, tiled=True)
        routed = lax.psum_scatter(routed_part, both, scatter_dimension=0, tiled=True)
        dshare = lax.psum_scatter(spread, both, scatter_dimension=0, tiled=True)
        return (
            (second_grad.astype(F32), routed.astype(F32), dshare),
            (
                dot(gate_grad, second_all, TN),
                dot(up_grad, second_all, TN),
                dot(hidden_low, cot_all, TN),
            ),
        )

    chunks = max(1, ring * groups // 32)
    if one_block:
        sums, *weight_grads, _ = experts_in_one(second_wide, cot_all, gate_w, up_w, down_w)
        weight_grads = [grad.astype(F32) for grad in weight_grads]
    elif chunks == 1:
        rows_out, weight_grads = experts(second, share, cotangent)
    else:
        def turn(total, rows):
            rows_out, grads = experts(*rows)
            return jax.tree.map(jnp.add, total, grads), rows_out

        start = (
            jnp.zeros((wide, MODEL_WIDTH), F32),
            jnp.zeros((wide, MODEL_WIDTH), F32),
            jnp.zeros((wide, MODEL_WIDTH), F32),
        )
        weight_grads, rows_out = lax.scan(
            turn,
            start,
            [v.reshape(chunks, -1, v.shape[1]) for v in (second, share, cotangent)],
        )
        rows_out = [v.reshape(-1, v.shape[2]) for v in rows_out]
    gate_wgrad, up_wgrad, down_wgrad = weight_grads
    grad_w_gate = gate_wgrad.reshape(local_experts, units, MODEL_WIDTH).transpose(0, 2, 1)
    grad_w_up = up_wgrad.reshape(local_experts, units, MODEL_WIDTH).transpose(0, 2, 1)
    grad_w_down = down_wgrad.reshape(local_experts, units, MODEL_WIDTH)
    if one_block:
        at_gain = experts_all
        part_width = HEAD_WIDTH // ring
        head_lane = np.arange(HEAD_WIDTH)
        place_of = head_lane // part_width * in_rows + head_lane % part_width
        placing = jnp.asarray(place_of[:, None] == np.arange(MODEL_WIDTH)[None, :], BF)
        normed_grad, block_out, middle_grad, out_sum, cols_sum = back_in_one(
            (
                middle,
                share,
                cotangent,
                router_all,
                small_all,
                cosine,
                sine_table,
                second_wide,
                placing,
            ),
            sums,
            (w_out, w_cols, mixed, normed_all, raw, probabilities),
        )
        tokens_grad = middle_grad + norm_back(normed_grad * attn_gain_f, attn_unit, attn_inverse)
        out_grad = out_sum.astype(F32)
        ends = [ring * n for n in (q_cols, q_cols + kv_cols, cols)]
        grad_w_query = cols_sum[:, : ends[0]].astype(F32)
        grad_w_key = cols_sum[:, ends[0] : ends[1]].astype(F32)
        grad_w_value = cols_sum[:, ends[1] : ends[2]].astype(F32)
        small_own = sum(
            cols_sum[:, ends[2] + j * EXTRA : ends[2] + (j + 1) * EXTRA].astype(F32)
            for j in range(ring)
        )
        own_grads = (
            small_own[:, at_gain + 1],
            small_own[:part_width, at_gain + 2],
            small_own[:part_width, at_gain + 3],
            small_own[:, at_gain],
            small_own[:, :experts_all],
        )
    else:
        second_grad, routed, dshare = rows_out
        block_out = (middle + routed).astype(BF)

        mean_grad = jnp.sum(share * dshare, axis=1, keepdims=True)
        logit_grad = (share * (dshare - mean_grad)).astype(BF)
        upstream = cotangent.astype(F32)
        second_grad = second_grad + dot(logit_grad, router_all, NT)
        middle_grad = upstream + norm_back(second_grad * ffn_gain_f, ffn_unit, ffn_inverse)
        router_grad = dot(second, logit_grad, TN)
        ffn_gain_grad = jnp.sum(second_grad * ffn_unit, axis=0)
        branch_all = lax.all_gather(middle_grad.astype(BF), "fsdp", axis=0, tiled=True)
        out_grad = lax.psum(dot(mixed, branch_all, TN).astype(BF), "expert").astype(F32)
        mixed_grad = dot(branch_all, w_out, NT).astype(BF)
        mixed_grad = mixed_grad.reshape(ring, DEVICE_TOKENS, kv, group_width, HEAD_WIDTH)
        value_grad = jnp.einsum("bhgqk,bqhgd->bkhd", prob_low, mixed_grad, preferred_element_type=F32)
        prob_grad = jnp.einsum("bqhgd,bkhd->bhgqk", mixed_grad, value_low, preferred_element_type=F32)
        score_grad = (
            probabilities * (prob_grad - jnp.sum(probabilities * prob_grad, axis=-1, keepdims=True))
        ).astype(BF)
        query_grad = (
            jnp.einsum("bhgqk,bkhd->bqhgd", score_grad, key_low, preferred_element_type=F32)
            * score_scale
        )
        key_grad = (
            jnp.einsum("bhgqk,bqhgd->bkhd", score_grad, query_low, preferred_element_type=F32)
            * score_scale
        )
        query_turned = unrotate(query_grad, cos_q, sin_q)
        query_gain_grad = jnp.sum(query_turned * query_unit, axis=(0, 1, 2, 3))
        query_back = norm_back(query_turned * query_gain_f, query_unit, query_inverse)
        key_turned = unrotate(key_grad, cos_k, sin_k)
        key_gain_grad = jnp.sum(key_turned * key_unit, axis=(0, 1, 2))
        key_back = norm_back(key_turned * key_gain_f, key_unit, key_inverse)
        raw_grad = jnp.concatenate(
            [
                query_back.astype(BF).reshape(line_tokens, q_cols),
                key_back.astype(BF).reshape(line_tokens, kv_cols),
                value_grad.astype(BF).reshape(line_tokens, kv_cols),
            ],
            axis=1,
        )
        cols_grad = dot(normed_all, raw_grad, TN).astype(BF)
        normed_part = dot(raw_grad, w_cols, NT).astype(BF)
        normed_grad = lax.psum_scatter(normed_part, "fsdp", scatter_dimension=0, tiled=True).astype(F32)
        attn_gain_grad = jnp.sum(normed_grad * attn_unit, axis=0)
        tokens_grad = middle_grad + norm_back(normed_grad * attn_gain_f, attn_unit, attn_inverse)

        own = lax.psum_scatter(
            cols_grad.reshape(ring, groups, piece_rows, cols), "expert", scatter_dimension=1, tiled=False
        )
        own = lax.all_to_all(own, "fsdp", split_axis=0, concat_axis=0, tiled=True)
        rows_grad = lax.all_gather(own, "expert", axis=1, tiled=True)
        rows_grad = rows_grad.transpose(1, 0, 2).astype(F32)
        grad_w_query = rows_grad[:, :, :q_cols].reshape(in_rows, QUERY_HEADS * HEAD_WIDTH)
        grad_w_key = rows_grad[:, :, q_cols : q_cols + kv_cols].reshape(in_rows, -1)
        grad_w_value = rows_grad[:, :, q_cols + kv_cols :].reshape(in_rows, -1)

        small_grad = jnp.concatenate(
            [
                attn_gain_grad.reshape(ring, -1),
                ffn_gain_grad.reshape(ring, -1),
                query_gain_grad.reshape(ring, -1),
                key_gain_grad.reshape(ring, -1),
                router_grad.reshape(ring, -1),
            ],
            axis=1,
        )
        small_own = lax.psum(small_grad, both)
        small_own = lax.dynamic_index_in_dim(small_own, lax.axis_index("fsdp"), 0, keepdims=False)
        a, b = in_rows, HEAD_WIDTH // ring
        own_grads = (
            small_own[:a],
            small_own[2 * a : 2 * a + b],
            small_own[2 * a + b : 2 * a + 2 * b],
            small_own[a : 2 * a],
            small_own[2 * a + 2 * b :].reshape(in_rows, experts_all),
        )
    return (
        block_out,
        tokens_grad,
        own_grads[0],
        grad_w_query,
        grad_w_key,
        grad_w_value,
        out_grad,
        own_grads[1],
        own_grads[2],
        own_grads[3],
        own_grads[4],
        grad_w_gate,
        grad_w_up,
        grad_w_down,
    )


def solution(mesh):
    rows = P(("expert", "fsdp"), None)
    return jax.shard_map(
        per_device,
        mesh=mesh,
        in_specs=(
            rows,
            rows,
            rows,
            P("fsdp"),
            P("fsdp", None),
            P("fsdp", None),
            P("fsdp", None),
            P("fsdp", None),
            P("fsdp"),
            P("fsdp"),
            P("fsdp"),
            P("fsdp", None),
            P("expert", None, "fsdp"),
            P("expert", None, "fsdp"),
            P("expert", "fsdp", None),
            rows,
        ),
        out_specs=(
            rows,
            rows,
            P("fsdp"),
            P("fsdp", None),
            P("fsdp", None),
            P("fsdp", None),
            P("fsdp", None),
            P("fsdp"),
            P("fsdp"),
            P("fsdp"),
            P("fsdp", None),
            P("expert", None, "fsdp"),
            P("expert", None, "fsdp"),
            P("expert", "fsdp", None),
        ),
        check_vma=False,
    )
```

```python
import jax
import jax.numpy as jnp
import ml_dtypes
import numpy as np
from jax import lax
from jax.experimental import pallas as pl
from jax.experimental.pallas import tpu as pltpu
from jax.sharding import PartitionSpec as P

MODEL_WIDTH = 2048
QUERY_HEADS = 32
KEY_VALUE_HEADS = 4
HEAD_WIDTH = 128
TOPK = 8
DEVICE_TOKENS = 128
SEQ_SLOTS = 4

epsilon = 1e-06
rope_base = 1000000.0
masked_score = -1e30
BF = jnp.bfloat16
F32 = jnp.float32


def layout(lengths_row, tok_count, slot_count):
    seq_ends = jnp.cumsum(lengths_row)
    starts = seq_ends - lengths_row
    places = jnp.arange(tok_count, dtype=jnp.int32)
    segment = jnp.sum((places[:, None] >= seq_ends[None, :]).astype(jnp.int32), axis=1)
    member = segment[:, None] == jnp.arange(slot_count, dtype=jnp.int32)[None, :]
    start_of = jnp.sum(jnp.where(member, starts[None, :], 0), axis=1)
    return (places - start_of, segment)


def rope_tables(places, head_size):
    frequency = rope_base ** (-jnp.arange(0, head_size, 2, dtype=jnp.float32) / head_size)
    angles = places.astype(jnp.float32)[..., None] * frequency
    angles = jnp.concatenate([angles, angles], axis=-1)
    return (jnp.cos(angles), jnp.sin(angles))


def rotate(values, cosine, sine_table):
    half_width = values.shape[-1] // 2
    turned = jnp.concatenate([-values[..., half_width:], values[..., :half_width]], axis=-1)
    return values * cosine + turned * sine_table


def unrotate(gradient, cosine, sine_table):
    scaled = gradient * sine_table
    half_width = gradient.shape[-1] // 2
    return gradient * cosine + jnp.concatenate(
        [scaled[..., half_width:], -scaled[..., :half_width]], axis=-1
    )


def norm_back(gradient, unit_value, inverse):
    return inverse * (
        gradient - unit_value * jnp.mean(gradient * unit_value, axis=-1, keepdims=True)
    )


def dot(a, b, dims):
    return lax.dot_general(a, b, (dims, ((), ())), preferred_element_type=F32)


NN = ((1,), (0,))
NT = ((1,), (1,))
TN = ((0,), (0,))
VMEM_BYTES = 63 * 1024 * 1024

MESH = pl.DeviceIdType.MESH
EXTRA = 128
DIAG, XCOL, YCOL, OWN = 0, 1, 2, 3


def remote(src, dst, send, recv, device):
    return pltpu.make_async_remote_copy(
        src_ref=src,
        dst_ref=dst,
        send_sem=send,
        recv_sem=recv,
        device_id=device,
        device_id_type=MESH,
    )


class Place:
    def __init__(self):
        e = lax.axis_index("expert")
        z = lax.axis_index("fsdp")
        self.e, self.z = e, z
        self.core = lax.rem(e, 2)
        self.x = lax.rem(lax.div(e, 2), 2)
        self.y = lax.div(e, 4)
        self.x_near = (e + 2 - 4 * self.x, z)
        self.y_near = (e + 4 - 8 * self.y, z)
        self.sibling = (e + 1 - 2 * self.core, z)
        self.diagonal = (1 - self.y) * 4 + (1 - self.x) * 2 + self.core
        self.partner = z + 1 - 2 * lax.rem(z, 2)
        self.half = lax.div(z, 2)

    def plane(self, k):
        far = jnp.where(self.half == 0, k, 3 - k)
        return jnp.where(k == 0, self.z, jnp.where(k == 1, self.partner, far))

    def turn_at(self, z_there):
        far = jnp.where(z_there < 2, self.z, 3 - self.z)
        return jnp.where(z_there == self.partner, 1, far)

    def column_base(self, q):
        x = self.x if q in (YCOL, OWN) else 1 - self.x
        y = self.y if q in (XCOL, OWN) else 1 - self.y
        return (y * 2 + x) * 2

    def own(self, q):
        return self.column_base(q) + self.core

    def everyone(self):
        return [self.x_near, self.y_near, self.sibling] + [(self.e, self.plane(k)) for k in (1, 2, 3)]


def when(condition):
    def run(body):
        if isinstance(condition, bool):
            if condition:
                body()
        else:
            pl.when(condition)(body)

    return run


def greet(devices):
    barrier = pltpu.get_barrier_semaphore()
    for device in devices:
        pl.semaphore_signal(barrier, inc=1, device_id=device, device_id_type=MESH)


def meet(devices, greeted=False):
    if not greeted:
        greet(devices)
    pl.semaphore_wait(pltpu.get_barrier_semaphore(), len(devices))


class Line:
    def __init__(self, at, block, sems):
        self.at, self.block = at, block
        self.send, self.recv = sems

    def up(self, b):
        block = self.block(b)
        return remote(
            block, block, self.send.at[0, b], self.recv.at[b], (self.at.e, self.at.z + 1)
        )

    def down(self, b):
        block = self.block(b)
        return remote(
            block, block, self.send.at[1, b], self.recv.at[b], (self.at.e, self.at.z - 1)
        )

    def begin(self):
        z = self.at.z

        @pl.when(z < 3)
        def _():
            self.up(z).start()

        @pl.when(z > 0)
        def _():
            self.down(z).start()

    def arrive(self, k):
        z = self.at.z
        b = self.at.plane(k)
        block = self.block(b)
        remote(block, block, self.send.at[0, b], self.recv.at[b], self.at.sibling).wait_recv()

        @pl.when((b < z) & (z < 3))
        def _():
            self.up(b).start()

        @pl.when((b > z) & (z > 0))
        def _():
            self.down(b).start()

    def end(self):
        z = self.at.z
        for b in range(4):

            @pl.when((b <= z) & (z < 3))
            def _():
                self.up(b).wait_send()

            @pl.when((b >= z) & (z > 0))
            def _():
                self.down(b).wait_send()

    @staticmethod
    def semaphores():
        return [pltpu.SemaphoreType.DMA((2, 4)), pltpu.SemaphoreType.DMA((4,))]


class LineSum:
    def __init__(self, at, part, came, sems):
        self.at, self.part, self.came = at, part, came
        self.send, self.recv = sems

    def arrival(self, slot):
        block = self.came.at[slot]
        return remote(block, block, self.send.at[0], self.recv.at[slot], self.at.sibling)

    def copy(self, t):
        z = self.at.z
        up = (t > z).astype(jnp.int32)
        there = z + 2 * up - 1
        slot = jnp.where((t == there) & (up == 0), 4, t)
        return remote(
            self.part.at[t], self.came.at[slot], self.send.at[t], self.recv.at[slot], (self.at.e, there)
        )

    def give(self, t):
        z = self.at.z

        @pl.when(((t > z) & (z > 0)) | ((t < z) & (z < 3)))
        def _():
            self.arrival(t).wait_recv()

            @pl.loop(0, self.part.shape[1] // 32)
            def _(i):
                here = pl.ds(pl.multiple_of(i * 32, 32), 32)
                self.part[t, here] = (
                    self.part[t, here].astype(F32) + self.came[t, here].astype(F32)
                ).astype(BF)

        self.copy(t).start()

    def give_far(self):
        half = self.at.half
        self.give(jnp.where(half == 0, 3, 0))
        self.give(jnp.where(half == 0, 2, 1))

    def give_near(self, early):
        z = self.at.z
        outer = (z == 0) | (z == 3)

        @pl.when(outer if early else jnp.logical_not(outer))
        def _():
            self.give(self.at.partner)

    def wait(self):
        z = self.at.z
        zero = jnp.zeros(self.came.shape[1:], BF)

        @pl.when(z > 0)
        def _():
            self.arrival(z).wait_recv()

        @pl.when(z == 0)
        def _():
            self.came[0] = zero

        @pl.when(z < 3)
        def _():
            self.arrival(4).wait_recv()

        @pl.when(z == 3)
        def _():
            self.came[4] = zero

    def total(self, here):
        return self.came[self.at.z, here].astype(F32) + self.came[4, here].astype(F32)

    def end(self):
        for t in range(4):

            @pl.when(t != self.at.z)
            def _():
                self.copy(t).wait_send()

    @staticmethod
    def semaphores():
        return [pltpu.SemaphoreType.DMA((4,)), pltpu.SemaphoreType.DMA((5,))]


class Gather:
    def __init__(self, at, block, sems, sibling=True):
        self.at, self.block, self.sibling = at, block, sibling
        (self.x_send, self.x_recv, self.y_send, self.y_recv) = sems[:4]
        self.half_send, self.half_recv = sems[4:6]
        if sibling:
            self.sib_send, self.sib_recv = sems[6:8]

    def to_x(self, k):
        block = self.block(k, OWN)
        return remote(block, block, self.x_send.at[k], self.x_recv.at[k], self.at.x_near)

    def to_y(self, k):
        block = self.block(k, OWN)
        return remote(block, block, self.y_send.at[k], self.y_recv.at[k], self.at.y_near)

    def on_y(self, k):
        block = self.block(k, XCOL, 0)
        sem = 2 * k
        return remote(block, block, self.half_send.at[sem], self.half_recv.at[sem], self.at.y_near)

    def on_x(self, k):
        block = self.block(k, YCOL, 1)
        sem = 2 * k + 1
        return remote(block, block, self.half_send.at[sem], self.half_recv.at[sem], self.at.x_near)

    def to_sib(self, k, q):
        block = self.block(k, q)
        sem = 4 * k + q
        return remote(block, block, self.sib_send.at[sem], self.sib_recv.at[sem], self.at.sibling)

    def share(self, k, q):
        if self.sibling:
            self.to_sib(k, q).start()

    def own(self, k):
        self.to_x(k).start()
        self.to_y(k).start()
        self.share(k, OWN)

    def cross(self, k, halves=True):
        self.to_x(k).wait_recv()
        if halves:
            self.on_y(k).start()
        self.share(k, XCOL)
        self.to_y(k).wait_recv()
        if halves:
            self.on_x(k).start()
        self.share(k, YCOL)

    def diag(self, k):
        self.on_y(k).wait_recv()
        self.on_x(k).wait_recv()
        self.share(k, DIAG)

    def ready(self, k, q):
        self.to_sib(k, q).wait_recv()

    def end(self, k, halves=True):
        self.to_x(k).wait_send()
        self.to_y(k).wait_send()
        if halves:
            self.on_x(k).wait_send()
            self.on_y(k).wait_send()
        for q in range(4) if self.sibling else ():
            self.to_sib(k, q).wait_send()

    @staticmethod
    def semaphores(sibling=True):
        dma = pltpu.SemaphoreType.DMA
        return [dma((4,))] * 4 + [dma((8,))] * 2 + [dma((16,))] * 2 * sibling


def expert_kernel(
    second_ref,
    cot_ref,
    gate_ref,
    up_ref,
    down_ref,
    sums_ref,
    gate_grad_ref,
    up_grad_ref,
    down_grad_ref,
    kept_ref,
    held,
    part,
    diag_a,
    diag_b,
    diag_z,
    x_whole,
    y_whole,
    z_part,
    pair_part,
    cot_tile,
    gate_up,
    down,
    acts,
    back,
    gate_tile,
    hidden_tile,
    kept_tile,
    grad_tile,
    widen,
    narrow,
    load_sem,
    gift_send,
    gift_recv,
    cot_sem,
    kept_sem,
    grad_sem,
    reload_sem,
    over_sem,
    red_send,
    red_recv,
    zr_send,
    zr_recv,
    pair_send,
    pair_recv,
    give_send,
    give_recv,
    give_ready,
    *sems,
):
    at = Place()
    rows = second_ref.shape[0]
    pair, quad = 2 * rows, 4 * rows
    total_rows, carried = held.shape
    model = cot_ref.shape[1]
    wide = down.shape[0]
    own_wide = wide // 2
    units = wide // 4
    half = rows // 2
    partner = (at.e, at.partner)
    experts_all = 16
    loads, gifts = [], []
    for i, (ref, held_weights, first) in enumerate(
        ((gate_ref, gate_up, 0), (up_ref, gate_up, wide), (down_ref, down, 0))
    ):
        here = pl.ds(pl.multiple_of(first + at.core * own_wide, own_wide), own_wide)
        loads.append(pltpu.make_async_copy(ref, held_weights.at[here], load_sem.at[i]))
        gifts.append(
            remote(ref, held_weights.at[here], gift_send.at[i], gift_recv.at[i], at.sibling)
        )
    for copy in loads:
        copy.start()

    def named(shape, unit_axis):
        unit = lax.broadcasted_iota(jnp.int32, shape, unit_axis)
        lane = lax.broadcasted_iota(jnp.int32, shape, 1 - unit_axis)
        expert = at.e // 2 * 4
        for i in (1, 2, 3):
            expert = expert + (unit >= i * units).astype(jnp.int32)
        return ((lane == expert) | (lane == expert + experts_all)).astype(F32).astype(BF)

    widen[...] = named((EXTRA, wide), 1)
    narrow[...] = named((wide, EXTRA), 0)
    meet(at.everyone())
    for copy in gifts:
        copy.start()

    def side_first(k, side):
        return (at.plane(k) * 4 + (at.y if side else 1 - at.y) * 2) * rows

    def side_rows(k, side):
        return pl.ds(pl.multiple_of(side_first(k, side), pair), pair)

    def block(k, q, i=None):
        first, count = (0, rows) if i is None else (i * half, half)
        first = (at.plane(k) * 4 + at.column_base(q) // 2) * rows + first
        return held.at[pl.ds(pl.multiple_of(first, half), count)]

    def line_block(b):
        first = (b * 4 + at.column_base(OWN) // 2) * rows
        return held.at[pl.ds(pl.multiple_of(first, rows), rows)]

    line = Line(at, line_block, sems[:2])
    gather = Gather(at, block, sems[2:], sibling=False)
    first_row = (at.z * 4 + at.column_base(OWN) // 2) * rows
    held[pl.ds(pl.multiple_of(first_row, rows), rows)] = second_ref[...]
    line.begin()
    gather.own(0)

    def over_z(k):
        there = block(k, DIAG)
        return remote(there, there, over_sem.at[0], over_sem.at[1], partner)

    def cot_copy(k, side):
        return pltpu.make_async_copy(cot_ref.at[side_rows(k, side)], cot_tile, cot_sem)

    def kept_copy(k, side):
        return pltpu.make_async_copy(kept_tile, kept_ref.at[:, side_rows(k, side)], kept_sem)

    def compute(r, k, side, following):
        here = side_rows(k, side)
        acts[...] = lax.dot_general(
            held[here, :model], gate_up[...], (NT, ((), ())), preferred_element_type=F32
        )
        cot_copy(k, side).wait()
        back[...] = lax.dot_general(
            cot_tile[...], down[...], (NT, ((), ())), preferred_element_type=F32
        )
        following()

        @when(not (isinstance(r, int) and r == 0 and side == 1))
        def _():
            kept_copy(k, side).wait()

        out_first = r * quad + side * pair
        for i in range(pair // rows):
            strip_rows = slice(i * rows, (i + 1) * rows)
            first = side_first(k, side) + i * rows
            share_rows = held[pl.ds(pl.multiple_of(first, rows), rows), model:]
            gate_act, up_act = acts[strip_rows, :wide], acts[strip_rows, wide:]
            raw_back = back[strip_rows]
            share = jnp.dot(share_rows, widen[...], preferred_element_type=F32)
            sigmoid = 1.0 / (1.0 + jnp.exp(-gate_act))
            silu = gate_act * sigmoid
            hidden = silu * up_act
            product = hidden * raw_back
            high = product.astype(BF)
            low = (product - high.astype(F32)).astype(BF)
            share_grad = jnp.dot(high, narrow[...], preferred_element_type=F32) + jnp.dot(
                low, narrow[...], preferred_element_type=F32
            )
            lane = lax.broadcasted_iota(jnp.int32, share_grad.shape, 1)
            rounded = share_grad.astype(BF).astype(F32)
            share_grad = jnp.where(lane < experts_all, rounded, share_grad - rounded)
            hidden_low = (share * hidden).astype(BF)
            hidden_grad = share * raw_back
            gate_grad = (
                hidden_grad * up_act * sigmoid * (1.0 + gate_act * (1.0 - sigmoid))
            ).astype(BF)
            up_grad = (hidden_grad * silu).astype(BF)
            gate_tile[strip_rows, :wide] = gate_grad
            gate_tile[strip_rows, wide:] = up_grad
            hidden_tile[strip_rows] = hidden_low
            kept_tile[:wide, strip_rows] = gate_grad.T
            kept_tile[wide : 2 * wide, strip_rows] = up_grad.T
            kept_tile[2 * wide :, strip_rows] = hidden_low.T
            out_rows = pl.ds(pl.multiple_of(out_first + i * rows, rows), rows)
            part[out_rows, 2 * model :] = share_grad.astype(BF)
        kept_copy(k, side).start()
        there = pl.ds(pl.multiple_of(out_first, pair), pair)
        step = 512
        for start in range(0, model, step):
            part[there, start : start + step] = jnp.dot(
                hidden_tile[...], down[:, start : start + step], preferred_element_type=F32
            ).astype(BF)
            part[there, model + start : model + start + step] = jnp.dot(
                gate_tile[...], gate_up[:, start : start + step], preferred_element_type=F32
            ).astype(BF)

    def part_row(r, q, first=0):
        x = at.x if q in (YCOL, OWN) else 1 - at.x
        return r * quad + (pair if q in (XCOL, OWN) else 0) + x * rows + first

    def part_rows(r, q, first, count):
        return pl.ds(pl.multiple_of(part_row(r, q, first), min(count, half)), count)

    def half_a(r):
        src = part.at[part_rows(r, DIAG, 0, half)]
        return remote(src, diag_a.at[r % 2], red_send.at[0, r], red_recv.at[0, r], at.y_near)

    def half_b(r):
        src = part.at[part_rows(r, DIAG, half, half)]
        return remote(src, diag_b.at[r % 2], red_send.at[1, r], red_recv.at[1, r], at.x_near)

    def x_copy(r):
        src = part.at[part_rows(r, XCOL, 0, rows)]
        return remote(src, x_whole.at[r % 2], red_send.at[2, r], red_recv.at[2, r], at.x_near)

    def y_copy(r):
        src = part.at[part_rows(r, YCOL, 0, rows)]
        return remote(src, y_whole.at[r % 2], red_send.at[3, r], red_recv.at[3, r], at.y_near)

    def diag_over():
        src = part.at[part_rows(0, DIAG, 0, rows)]
        return remote(src, diag_z, red_send.at[0, 0], red_recv.at[0, 0], partner)

    strip = 32

    def by_strips(count, body):
        @pl.loop(0, count // strip)
        def _(i):
            body(pl.multiple_of(i * strip, strip))

    def reduce_diag(r):
        @when(r == 3)
        def _():
            diag_over().wait_recv()

            def body(row):
                here = part_rows(r, DIAG, row, strip)
                part[here] = (
                    part[here].astype(F32) + diag_z[pl.ds(row, strip)].astype(F32)
                ).astype(BF)

            by_strips(rows, body)

        @when(r == 0)
        def _():
            diag_over().start()

        @when(r > 0)
        def _():
            half_a(r).start()
            half_b(r).start()

    def reduce_x(r):
        @when(r > 0)
        def _():
            half_a(r).wait_recv()

            def body(row):
                here = part_rows(r, XCOL, row, strip)
                part[here] = (
                    part[here].astype(F32) + diag_a[r % 2, pl.ds(row, strip)].astype(F32)
                ).astype(BF)

            by_strips(half, body)

        x_copy(r).start()

    def reduce_y(r):
        @when(r > 0)
        def _():
            half_b(r).wait_recv()

            def body(row):
                here = part_rows(r, YCOL, half + row, strip)
                part[here] = (
                    part[here].astype(F32) + diag_b[r % 2, pl.ds(row, strip)].astype(F32)
                ).astype(BF)

            by_strips(half, body)

        y_copy(r).start()

    inner = (at.z == 1) | (at.z == 2)

    def near_copy():
        src = part.at[part_rows(0, OWN, 0, rows)]
        return remote(src, z_part.at[0], zr_send.at[0], zr_recv.at[0], partner)

    def pair_copy(r):
        block = pair_part.at[r - 1]
        return remote(block, block, pair_send.at[r - 1], pair_recv.at[r - 1], partner)

    def far_copy(r):
        there = at.plane(r + 1)
        return remote(
            pair_part.at[r - 1], z_part.at[1], zr_send.at[r], zr_recv.at[1], (at.e, there)
        )

    def pass_on(r):
        @pl.when(inner)
        def _():
            pair_copy(r).wait_recv()

            def body(row):
                here = pl.ds(row, strip)
                pair_part[r - 1, here] = (
                    pair_part[r - 1, here].astype(F32)
                    + part[part_rows(r, OWN, row, strip)].astype(F32)
                ).astype(BF)

            by_strips(rows, body)
            far_copy(r).start()

    def reduce_own(r):
        x_copy(r).wait_recv()
        y_copy(r).wait_recv()

        def total(row):
            here = pl.ds(row, strip)
            return (
                part[part_rows(r, OWN, row, strip)].astype(F32)
                + x_whole[r % 2, here].astype(F32)
                + y_whole[r % 2, here].astype(F32)
            )

        @when(r == 3)
        def _():
            near_copy().wait_recv()
            block = z_part.at[1]
            remote(block, block, zr_send.at[0], zr_recv.at[1], at.sibling).wait_recv()

            def body(row):
                here = pl.ds(row, strip)
                sums_ref[here] = total(row) + (
                    z_part[0, here].astype(F32) + z_part[1, here].astype(F32)
                )

            by_strips(rows, body)

        def keep(row):
            part[part_rows(r, OWN, row, strip)] = total(row).astype(BF)

        def lay_out(row):
            pair_part[r - 1, pl.ds(row, strip)] = total(row).astype(BF)

        @when(r == 0)
        def _():
            by_strips(rows, keep)
            near_copy().start()

        @when(between(r, 1, 2))
        def _():
            @pl.when(inner)
            def _():
                by_strips(rows, keep)

            @pl.when(jnp.logical_not(inner))
            def _():
                by_strips(rows, lay_out)
                pair_copy(r).start()

    def far_rows(k):
        line.arrive(k)
        gather.own(k)

    cot_copy(1, 1).start()
    line.arrive(1)
    gather.own(1)

    @pl.when(inner)
    def _():
        far_rows(2)

    gather.cross(0)
    gather.cross(1, halves=False)

    @pl.when(inner)
    def _():
        far_rows(3)

    for copy in loads + gifts:
        copy.wait()
    compute(0, 1, 1, lambda: cot_copy(1, 0).start())
    reduce_x(0)
    gather.diag(0)
    over_z(0).start()

    @pl.when(jnp.logical_not(inner))
    def _():
        far_rows(2)

    over_z(1).wait_recv()
    compute(0, 1, 0, lambda: cot_copy(2, 0).start())
    reduce_y(0)
    reduce_diag(0)

    @pl.when(jnp.logical_not(inner))
    def _():
        far_rows(3)

    gather.cross(2)
    gather.diag(2)
    compute(1, 2, 0, lambda: cot_copy(2, 1).start())
    reduce_diag(1)
    gather.cross(3)

    @pl.loop(1, 3)
    def _(r):
        k, later = r + 1, lax.rem(r + 2, 4)
        compute(r, k, 1, lambda: cot_copy(later, 0).start())
        reduce_own(r - 1)

        @pl.when(r == 1)
        def _():
            gather.diag(3)

        compute(r + 1, later, 0, lambda: cot_copy(later, 1).start())
        reduce_x(r)
        reduce_y(r)

        @pl.when(r == 2)
        def _():
            pass_on(1)

        reduce_diag(r + 1)

    compute(3, 0, 1, lambda: None)

    line.end()
    over_z(0).wait_send()
    diag_over().wait_send()
    near_copy().wait_send()
    x_copy(0).wait_send()
    y_copy(0).wait_send()
    for copy in (half_a(1), half_b(1), x_copy(1), y_copy(1)):
        copy.wait_send()
    pl.semaphore_signal(give_ready, inc=1, device_id=at.sibling, device_id_type=MESH)
    for k in range(4):
        gather.end(k, halves=k != 1)
    kept_copy(0, 1).wait()
    turned = [
        pltpu.make_async_copy(kept_ref.at[pl.ds(0, 2 * wide)], gate_up, load_sem.at[0]),
        pltpu.make_async_copy(kept_ref.at[pl.ds(2 * wide, wide)], down, load_sem.at[1]),
    ]
    for copy in turned:
        copy.start()
    step = 256
    chunks = model // step
    mine, theirs = at.core * own_wide, (1 - at.core) * own_wide

    def lanes_of(n):
        return pl.ds(pl.multiple_of(n * step, step), step)

    def turned_rows(first):
        return pl.ds(pl.multiple_of(first, own_wide), own_wide)

    def given(i, first, size):
        return part.at[pl.ds(0, own_wide), pl.ds(pl.multiple_of(i * model + first, step), size)]

    def taken(i, first, size):
        return part.at[pl.ds(quad, own_wide), pl.ds(pl.multiple_of(i * model + first, step), size)]

    def give_copies(n):
        first, size = n % 2 * (model // 2), model // 2
        return [
            remote(
                given(i, first, size),
                taken(i, first, size),
                give_send.at[n, i],
                give_recv.at[n, i],
                at.sibling,
            )
            for i in ((0, 1) if n < 2 else (0,))
        ]

    def gate_out(n):
        slot = lax.rem(n, 2)
        return [
            pltpu.make_async_copy(
                grad_tile.at[slot, pl.ds(i * own_wide, own_wide)],
                ref.at[:, lanes_of(n)],
                grad_sem.at[slot, i],
            )
            for i, ref in enumerate((gate_grad_ref, up_grad_ref))
        ]

    def down_out(n):
        slot = lax.rem(n, 2)
        return pltpu.make_async_copy(
            grad_tile.at[slot, pl.ds(0, own_wide)],
            down_grad_ref.at[:, lanes_of(n)],
            grad_sem.at[slot, 0],
        )

    def reload(n):
        return pltpu.make_async_copy(
            cot_ref.at[:, lanes_of(n)], held.at[:, lanes_of(n)], reload_sem.at[n]
        )

    def gate_up_chunk(first, i, n):
        return jnp.dot(
            gate_up[turned_rows(i * wide + first)],
            held[:, lanes_of(n)],
            preferred_element_type=F32,
        )

    def down_chunk(first, n):
        return jnp.dot(
            down[turned_rows(first)], held[:, lanes_of(n)], preferred_element_type=F32
        )

    def in_half(n, body):
        half_chunks = chunks // 2
        pl.loop(n % 2 * half_chunks, (n % 2 + 1) * half_chunks)(body)

    for copy in turned:
        copy.wait()
    for part_of in (0, 1):

        def give_gate_up(n):
            for i in (0, 1):
                given(i, n * step, step)[...] = gate_up_chunk(theirs, i, n).astype(BF)

        in_half(part_of, give_gate_up)
        if part_of == 0:
            pl.semaphore_wait(give_ready, 1)
        for copy in give_copies(part_of):
            copy.start()

    reduce_own(2)
    for part_of in (0, 1):
        for copy in give_copies(part_of):
            copy.wait_recv()

        def own_gate_up(n):
            @pl.when(n >= 2)
            def _():
                for copy in gate_out(n):
                    copy.wait()

            for i in (0, 1):
                grad_tile[lax.rem(n, 2), i * own_wide : (i + 1) * own_wide] = (
                    gate_up_chunk(mine, i, n) + taken(i, n * step, step)[...].astype(F32)
                ).astype(BF)
            for copy in gate_out(n):
                copy.start()
            reload(n).start()

        in_half(part_of, own_gate_up)

    pl.semaphore_signal(give_ready, inc=1, device_id=at.sibling, device_id_type=MESH)
    reduce_x(3)
    reduce_y(3)
    pass_on(2)
    for part_of in (0, 1):
        for copy in give_copies(part_of):
            copy.wait_send()
    for part_of in (2, 3):

        def give_down(n):
            reload(n).wait()
            given(0, n * step, step)[...] = down_chunk(theirs, n).astype(BF)

        in_half(part_of, give_down)
        if part_of == 2:
            pl.semaphore_wait(give_ready, 1)
        for copy in give_copies(part_of):
            copy.start()

    for n in (0, 1):
        for copy in gate_out(n):
            copy.wait()
    for part_of in (2, 3):
        for copy in give_copies(part_of):
            copy.wait_recv()

        def own_down(n):
            @pl.when(n >= 2)
            def _():
                down_out(n).wait()

            grad_tile[lax.rem(n, 2), :own_wide] = (
                down_chunk(mine, n) + taken(0, n * step, step)[...].astype(F32)
            ).astype(BF)
            down_out(n).start()

        in_half(part_of, own_down)

    reduce_own(3)
    for n in (0, 1):
        down_out(n).wait()

    for n in (2, 3):
        for copy in give_copies(n):
            copy.wait_send()
    for r in (2, 3):
        for copy in (half_a(r), half_b(r), x_copy(r), y_copy(r)):
            copy.wait_send()
    for r in (1, 2):

        @pl.when(inner)
        def _():
            far_copy(r).wait_send()

        @pl.when(jnp.logical_not(inner))
        def _():
            pair_copy(r).wait_send()


def experts_in_one(second_wide, cot_all, gate, up, down):
    rows, carried = second_wide.shape
    total_rows, model = cot_all.shape
    wide = 2 * down.shape[0]
    pair, half = 2 * rows, rows // 2
    both = 2 * model + EXTRA
    vmem = pl.BlockSpec(memory_space=pltpu.VMEM)
    hbm = pl.BlockSpec(memory_space=pl.ANY)
    dma = pltpu.SemaphoreType.DMA
    shape = jax.ShapeDtypeStruct
    return pl.pallas_call(
        expert_kernel,
        out_shape=(
            shape((rows, both), F32),
            shape((wide // 2, model), BF),
            shape((wide // 2, model), BF),
            shape((wide // 2, model), BF),
            shape((3 * wide, total_rows), BF),
        ),
        in_specs=[vmem, hbm, hbm, hbm, hbm],
        out_specs=(vmem, hbm, hbm, hbm, hbm),
        scratch_shapes=[
            pltpu.VMEM((total_rows, carried), BF),
            pltpu.VMEM((16 * rows, both), BF),
            pltpu.VMEM((2, half, both), BF),
            pltpu.VMEM((2, half, both), BF),
            pltpu.VMEM((rows, both), BF),
            pltpu.VMEM((2, rows, both), BF),
            pltpu.VMEM((2, rows, both), BF),
            pltpu.VMEM((2, rows, both), BF),
            pltpu.VMEM((2, rows, both), BF),
            pltpu.VMEM((pair, model), BF),
            pltpu.VMEM((2 * wide, model), BF),
            pltpu.VMEM((wide, model), BF),
            pltpu.VMEM((pair, 2 * wide), F32),
            pltpu.VMEM((pair, wide), F32),
            pltpu.VMEM((pair, 2 * wide), BF),
            pltpu.VMEM((pair, wide), BF),
            pltpu.VMEM((3 * wide, pair), BF),
            pltpu.VMEM((2, wide, 256), BF),
            pltpu.VMEM((EXTRA, wide), BF),
            pltpu.VMEM((wide, EXTRA), BF),
            dma((3,)),
            dma((3,)),
            dma((3,)),
            dma,
            dma,
            dma((2, 2)),
            dma((model // 256,)),
            dma((2,)),
            dma((4, 4)),
            dma((4, 4)),
            dma((3,)),
            dma((2,)),
            dma((2,)),
            dma((2,)),
            dma((4, 2)),
            dma((4, 2)),
            pltpu.SemaphoreType.REGULAR,
            *Line.semaphores(),
            *Gather.semaphores(False),
        ],
        compiler_params=pltpu.CompilerParams(
            collective_id=0, has_side_effects=True, vmem_limit_bytes=VMEM_BYTES
        ),
        cost_estimate=pl.CostEstimate(
            flops=2 * total_rows * model * wide * 9,
            bytes_accessed=8 * total_rows * model,
            transcendentals=total_rows * wide,
        ),
    )(second_wide, cot_all, gate, up, down)


def between(r, low, high):
    if isinstance(r, int):
        return low <= r <= high
    return (r >= low) & (r <= high)


class Tree:
    def __init__(self, at, refs, sems):
        (self.part, self.from_sib, self.diag_sum, self.x_sum, self.y_sum) = refs[:5]
        (self.diag_a, self.diag_b, self.x_whole, self.y_whole) = refs[5:]
        self.part_send, self.part_recv, self.send, self.recv = sems
        self.at = at
        self.rows = self.diag_sum.shape[0]
        self.half = self.rows // 2
        self.strip = 32

    def part_copy(self, q):
        return remote(
            self.part.at[q, 1 - self.at.core],
            self.from_sib.at[q],
            self.part_send.at[q],
            self.part_recv.at[q],
            self.at.sibling,
        )

    def half_a(self):
        there = self.diag_sum.at[pl.ds(0, self.half)]
        return remote(there, self.diag_a, self.send.at[0], self.recv.at[0], self.at.y_near)

    def half_b(self):
        there = self.diag_sum.at[pl.ds(self.half, self.half)]
        return remote(there, self.diag_b, self.send.at[1], self.recv.at[1], self.at.x_near)

    def x_copy(self):
        return remote(self.x_sum, self.x_whole, self.send.at[2], self.recv.at[2], self.at.x_near)

    def y_copy(self):
        return remote(self.y_sum, self.y_whole, self.send.at[3], self.recv.at[3], self.at.y_near)

    def strips(self, first, count, body):
        strip = self.strip

        @pl.loop(first // strip, (first + count) // strip)
        def _(i):
            body(pl.ds(pl.multiple_of(i * strip, strip), strip), i)

    def chip_sum(self, q, here):
        return self.part[q, self.at.core, here].astype(F32) + self.from_sib[q, here].astype(F32)

    def do_diag(self):
        self.part_copy(DIAG).wait_recv()

        def body(here, i):
            self.diag_sum[here] = self.chip_sum(DIAG, here).astype(BF)

        self.strips(0, self.rows, body)
        self.half_a().start()
        self.half_b().start()

    def do_x(self):
        self.part_copy(XCOL).wait_recv()
        self.half_a().wait_recv()

        def with_half(here, i):
            self.x_sum[here] = (
                self.chip_sum(XCOL, here) + self.diag_a[here].astype(F32)
            ).astype(BF)

        def alone(here, i):
            self.x_sum[here] = self.chip_sum(XCOL, here).astype(BF)

        self.strips(0, self.half, with_half)
        self.strips(self.half, self.half, alone)
        self.x_copy().start()

    def do_y(self):
        self.part_copy(YCOL).wait_recv()
        self.half_b().wait_recv()

        def alone(here, i):
            self.y_sum[here] = self.chip_sum(YCOL, here).astype(BF)

        def with_half(here, i):
            low = pl.ds(pl.multiple_of(i * self.strip - self.half, self.strip), self.strip)
            self.y_sum[here] = (self.chip_sum(YCOL, here) + self.diag_b[low].astype(F32)).astype(BF)

        self.strips(0, self.half, alone)
        self.strips(self.half, self.half, with_half)
        self.y_copy().start()

    def do_own(self, result):
        self.part_copy(OWN).wait_recv()
        self.x_copy().wait_recv()
        self.y_copy().wait_recv()

        def body(here, i):
            result[here] = (
                self.chip_sum(OWN, here)
                + self.x_whole[here].astype(F32)
                + self.y_whole[here].astype(F32)
            ).astype(BF)

        self.strips(0, self.rows, body)

    def drain(self):
        for q in range(4):
            self.part_copy(q).wait_send()
        for copy in (self.half_a(), self.half_b(), self.x_copy(), self.y_copy()):
            copy.wait_send()

    @staticmethod
    def buffers(rows, width):
        piece = pltpu.VMEM((rows, width), BF)
        half = pltpu.VMEM((rows // 2, width), BF)
        return [
            pltpu.VMEM((4, 2, rows, width), BF),
            pltpu.VMEM((4, rows, width), BF),
            piece,
            piece,
            piece,
            half,
            half,
            piece,
            piece,
        ]

    @staticmethod
    def semaphores():
        return [pltpu.SemaphoreType.DMA((4,))] * 4


class Spread:
    def __init__(self, at, own, out, sems, first=0):
        self.at, self.own, self.out, self.first = at, own, out, first
        self.send, self.recv, self.local = sems
        self.rows = own.shape[0]
        self.stride = out.shape[0] // 8
        self.e_x, self.e_y, self.e_d = at.x_near[0], at.y_near[0], at.diagonal

    def place(self, slot, first=0, rows=None):
        row = slot * self.stride + self.first + first
        rows = rows or self.rows
        return self.out.at[pl.ds(pl.multiple_of(row, rows), rows)]

    def to(self, src, slot, device, sem):
        return remote(src, self.place(slot), self.send.at[sem], self.recv.at[sem], device)

    def own_copies(self):
        e = self.at.e
        return (
            self.to(self.own, e, self.at.x_near, 0),
            self.to(self.own, e, self.at.y_near, 1),
            self.to(self.own, e, self.at.sibling, 2),
        )

    def here(self):
        return pltpu.make_async_copy(self.own, self.place(self.at.e), self.local)

    def half_copy(self, slot, first, device, sem):
        there = self.place(slot, first, self.rows // 2)
        return remote(there, there, self.send.at[sem], self.recv.at[sem], device)

    def cross_copies(self):
        return (
            self.half_copy(self.e_x, 0, self.at.y_near, 3),
            self.half_copy(self.e_y, self.rows // 2, self.at.x_near, 4),
            self.to(self.place(self.e_x), self.e_x, self.at.sibling, 5),
            self.to(self.place(self.e_y), self.e_y, self.at.sibling, 6),
        )

    def diag_copy(self):
        return self.to(self.place(self.e_d), self.e_d, self.at.sibling, 7)

    def begin(self):
        for copy in self.own_copies():
            copy.start()
        self.here().start()

    def cross(self):
        x, y, s = self.own_copies()
        x.wait_recv()
        y.wait_recv()
        for copy in self.cross_copies():
            copy.start()
        s.wait_recv()

    def diag(self):
        a, b, s, t = self.cross_copies()
        a.wait_recv()
        b.wait_recv()
        self.diag_copy().start()
        s.wait_recv()
        t.wait_recv()

    def end(self):
        self.diag_copy().wait()
        for copy in self.own_copies() + self.cross_copies():
            copy.wait_send()
        self.here().wait()

    @staticmethod
    def semaphores():
        dma = pltpu.SemaphoreType.DMA
        return [dma((8,)), dma((8,)), dma]


def swap(v):
    return pltpu.roll(v, v.shape[-1] // 2, v.ndim - 1)


def fold(v):
    return jnp.sum(v.reshape(v.shape[0] // 8, 8, v.shape[1]), axis=0)


def split_rows(v):
    high = v.astype(BF)
    return jnp.concatenate([v, v - high.astype(F32)], axis=0).astype(BF)


def back_kernel(
    middle_ref,
    share_ref,
    cot_ref,
    router_ref,
    small_ref,
    cos_ref,
    sin_ref,
    second_ref,
    place_ref,
    sums_ref,
    w_out_ref,
    w_cols_ref,
    mixed_ref,
    normed_ref,
    raw_ref,
    prob_ref,
    dnormed_ref,
    block_out_ref,
    middle_grad_ref,
    out_grad_ref,
    cols_grad_ref,
    w_out_held,
    w_cols_held,
    mixed_held,
    normed_held,
    raw_held,
    prob_held,
    held,
    raw_grad,
    left,
    right,
    share_sum,
    router_wide,
    rows_out,
    rows_in,
    gain_total,
    head_total,
    out_total,
    *rest,
):
    at = Place()
    rows, model = middle_ref.shape
    quarter = model // 4
    experts_all = router_ref.shape[1]
    own_part = dnormed_ref
    pair = 2 * rows
    width = HEAD_WIDTH
    heads = w_out_ref.shape[0] // width
    q_cols = heads * width
    cols = w_cols_ref.shape[1]
    count = model // 4 // 8
    scale = HEAD_WIDTH ** (-0.5)
    rest = list(rest)

    def grab(count):
        got, rest[:] = rest[:count], rest[count:]
        return got

    cols_totals, cols_alls = grab(2), grab(2)
    out_tree = Tree(at, grab(9), grab(4))
    cols_trees = [Tree(at, grab(9), grab(4)) for _ in (0, 1)]
    out_spread = Spread(at, out_total, out_grad_ref, grab(3))
    cols_spreads = [
        Spread(at, cols_alls[i], cols_grad_ref, grab(3), i * (count // 2)) for i in (0, 1)
    ]

    def line_block(b):
        return held.at[pl.ds(pl.multiple_of(b * rows, rows), rows)]

    line = Line(at, line_block, grab(2))
    sums = LineSum(at, rows_out, rows_in, grab(2))
    outer = (at.z == 0) | (at.z == 3)
    ex_send, ex_recv, ex_local, load_sem, sum_sem = grab(5)
    loads = [
        pltpu.make_async_copy(src, dst, load_sem.at[i])
        for i, (src, dst) in enumerate(
            (
                (w_out_ref, w_out_held),
                (raw_ref, raw_held),
                (w_cols_ref, w_cols_held),
                (normed_ref, normed_held),
                (prob_ref, prob_held),
                (mixed_ref, mixed_held),
            )
        )
    ]

    def sum_copy(j):
        lanes = pl.ds(pl.multiple_of(j * EXTRA, EXTRA), EXTRA)
        return pltpu.make_async_copy(sums_ref.at[:, lanes], prob_held.at[j], sum_sem.at[0])

    greet(at.everyone())
    columns = 2 * model // EXTRA
    share_copy = pltpu.make_async_copy(
        sums_ref.at[:, pl.ds(2 * model, EXTRA)], share_sum, sum_sem.at[1]
    )
    share_copy.start()

    @pl.loop(0, columns)
    def _(j):
        sum_copy(j).start()

    for copy in loads[:4]:
        copy.start()

    row_id = lax.broadcasted_iota(jnp.int32, right.shape, 0)
    lane_id = lax.broadcasted_iota(jnp.int32, right.shape, 1)
    chosen = (lane_id == experts_all) & (row_id >= rows) & (row_id < 2 * rows)
    for i in (0, 1, 2):
        first = 2 * rows + 16 * i
        chosen = chosen | (
            (lane_id == experts_all + 1 + i) & (row_id >= first) & (row_id < first + 16)
        )
    right[...] = chosen.astype(F32).astype(BF)
    router_wide[...] = jnp.zeros_like(router_wide)
    left[pl.ds(0, rows)] = second_ref[:, :model]
    left[pl.ds(2 * rows, rows)] = jnp.zeros((rows, model), BF)
    lane = lax.broadcasted_iota(jnp.int32, (rows, EXTRA), 1)
    share = share_ref[...]
    share_copy.wait()
    dshare = share_sum[...]
    dshare = dshare + pltpu.roll(dshare, EXTRA - experts_all, 1)
    weighed = jnp.where(lane < experts_all, share * dshare, 0.0)
    mean_share = jnp.sum(weighed, axis=-1, keepdims=True)
    logit_grad = jnp.where(lane < experts_all, share * (dshare - mean_share), 0.0).astype(BF)
    right[pl.ds(0, rows)] = logit_grad
    middle = middle_ref[...]
    inverse = lax.rsqrt(jnp.mean(middle * middle, axis=-1, keepdims=True) + epsilon)
    mean = jnp.zeros((rows, 1), F32)

    @pl.loop(0, columns)
    def _(j):
        sum_copy(j).wait()

    for j in range(4):
        router_wide[:experts_all, j * quarter : (j + 1) * quarter] = router_ref[j]
    for j in range(model // EXTRA):
        lanes = slice(j * EXTRA, (j + 1) * EXTRA)
        block_out_ref[:, lanes] = (middle[:, lanes] + prob_held[j]).astype(BF)
        second_grad = prob_held[model // EXTRA + j] + dot(logit_grad, router_wide[:, lanes], NN)
        unit = middle[:, lanes] * inverse
        left[rows : 2 * rows, lanes] = (second_grad * unit).astype(BF)
        of = j * EXTRA % quarter
        scaled = second_grad * small_ref[j * EXTRA // quarter, 1:2, of : of + EXTRA]
        middle_grad_ref[:, lanes] = scaled
        mean += jnp.sum(scaled * unit, axis=-1, keepdims=True)
    loads[4].start()
    loads[5].start()
    mean = mean / model
    middle_grad = cot_ref[...].astype(F32) + inverse * (
        middle_grad_ref[...] - middle * inverse * mean
    )
    middle_grad_ref[...] = middle_grad
    head_gains = small_ref[0, 2:3, :] + small_ref[1, 2:3, :]
    head_gains += small_ref[2, 2:3, :] + small_ref[3, 2:3, :]

    held[pl.ds(pl.multiple_of(at.z * rows, rows), rows)] = middle_grad.astype(BF)
    meet(at.everyone(), greeted=True)
    line.begin()
    gain_total[...] = jnp.zeros_like(gain_total)
    head_total[...] = jnp.zeros_like(head_total)

    def attention(far):
        first = 2 * (1 - at.half if far else at.half)
        both = pl.ds(pl.multiple_of(first * rows, pair), pair)
        mixed_grads = lax.dot_general(
            held[both, :], w_out_held[...], (NT, ((), ())), preferred_element_type=F32
        ).astype(BF)
        for i in (0, 1):
            heads_back(first + i, mixed_grads[i * rows : (i + 1) * rows])
            if not far and i == 0:

                @pl.when(jnp.logical_not(outer))
                def _():
                    line.arrive(3)

            if far and i == 0:
                out_tree.do_x()
                out_tree.do_y()
        step = 512
        for start in range(0, model, step):
            lanes = slice(start, start + step)
            part = lax.dot_general(
                raw_grad[both, :],
                w_cols_held[start : start + step, :],
                (NT, ((), ())),
                preferred_element_type=F32,
            )
            gain_total[:, lanes] += fold(part * normed_held[both, lanes].astype(F32))
            if not far:
                own_part[:, lanes] = jnp.where(at.z % 2 == 0, part[:rows], part[rows:])
            rows_out[first, :, lanes] = part[:rows].astype(BF)
            rows_out[first + 1, :, lanes] = part[rows:].astype(BF)
        if not far:
            sums.give_near(True)
        else:

            @pl.when(outer)
            def _():
                sums.give_far()

    def heads_back(b, mixed_grad):
        here = pl.ds(pl.multiple_of(b * rows, rows), rows)
        cosine, sine = cos_ref[here, :], sin_ref[here, :]

        def unit_of(v):
            inverse = lax.rsqrt(jnp.mean(v * v, axis=-1, keepdims=True) + epsilon)
            return v * inverse, inverse

        def low_of(unit, gain):
            scaled = unit * gain
            return (scaled * cosine + swap(scaled) * sine).astype(BF)

        def back_of(gradient, unit, inverse, gain, slot):
            turned = gradient * cosine - swap(gradient) * sine
            head_total[slot] += fold(turned * unit)
            return norm_back(turned * gain, unit, inverse).astype(BF)

        q_gain, k_gain = head_gains[:, :width], head_gains[:, width : 2 * width]
        k_unit, k_inverse = unit_of(raw_held[here, q_cols : q_cols + width])
        k_low = low_of(k_unit, k_gain)
        v_low = raw_held[here, q_cols + width : q_cols + 2 * width].astype(BF)
        k_grad = jnp.zeros((rows, width), F32)
        v_grad = jnp.zeros((rows, width), F32)
        for h in range(heads):
            lanes = slice(h * width, (h + 1) * width)
            q_unit, q_inverse = unit_of(raw_held[here, lanes])
            q_low = low_of(q_unit, q_gain)
            prob = prob_held[b * heads + h]
            own_grad = mixed_grad[:, lanes]
            v_grad += dot(prob.astype(BF), own_grad, TN)
            prob_grad = dot(own_grad, v_low, NT)
            score_grad = (
                prob * (prob_grad - jnp.sum(prob * prob_grad, axis=-1, keepdims=True))
            ).astype(BF)
            q_grad = dot(score_grad, k_low, NN) * scale
            k_grad += dot(score_grad, q_low, TN)
            raw_grad[here, lanes] = back_of(q_grad, q_unit, q_inverse, q_gain, 0)
        raw_grad[here, q_cols : q_cols + width] = back_of(
            k_grad * scale, k_unit, k_inverse, k_gain, 1
        )
        raw_grad[here, q_cols + width : q_cols + 2 * width] = v_grad.astype(BF)

    def out_piece(q):
        base = at.column_base(q)
        lanes = pl.ds(pl.multiple_of(base * width, 2 * width), 2 * width)
        left_side = mixed_held[:, lanes]
        step = 512
        for start in range(0, model, step):
            total = dot(left_side, held[:, start : start + step], TN)
            for c in (0, 1):
                out_tree.part[q, c, :, start : start + step] = total[
                    c * width : (c + 1) * width
                ].astype(BF)
        out_tree.part_copy(q).start()

    some = count // 2

    def cols_piece(q):
        base = at.column_base(q)
        for there in range(4):
            lanes = pl.ds(
                pl.multiple_of(there * (model // 4) + base * count, 2 * count), 2 * count
            )
            block = dot(normed_held[:, lanes], raw_grad[...], TN)
            small = dot(left[:, lanes], right[...], TN)
            for c in (0, 1):
                for i, tree in enumerate(cols_trees):
                    of = slice(c * count + i * some, c * count + (i + 1) * some)
                    here = pl.ds(there * some, some)
                    tree.part[q, c, here, :cols] = block[of].astype(BF)
                    tree.part[q, c, here, cols:] = small[of].astype(BF)
        cols_trees[0].part_copy(q).start()

    groups = ((0, q_cols), (q_cols, width), (q_cols + width, width), (cols, EXTRA))

    def exchange_refs(i, to, of):
        here = pl.ds(pl.multiple_of(to * some, some), some)
        first = 0
        refs = []
        for start, size in groups:
            lanes = pl.ds(pl.multiple_of(first + of * size, size), size)
            refs.append((cols_totals[i].at[here, pl.ds(start, size)], cols_alls[i].at[:, lanes]))
            first += 4 * size
        return refs

    def exchange(i, k):
        there = at.plane(k)
        turn = at.turn_at(there)
        return [
            remote(src, dst, ex_send.at[i, k - 1, j], ex_recv.at[i, turn - 1, j], (at.e, there))
            for j, (src, dst) in enumerate(exchange_refs(i, there, at.z))
        ]

    def exchange_arrival(i, k):
        return [
            remote(dst, dst, ex_send.at[i, k - 1, j], ex_recv.at[i, k - 1, j], at.sibling)
            for j, (src, dst) in enumerate(exchange_refs(i, at.z, at.plane(k)))
        ]

    def own_exchange(i):
        return [
            pltpu.make_async_copy(src, dst, ex_local.at[i, j])
            for j, (src, dst) in enumerate(exchange_refs(i, at.z, at.z))
        ]

    def begin_exchange(i):
        cols_trees[i].do_own(cols_totals[i])
        for k in (1, 2, 3):
            for copy in exchange(i, k):
                copy.start()
        for copy in own_exchange(i):
            copy.start()

    def end_exchange(i):
        for copy in own_exchange(i):
            copy.wait()
        for k in (1, 2, 3):
            for copy in exchange_arrival(i, k):
                copy.wait_recv()
        cols_spreads[i].begin()

    line.arrive(1)

    @pl.when(jnp.logical_not(outer))
    def _():
        line.arrive(2)

    for copy in loads[:5]:
        copy.wait()
    attention(False)

    @pl.when(outer)
    def _():
        line.arrive(2)
        line.arrive(3)

    loads[5].wait()
    for q in (DIAG, XCOL, YCOL, OWN):
        out_piece(q)
    out_tree.do_diag()
    attention(True)
    out_tree.do_own(out_total)
    out_spread.begin()
    for j in range(4):
        lanes = slice(j * quarter, (j + 1) * quarter)
        left[pl.ds(2 * rows, 16), lanes] = split_rows(
            gain_total[:, lanes] / small_ref[j, 0:1, :]
        )
    for slot in (0, 1):
        placed = jnp.dot(
            split_rows(head_total[slot]), place_ref[...], preferred_element_type=F32
        )
        left[pl.ds(2 * rows + 16 * (slot + 1), 16)] = placed.astype(BF)
    first, last = cols_trees
    for q in (DIAG, XCOL, YCOL, OWN):
        cols_piece(q)
    for q in (DIAG, XCOL, YCOL, OWN):
        last.part_copy(q).start()
    first.do_diag()
    last.do_diag()
    out_spread.cross()
    first.do_x()
    first.do_y()

    @pl.when(jnp.logical_not(outer))
    def _():
        sums.give_far()

    last.do_x()
    last.do_y()
    begin_exchange(0)
    sums.give_near(False)
    begin_exchange(1)
    end_exchange(0)
    out_spread.diag()
    end_exchange(1)
    cols_spreads[0].cross()
    sums.wait()

    @pl.loop(0, rows // 32)
    def _(i):
        here = pl.ds(pl.multiple_of(i * 32, 32), 32)
        dnormed_ref[here] += sums.total(here)

    cols_spreads[1].cross()
    cols_spreads[0].diag()
    cols_spreads[1].diag()
    out_spread.end()
    for spread in cols_spreads:
        spread.end()
    out_tree.drain()
    for tree in cols_trees:
        tree.drain()
    line.end()
    sums.end()
    for i in (0, 1):
        for k in (1, 2, 3):
            for copy in exchange(i, k):
                copy.wait_send()


def back_in_one(resident, sums, loaded):
    w_out, w_cols = loaded[:2]
    rows, model = resident[0].shape
    cols = w_cols.shape[1]
    wide = cols + EXTRA
    count = model // 4 // 8
    vmem = pl.BlockSpec(memory_space=pltpu.VMEM)
    hbm = pl.BlockSpec(memory_space=pl.ANY)
    dma = pltpu.SemaphoreType.DMA
    return pl.pallas_call(
        back_kernel,
        out_shape=(
            jax.ShapeDtypeStruct((rows, model), F32),
            jax.ShapeDtypeStruct((rows, model), BF),
            jax.ShapeDtypeStruct((rows, model), F32),
            jax.ShapeDtypeStruct((8 * HEAD_WIDTH, model), BF),
            jax.ShapeDtypeStruct((8 * count, 4 * wide), BF),
        ),
        in_specs=[vmem] * len(resident) + [hbm] * (1 + len(loaded)),
        out_specs=(vmem, vmem, vmem, hbm, hbm),
        scratch_shapes=[
            *[pltpu.VMEM(v.shape, v.dtype) for v in loaded],
            pltpu.VMEM((4 * rows, model), BF),
            pltpu.VMEM((4 * rows, cols), BF),
            pltpu.VMEM((3 * rows, model), BF),
            pltpu.VMEM((3 * rows, EXTRA), BF),
            pltpu.VMEM((rows, EXTRA), F32),
            pltpu.VMEM((EXTRA, model), BF),
            pltpu.VMEM((4, rows, model), BF),
            pltpu.VMEM((5, rows, model), BF),
            pltpu.VMEM((8, model), F32),
            pltpu.VMEM((2, 8, HEAD_WIDTH), F32),
            pltpu.VMEM((HEAD_WIDTH, model), BF),
            *[pltpu.VMEM((2 * count, wide), BF)] * 2,
            *[pltpu.VMEM((count // 2, 4 * wide), BF)] * 2,
            *Tree.buffers(HEAD_WIDTH, model),
            *Tree.semaphores(),
            *Tree.buffers(2 * count, wide),
            *Tree.semaphores(),
            *Tree.buffers(2 * count, wide),
            *Tree.semaphores(),
            *Spread.semaphores(),
            *Spread.semaphores(),
            *Spread.semaphores(),
            *Line.semaphores(),
            *LineSum.semaphores(),
            dma((2, 3, 4)),
            dma((2, 3, 4)),
            dma((2, 4)),
            dma((6,)),
            dma((2,)),
        ],
        compiler_params=pltpu.CompilerParams(
            collective_id=1, has_side_effects=True, vmem_limit_bytes=VMEM_BYTES
        ),
        cost_estimate=pl.CostEstimate(
            flops=2 * 4 * rows * model * cols * 5,
            bytes_accessed=64 * 1024 * 1024,
            transcendentals=4 * rows * cols,
        ),
    )(*resident, sums, *loaded)


def front_kernel(
    tokens_ref,
    small_ref,
    router_ref,
    w_query_ref,
    w_key_ref,
    w_value_ref,
    w_out_ref,
    table_ref,
    chosen_ref,
    cot_ref,
    second_ref,
    middle_ref,
    share_ref,
    w_cols_out,
    normed_out,
    raw_out,
    prob_out,
    mixed_out,
    cos_ref,
    sin_ref,
    small_all_ref,
    router_all_ref,
    cot_all_ref,
    w_cols_ref,
    normed_ref,
    raw_ref,
    prob_ref,
    mixed_ref,
    own_part,
    router_wide,
    rows_out,
    rows_in,
    small_send,
    small_recv,
    piece_send,
    piece_recv,
    piece_local,
    cot_local,
    store_sem,
    *sems,
):
    at = Place()
    rows, model = tokens_ref.shape
    pair = 2 * rows
    width = HEAD_WIDTH
    q_cols = w_query_ref.shape[1] // 4
    heads = q_cols // width
    cols = q_cols + 2 * width
    quarter = model // 4
    count = quarter // 8
    half = rows // 2
    experts_all = router_ref.shape[0]
    scale = HEAD_WIDTH ** (-0.5)
    meet(at.everyone())

    cot_here = pltpu.make_async_copy(cot_ref, cot_all_ref.at[at.z, at.e // 2], cot_local)
    cot_here.start()

    small_all_ref[at.z] = small_ref[...]
    router_all_ref[at.z] = router_ref[...]

    def small_copies(k):
        there = at.plane(k)
        turn = at.turn_at(there)
        return [
            remote(
                ref,
                ref_all.at[at.z],
                small_send.at[k - 1, i],
                small_recv.at[turn - 1, i],
                (at.e, there),
            )
            for i, (ref, ref_all) in enumerate(
                ((small_ref, small_all_ref), (router_ref, router_all_ref))
            )
        ]

    for k in (1, 2, 3):
        for copy in small_copies(k):
            copy.start()

    def w_block(k, q, i=None):
        first, size = (0, count) if i is None else (i * (count // 2), count // 2)
        row = at.plane(k) * quarter + at.own(q) * count + first
        return w_cols_ref.at[pl.ds(pl.multiple_of(row, count // 2), size)]

    def piece_refs(there):
        own = pl.ds(pl.multiple_of(at.e * count, count), count)
        row = pl.ds(pl.multiple_of(at.z * quarter + at.e * count, count), count)
        narrow = pl.ds(pl.multiple_of(there * width, width), width)
        return (
            (
                w_query_ref.at[own, pl.ds(pl.multiple_of(there * q_cols, q_cols), q_cols)],
                w_cols_ref.at[row, pl.ds(0, q_cols)],
            ),
            (w_key_ref.at[own, narrow], w_cols_ref.at[row, pl.ds(q_cols, width)]),
            (w_value_ref.at[own, narrow], w_cols_ref.at[row, pl.ds(q_cols + width, width)]),
        )

    def piece_copies(k):
        there = at.plane(k)
        turn = at.turn_at(there)
        return [
            remote(
                src, dst, piece_send.at[k - 1, i], piece_recv.at[turn - 1, i], (at.e, there)
            )
            for i, (src, dst) in enumerate(piece_refs(there))
        ]

    def pieces_arrive(k):
        block = w_block(k, OWN)
        for i, (first, size) in enumerate(((0, q_cols), (q_cols, width), (q_cols, width))):
            part = block.at[:, pl.ds(first, size)]
            remote(
                part, part, piece_send.at[k - 1, i], piece_recv.at[k - 1, i], at.sibling
            ).wait_recv()

    own_pieces = [
        pltpu.make_async_copy(src, dst, piece_local.at[i])
        for i, (src, dst) in enumerate(piece_refs(at.z))
    ]
    for copy in own_pieces:
        copy.start()
    for k in (1, 2, 3):
        for copy in piece_copies(k):
            copy.start()
    weights = Gather(at, w_block, sems[2:10])
    for copy in own_pieces:
        copy.wait()
    weights.own(0)

    def normed_block(b):
        return normed_ref.at[pl.ds(pl.multiple_of(b * rows, rows), rows)]

    line = Line(at, normed_block, sems[10:12])
    source = tokens_ref[...].astype(F32)
    inverse = lax.rsqrt(jnp.mean(source * source, axis=-1, keepdims=True) + epsilon)
    for k in (1, 2, 3):
        for i, ref_all in enumerate((small_all_ref, router_all_ref)):
            block = ref_all.at[at.plane(k)]
            remote(
                block, block, small_send.at[k - 1, i], small_recv.at[k - 1, i], at.sibling
            ).wait_recv()
    own_rows = pl.ds(pl.multiple_of(at.z * rows, rows), rows)
    for j in range(4):
        lanes = slice(j * quarter, (j + 1) * quarter)
        normed_ref[own_rows, lanes] = (source[:, lanes] * inverse * small_all_ref[j, 0:1, :]).astype(BF)
        router_wide[0:experts_all, lanes] = router_all_ref[j]
        router_wide[experts_all : 2 * experts_all, lanes] = router_all_ref[j]
    router_wide[2 * experts_all :] = jnp.zeros((EXTRA - 2 * experts_all, model), BF)
    line.begin()

    def cot_block(k, q, i=None):
        block = cot_all_ref.at[at.plane(k), at.column_base(q) // 2]
        return block if i is None else block.at[pl.ds(i * half, half)]

    def cot_line_block(b):
        return cot_all_ref.at[b, at.e // 2]

    cot_line = Line(at, cot_line_block, sems[12:14])
    cot_gather = Gather(at, cot_block, sems[14:], sibling=False)
    outer = (at.z == 0) | (at.z == 3)
    cot_here.wait()

    @pl.when(outer)
    def _():
        cot_line.begin()


    pieces_arrive(1)
    weights.own(1)
    line.arrive(1)
    pieces_arrive(2)
    weights.own(2)
    pieces_arrive(3)
    weights.own(3)

    @pl.when(jnp.logical_not(outer))
    def _():
        line.arrive(2)

    weights.cross(0)
    weights.cross(1)

    @pl.when(jnp.logical_not(outer))
    def _():
        line.arrive(3)
        cot_line.begin()

    cot_gather.own(0)
    weights.diag(0)
    weights.cross(2)
    weights.diag(1)
    weights.cross(3)
    weights.diag(2)
    weights.diag(3)
    stores = [
        pltpu.make_async_copy(src, dst, store_sem.at[i])
        for i, (src, dst) in enumerate(
            (
                (normed_ref, normed_out),
                (w_cols_ref, w_cols_out),
                (raw_ref, raw_out),
                (prob_ref, prob_out),
                (mixed_ref, mixed_out),
            )
        )
    ]
    for k in range(4):
        for q in range(4):
            weights.ready(k, q)
    stores[1].start()
    sums = LineSum(at, rows_out, rows_in, sems[:2])

    def is_far(turn):
        return outer if turn == 0 else jnp.logical_not(outer)

    def project(turn):
        first = 2 * jnp.where(is_far(turn), 1 - at.half, at.half)
        both = pl.ds(pl.multiple_of(first * rows, pair), pair)
        step = 256
        for start in range(0, cols, step):
            lanes = slice(start, start + step)
            raw_ref[both, lanes] = jnp.dot(
                normed_ref[both, :], w_cols_ref[:, lanes], preferred_element_type=F32
            )

    gains = small_all_ref[0, 2:3, :] + small_all_ref[1, 2:3, :] + small_all_ref[2, 2:3, :] + small_all_ref[3, 2:3, :]
    q_gain, k_gain = gains[:, :width], gains[:, width : 2 * width]
    row_id = lax.broadcasted_iota(jnp.int32, (rows, rows), 0).astype(F32)
    lane_id = lax.broadcasted_iota(jnp.int32, (rows, rows), 1).astype(F32)

    def attention(turn):
        first = 2 * jnp.where(is_far(turn), 1 - at.half, at.half)
        both = pl.ds(pl.multiple_of(first * rows, pair), pair)
        heads_of(first)
        if turn == 1:

            @pl.when(outer)
            def _():
                cot_line.arrive(2)
                cot_gather.own(2)

            @pl.when(jnp.logical_not(outer))
            def _():
                cot_gather.cross(2)

        heads_of(first + 1)
        step = 512
        for start in range(0, model, step):
            lanes = slice(start, start + step)
            part = jnp.dot(mixed_ref[both, :], w_out_ref[:, lanes], preferred_element_type=F32)

            @pl.when(jnp.logical_not(is_far(turn)))
            def _():
                own_part[:, lanes] = jnp.where(at.z % 2 == 0, part[:rows], part[rows:])

            rows_out[first, :, lanes] = part[:rows].astype(BF)
            rows_out[first + 1, :, lanes] = part[rows:].astype(BF)

        @pl.when(is_far(turn))
        def _():
            sums.give_far()

        if turn == 1:
            sums.give_near(True)
            sums.give_near(False)

    def heads_of(b):
        here = pl.ds(pl.multiple_of(b * rows, rows), rows)
        segment = jnp.zeros((rows, rows), F32)
        lane_segment = jnp.zeros((rows, rows), F32)
        place = row_id
        end = jnp.zeros((1, 1), F32)
        for i in range(SEQ_SLOTS - 1):
            length = small_all_ref[b, 2:3, 2 * width + i : 2 * width + i + 1]
            end = end + length
            past = (row_id >= end).astype(F32)
            segment += past
            place -= past * length
            lane_segment += (lane_id >= end).astype(F32)
        allowed = (segment == lane_segment) & (lane_id <= row_id)
        named = (lane_id == place).astype(BF)

        def looked_up(first):
            total = jnp.zeros((rows, width), F32)
            for i in range(3):
                part = table_ref[(first + i) * width : (first + i + 1) * width]
                total += jnp.dot(named, part, preferred_element_type=F32)
            return total

        cosine, sine = looked_up(0), looked_up(3)
        cos_ref[here, :] = cosine
        sin_ref[here, :] = sine

        def low_of(v, gain):
            inverse = lax.rsqrt(jnp.mean(v * v, axis=-1, keepdims=True) + epsilon)
            scaled = v * inverse * gain
            return (scaled * cosine + swap(scaled) * sine).astype(BF)

        k_low = low_of(raw_ref[here, q_cols : q_cols + width], k_gain)
        v_low = raw_ref[here, q_cols + width : q_cols + 2 * width].astype(BF)
        for h in range(heads):
            lanes = slice(h * width, (h + 1) * width)
            q_low = low_of(raw_ref[here, lanes], q_gain)
            scores = jnp.where(allowed, dot(q_low, k_low, NT) * scale, masked_score)
            weight = jnp.exp(scores - jnp.max(scores, axis=-1, keepdims=True))
            prob = weight / jnp.sum(weight, axis=-1, keepdims=True)
            prob_ref[b * heads + h] = prob
            mixed_ref[here, lanes] = dot(prob.astype(BF), v_low, NN).astype(BF)

    @pl.when(outer)
    def _():
        line.arrive(2)
        line.arrive(3)

    project(0)
    cot_line.arrive(1)
    cot_gather.own(1)
    attention(0)

    @pl.when(jnp.logical_not(outer))
    def _():
        cot_line.arrive(2)
        cot_gather.own(2)

    cot_gather.cross(0)
    stores[0].start()
    project(1)
    stores[2].start()

    @pl.when(jnp.logical_not(outer))
    def _():
        cot_line.arrive(3)
        cot_gather.own(3)

    cot_gather.cross(1)
    attention(1)
    stores[3].start()
    stores[4].start()

    @pl.when(outer)
    def _():
        cot_line.arrive(3)
        cot_gather.own(3)
        cot_gather.cross(2)

    cot_gather.diag(0)
    cot_gather.diag(1)
    cot_gather.cross(3)
    sums.wait()
    middle = (
        tokens_ref[...].astype(F32)
        + own_part[...]
        + sums.total(pl.ds(0, rows))
    )
    middle_ref[...] = middle
    inverse = lax.rsqrt(jnp.mean(middle * middle, axis=-1, keepdims=True) + epsilon)
    for j in range(4):
        lanes = slice(j * quarter, (j + 1) * quarter)
        second_ref[:, lanes] = (middle[:, lanes] * inverse * small_all_ref[j, 1:2, :]).astype(BF)
    logits = dot(second_ref[:, :model], router_wide[...], NT)
    chosen = chosen_ref[...] > 0.0
    lane = lax.broadcasted_iota(jnp.int32, (rows, EXTRA), 1)
    top = jnp.max(jnp.where(chosen, logits, masked_score), axis=-1, keepdims=True)
    lifted = jnp.where(chosen, jnp.exp(logits - top), 0.0)
    share = lifted / jnp.sum(jnp.where(lane < experts_all, lifted, 0.0), axis=-1, keepdims=True)
    share_ref[...] = share
    high = share.astype(BF).astype(F32)
    second_ref[:, model:] = jnp.where(lane < experts_all, high, share - high).astype(BF)
    cot_gather.diag(2)
    cot_gather.diag(3)
    for copy in stores:
        copy.wait()
    for k in range(4):
        cot_gather.end(k)
        weights.end(k)
    line.end()
    cot_line.end()
    sums.end()
    for k in (1, 2, 3):
        for copy in small_copies(k):
            copy.wait_send()
        for copy in piece_copies(k):
            copy.wait_send()


def front_in_one(tokens, small, router, w_query, w_key, w_value, w_out, table, chosen, cotangent):
    rows, model = tokens.shape
    q_cols = w_query.shape[1] // 4
    cols = q_cols + 2 * HEAD_WIDTH
    heads = q_cols // HEAD_WIDTH
    experts_all = router.shape[0]
    vmem = pl.BlockSpec(memory_space=pltpu.VMEM)
    hbm = pl.BlockSpec(memory_space=pl.ANY)
    dma = pltpu.SemaphoreType.DMA
    shape = jax.ShapeDtypeStruct
    return pl.pallas_call(
        front_kernel,
        out_shape=(
            shape((rows, model + EXTRA), BF),
            shape((rows, model), F32),
            shape((rows, EXTRA), F32),
            shape((model, cols), BF),
            shape((4 * rows, model), BF),
            shape((4 * rows, cols), F32),
            shape((4 * heads, rows, rows), F32),
            shape((4 * rows, q_cols), BF),
            shape((4 * rows, HEAD_WIDTH), F32),
            shape((4 * rows, HEAD_WIDTH), F32),
            shape((4, 8, model // 4), F32),
            shape((4, experts_all, model // 4), BF),
            shape((4, 4, rows, model), BF),
        ),
        in_specs=[vmem, vmem, vmem, hbm, hbm, hbm, vmem, vmem, vmem, hbm],
        out_specs=(vmem,) * 3 + (hbm,) * 5 + (vmem,) * 4 + (hbm,),
        scratch_shapes=[
            pltpu.VMEM((model, cols), BF),
            pltpu.VMEM((4 * rows, model), BF),
            pltpu.VMEM((4 * rows, cols), F32),
            pltpu.VMEM((4 * heads, rows, rows), F32),
            pltpu.VMEM((4 * rows, q_cols), BF),
            pltpu.VMEM((rows, model), F32),
            pltpu.VMEM((EXTRA, model), BF),
            pltpu.VMEM((4, rows, model), BF),
            pltpu.VMEM((5, rows, model), BF),
            dma((3, 2)),
            dma((3, 2)),
            dma((3, 3)),
            dma((3, 3)),
            dma((3,)),
            dma,
            dma((5,)),
            *LineSum.semaphores(),
            *Gather.semaphores(),
            *Line.semaphores(),
            *Line.semaphores(),
            *Gather.semaphores(False),
        ],
        compiler_params=pltpu.CompilerParams(
            collective_id=2, has_side_effects=True, vmem_limit_bytes=VMEM_BYTES
        ),
        cost_estimate=pl.CostEstimate(
            flops=2 * 4 * rows * model * (cols + q_cols),
            bytes_accessed=64 * 1024 * 1024,
            transcendentals=4 * rows * cols,
        ),
    )(tokens, small, router, w_query, w_key, w_value, w_out, table, chosen, cotangent)


def per_device(
    tokens,
    lengths,
    routes,
    attn_gain,
    w_query,
    key_projection,
    value_projection,
    w_out,
    query_gain,
    key_gain,
    ffn_gain,
    w_router,
    w_gate,
    w_up,
    w_down,
    cotangent,
):
    ring = lax.axis_size("fsdp")
    groups = lax.axis_size("expert")
    plane_rank = lax.axis_index("expert")
    experts_all = w_router.shape[1]
    local_experts = w_gate.shape[0]
    units = w_gate.shape[2]
    wide = local_experts * units
    in_rows = MODEL_WIDTH // ring
    heads = QUERY_HEADS // ring
    kv = KEY_VALUE_HEADS // ring
    group_width = heads // kv
    q_cols = heads * HEAD_WIDTH
    kv_cols = kv * HEAD_WIDTH
    cols = q_cols + 2 * kv_cols
    piece_rows = in_rows // groups
    score_scale = HEAD_WIDTH ** (-0.5)
    both = ("expert", "fsdp")
    one_block = (groups, ring, experts_all) == (8, 4, 16)

    gate_w = w_gate.transpose(0, 2, 1).reshape(wide, MODEL_WIDTH)
    up_w = w_up.transpose(0, 2, 1).reshape(wide, MODEL_WIDTH)
    down_w = w_down.reshape(wide, MODEL_WIDTH)
    line_tokens = ring * DEVICE_TOKENS
    source = tokens.astype(F32)
    expert_ids = jnp.arange(experts_all, dtype=jnp.int32)
    chosen = jnp.any(routes[:, :, None] == expert_ids[None, None, :], axis=1)

    if one_block:
        quarter_of = jnp.arange(HEAD_WIDTH) // (HEAD_WIDTH // ring)
        own_quarter = quarter_of == lax.axis_index("fsdp")

        def spread(gain, first):
            placed = jnp.where(own_quarter, jnp.tile(gain.astype(F32), ring), 0.0)
            return jnp.pad(placed, (first, in_rows - first - HEAD_WIDTH))

        first = 2 * HEAD_WIDTH
        third = spread(query_gain, 0) + spread(key_gain, HEAD_WIDTH)
        third += jnp.pad(
            lengths.reshape(-1).astype(F32), (first, in_rows - first - SEQ_SLOTS)
        )
        row = jnp.arange(8)[:, None]
        small = jnp.where(
            row == 0,
            attn_gain.astype(F32)[None, :],
            jnp.where(
                row == 1,
                ffn_gain.astype(F32)[None, :],
                jnp.where(row == 2, third[None, :], 0.0),
            ),
        )
        lane = jnp.arange(EXTRA)
        lane_expert = jnp.where(lane < 2 * experts_all, lane % experts_all, -1)
        wide_chosen = jnp.any(routes[:, :, None] == lane_expert[None, None, :], axis=1).astype(F32)
        frequency = rope_base ** (-np.arange(0, HEAD_WIDTH, 2) / HEAD_WIDTH)
        angles = np.arange(HEAD_WIDTH)[:, None] * np.tile(frequency, 2)[None, :]
        sine_sign = np.where(np.arange(HEAD_WIDTH) < HEAD_WIDTH // 2, -1.0, 1.0)
        parts = []
        for exact in (np.cos(angles), np.sin(angles) * sine_sign):
            for _ in range(3):
                parts.append(exact.astype(ml_dtypes.bfloat16))
                exact = exact - parts[-1].astype(np.float64)
        (
            second_wide,
            middle,
            share,
            w_cols,
            normed_all,
            raw,
            probabilities,
            mixed,
            cosine,
            sine_table,
            small_all,
            router_all,
            cot_all,
        ) = front_in_one(
            tokens,
            small,
            w_router.T,
            w_query,
            key_projection,
            value_projection,
            w_out,
            jnp.asarray(np.concatenate(parts)),
            wide_chosen,
            cotangent,
        )
        cot_all = cot_all.reshape(-1, MODEL_WIDTH)
        attn_gain_f = small_all[:, 0].reshape(-1)
        attn_inverse = lax.rsqrt(jnp.mean(source * source, axis=-1, keepdims=True) + epsilon)
        attn_unit = source * attn_inverse
    else:
        small = jnp.concatenate(
            [
                attn_gain,
                ffn_gain,
                query_gain,
                key_gain,
                w_router.reshape(-1),
                lengths.reshape(-1).astype(BF),
            ]
        )
        small_all = lax.all_gather(small, "fsdp", axis=0, tiled=False)
        at = 0

        def take(count):
            nonlocal at
            part = small_all[:, at : at + count]
            at += count
            return part

        attn_gain_f = take(in_rows).reshape(-1).astype(F32)
        ffn_gain_f = take(in_rows).reshape(-1).astype(F32)
        query_gain_f = take(HEAD_WIDTH // ring).reshape(-1).astype(F32)
        key_gain_f = take(HEAD_WIDTH // ring).reshape(-1).astype(F32)
        router_all = take(in_rows * experts_all).reshape(MODEL_WIDTH, experts_all)
        lengths_all = take(SEQ_SLOTS).astype(jnp.int32)

        by_col = jnp.concatenate(
            [
                w_query.reshape(in_rows, ring, q_cols),
                key_projection.reshape(in_rows, ring, kv_cols),
                value_projection.reshape(in_rows, ring, kv_cols),
            ],
            axis=2,
        )
        piece = lax.dynamic_slice_in_dim(by_col, plane_rank * piece_rows, piece_rows, 0)
        piece = lax.all_to_all(
            piece.transpose(1, 0, 2), "fsdp", split_axis=0, concat_axis=0, tiled=True
        )
        w_cols = lax.all_gather(piece, "expert", axis=1, tiled=True).reshape(MODEL_WIDTH, cols)

        attn_inverse = lax.rsqrt(jnp.mean(source * source, axis=-1, keepdims=True) + epsilon)
        attn_unit = source * attn_inverse
        normed = (attn_unit * attn_gain_f).astype(BF)
        normed_all = lax.all_gather(normed, "fsdp", axis=0, tiled=True)
        raw = dot(normed_all, w_cols, NN)
        query_raw = raw[:, :q_cols].reshape(ring, DEVICE_TOKENS, kv, group_width, HEAD_WIDTH)
        key_raw = raw[:, q_cols : q_cols + kv_cols].reshape(ring, DEVICE_TOKENS, kv, HEAD_WIDTH)
        value_low = raw[:, q_cols + kv_cols :].astype(BF).reshape(ring, DEVICE_TOKENS, kv, HEAD_WIDTH)
        places, segment_ids = jax.vmap(lambda row: layout(row, DEVICE_TOKENS, SEQ_SLOTS))(lengths_all)
        cosine, sine_table = rope_tables(places, HEAD_WIDTH)
        cos_k, sin_k = cosine[:, :, None, :], sine_table[:, :, None, :]
        cos_q, sin_q = cosine[:, :, None, None, :], sine_table[:, :, None, None, :]
        query_inverse = lax.rsqrt(jnp.mean(query_raw * query_raw, axis=-1, keepdims=True) + epsilon)
        query_unit = query_raw * query_inverse
        query_low = rotate(query_unit * query_gain_f, cos_q, sin_q).astype(BF)
        key_inverse = lax.rsqrt(jnp.mean(key_raw * key_raw, axis=-1, keepdims=True) + epsilon)
        key_unit = key_raw * key_inverse
        key_low = rotate(key_unit * key_gain_f, cos_k, sin_k).astype(BF)
        row_ids = jnp.arange(DEVICE_TOKENS, dtype=jnp.int32)
        allowed = (segment_ids[:, :, None] == segment_ids[:, None, :]) & (
            row_ids[None, None, :] <= row_ids[None, :, None]
        )
        scores = (
            jnp.einsum("bqhgd,bkhd->bhgqk", query_low, key_low, preferred_element_type=F32)
            * score_scale
        )
        scores = jnp.where(allowed[:, None, None], scores, masked_score)
        weights = jnp.exp(scores - jnp.max(scores, axis=-1, keepdims=True))
        probabilities = weights / jnp.sum(weights, axis=-1, keepdims=True)
        prob_low = probabilities.astype(BF)
        mixed = (
            jnp.einsum("bhgqk,bkhd->bqhgd", prob_low, value_low, preferred_element_type=F32)
            .astype(BF)
            .reshape(line_tokens, q_cols)
        )
        branch = lax.psum_scatter(
            dot(mixed, w_out, NN).astype(BF), "fsdp", scatter_dimension=0, tiled=True
        ).astype(F32)
        middle = source + branch
        ffn_inverse = lax.rsqrt(jnp.mean(middle * middle, axis=-1, keepdims=True) + epsilon)
        ffn_unit = middle * ffn_inverse
        second = (ffn_unit * ffn_gain_f).astype(BF)

        logits = dot(second, router_all, NN)
        top = jnp.max(jnp.where(chosen, logits, -jnp.inf), axis=1, keepdims=True)
        lifted = jnp.where(chosen, jnp.exp(logits - top), 0.0)
        share = lifted / jnp.sum(lifted, axis=1, keepdims=True)

    def experts(second, share, cotangent):
        second_all = lax.all_gather(second, both, axis=0, tiled=True)
        share_all = lax.all_gather(share, both, axis=0, tiled=True)
        cot_all = lax.all_gather(cotangent, both, axis=0, tiled=True)
        first = plane_rank * local_experts
        own_share = lax.dynamic_slice_in_dim(share_all, first, local_experts, 1)
        share_wide = jnp.repeat(own_share, units, axis=1)
        gate_act = dot(second_all, gate_w, NT)
        up_act = dot(second_all, up_w, NT)
        back = dot(cot_all, down_w, NT)
        sigmoid_gate = jax.nn.sigmoid(gate_act)
        silu_gate = gate_act * sigmoid_gate
        hidden = silu_gate * up_act
        share_grad = jnp.sum((hidden * back).reshape(-1, local_experts, units), axis=2)
        hidden_low = (share_wide * hidden).astype(BF)
        hidden_grad = share_wide * back
        gate_grad = (
            hidden_grad * up_act * sigmoid_gate * (1.0 + gate_act * (1.0 - sigmoid_gate))
        ).astype(BF)
        up_grad = (hidden_grad * silu_gate).astype(BF)
        routed_part = dot(hidden_low, down_w, NN).astype(BF)
        second_part = (dot(gate_grad, gate_w, NN) + dot(up_grad, up_w, NN)).astype(BF)
        spread = jnp.zeros((share_grad.shape[0], experts_all), F32)
        spread = lax.dynamic_update_slice_in_dim(spread, share_grad, first, 1)
        second_grad = lax.psum_scatter(second_part, both, scatter_dimension=0, tiled=True)
        routed = lax.psum_scatter(routed_part, both, scatter_dimension=0, tiled=True)
        dshare = lax.psum_scatter(spread, both, scatter_dimension=0, tiled=True)
        return (
            (second_grad.astype(F32), routed.astype(F32), dshare),
            (
                dot(gate_grad, second_all, TN),
                dot(up_grad, second_all, TN),
                dot(hidden_low, cot_all, TN),
            ),
        )

    chunks = max(1, ring * groups // 32)
    if one_block:
        sums, *weight_grads, _ = experts_in_one(second_wide, cot_all, gate_w, up_w, down_w)
        weight_grads = [grad.astype(F32) for grad in weight_grads]
    elif chunks == 1:
        rows_out, weight_grads = experts(second, share, cotangent)
    else:
        def turn(total, rows):
            rows_out, grads = experts(*rows)
            return jax.tree.map(jnp.add, total, grads), rows_out

        start = (
            jnp.zeros((wide, MODEL_WIDTH), F32),
            jnp.zeros((wide, MODEL_WIDTH), F32),
            jnp.zeros((wide, MODEL_WIDTH), F32),
        )
        weight_grads, rows_out = lax.scan(
            turn,
            start,
            [v.reshape(chunks, -1, v.shape[1]) for v in (second, share, cotangent)],
        )
        rows_out = [v.reshape(-1, v.shape[2]) for v in rows_out]
    gate_wgrad, up_wgrad, down_wgrad = weight_grads
    grad_w_gate = gate_wgrad.reshape(local_experts, units, MODEL_WIDTH).transpose(0, 2, 1)
    grad_w_up = up_wgrad.reshape(local_experts, units, MODEL_WIDTH).transpose(0, 2, 1)
    grad_w_down = down_wgrad.reshape(local_experts, units, MODEL_WIDTH)
    if one_block:
        at_gain = experts_all
        part_width = HEAD_WIDTH // ring
        head_lane = np.arange(HEAD_WIDTH)
        place_of = head_lane // part_width * in_rows + head_lane % part_width
        placing = jnp.asarray(place_of[:, None] == np.arange(MODEL_WIDTH)[None, :], BF)
        normed_grad, block_out, middle_grad, out_sum, cols_sum = back_in_one(
            (
                middle,
                share,
                cotangent,
                router_all,
                small_all,
                cosine,
                sine_table,
                second_wide,
                placing,
            ),
            sums,
            (w_out, w_cols, mixed, normed_all, raw, probabilities),
        )
        tokens_grad = middle_grad + norm_back(normed_grad * attn_gain_f, attn_unit, attn_inverse)
        out_grad = out_sum.astype(F32)
        ends = [ring * n for n in (q_cols, q_cols + kv_cols, cols)]
        grad_w_query = cols_sum[:, : ends[0]].astype(F32)
        grad_w_key = cols_sum[:, ends[0] : ends[1]].astype(F32)
        grad_w_value = cols_sum[:, ends[1] : ends[2]].astype(F32)
        small_own = sum(
            cols_sum[:, ends[2] + j * EXTRA : ends[2] + (j + 1) * EXTRA].astype(F32)
            for j in range(ring)
        )
        own_grads = (
            small_own[:, at_gain + 1],
            small_own[:part_width, at_gain + 2],
            small_own[:part_width, at_gain + 3],
            small_own[:, at_gain],
            small_own[:, :experts_all],
        )
    else:
        second_grad, routed, dshare = rows_out
        block_out = (middle + routed).astype(BF)

        mean_grad = jnp.sum(share * dshare, axis=1, keepdims=True)
        logit_grad = (share * (dshare - mean_grad)).astype(BF)
        upstream = cotangent.astype(F32)
        second_grad = second_grad + dot(logit_grad, router_all, NT)
        middle_grad = upstream + norm_back(second_grad * ffn_gain_f, ffn_unit, ffn_inverse)
        router_grad = dot(second, logit_grad, TN)
        ffn_gain_grad = jnp.sum(second_grad * ffn_unit, axis=0)
        branch_all = lax.all_gather(middle_grad.astype(BF), "fsdp", axis=0, tiled=True)
        out_grad = lax.psum(dot(mixed, branch_all, TN).astype(BF), "expert").astype(F32)
        mixed_grad = dot(branch_all, w_out, NT).astype(BF)
        mixed_grad = mixed_grad.reshape(ring, DEVICE_TOKENS, kv, group_width, HEAD_WIDTH)
        value_grad = jnp.einsum("bhgqk,bqhgd->bkhd", prob_low, mixed_grad, preferred_element_type=F32)
        prob_grad = jnp.einsum("bqhgd,bkhd->bhgqk", mixed_grad, value_low, preferred_element_type=F32)
        score_grad = (
            probabilities * (prob_grad - jnp.sum(probabilities * prob_grad, axis=-1, keepdims=True))
        ).astype(BF)
        query_grad = (
            jnp.einsum("bhgqk,bkhd->bqhgd", score_grad, key_low, preferred_element_type=F32)
            * score_scale
        )
        key_grad = (
            jnp.einsum("bhgqk,bqhgd->bkhd", score_grad, query_low, preferred_element_type=F32)
            * score_scale
        )
        query_turned = unrotate(query_grad, cos_q, sin_q)
        query_gain_grad = jnp.sum(query_turned * query_unit, axis=(0, 1, 2, 3))
        query_back = norm_back(query_turned * query_gain_f, query_unit, query_inverse)
        key_turned = unrotate(key_grad, cos_k, sin_k)
        key_gain_grad = jnp.sum(key_turned * key_unit, axis=(0, 1, 2))
        key_back = norm_back(key_turned * key_gain_f, key_unit, key_inverse)
        raw_grad = jnp.concatenate(
            [
                query_back.astype(BF).reshape(line_tokens, q_cols),
                key_back.astype(BF).reshape(line_tokens, kv_cols),
                value_grad.astype(BF).reshape(line_tokens, kv_cols),
            ],
            axis=1,
        )
        cols_grad = dot(normed_all, raw_grad, TN).astype(BF)
        normed_part = dot(raw_grad, w_cols, NT).astype(BF)
        normed_grad = lax.psum_scatter(normed_part, "fsdp", scatter_dimension=0, tiled=True).astype(F32)
        attn_gain_grad = jnp.sum(normed_grad * attn_unit, axis=0)
        tokens_grad = middle_grad + norm_back(normed_grad * attn_gain_f, attn_unit, attn_inverse)

        own = lax.psum_scatter(
            cols_grad.reshape(ring, groups, piece_rows, cols), "expert", scatter_dimension=1, tiled=False
        )
        own = lax.all_to_all(own, "fsdp", split_axis=0, concat_axis=0, tiled=True)
        rows_grad = lax.all_gather(own, "expert", axis=1, tiled=True)
        rows_grad = rows_grad.transpose(1, 0, 2).astype(F32)
        grad_w_query = rows_grad[:, :, :q_cols].reshape(in_rows, QUERY_HEADS * HEAD_WIDTH)
        grad_w_key = rows_grad[:, :, q_cols : q_cols + kv_cols].reshape(in_rows, -1)
        grad_w_value = rows_grad[:, :, q_cols + kv_cols :].reshape(in_rows, -1)

        small_grad = jnp.concatenate(
            [
                attn_gain_grad.reshape(ring, -1),
                ffn_gain_grad.reshape(ring, -1),
                query_gain_grad.reshape(ring, -1),
                key_gain_grad.reshape(ring, -1),
                router_grad.reshape(ring, -1),
            ],
            axis=1,
        )
        small_own = lax.psum(small_grad, both)
        small_own = lax.dynamic_index_in_dim(small_own, lax.axis_index("fsdp"), 0, keepdims=False)
        a, b = in_rows, HEAD_WIDTH // ring
        own_grads = (
            small_own[:a],
            small_own[2 * a : 2 * a + b],
            small_own[2 * a + b : 2 * a + 2 * b],
            small_own[a : 2 * a],
            small_own[2 * a + 2 * b :].reshape(in_rows, experts_all),
        )
    return (
        block_out,
        tokens_grad,
        own_grads[0],
        grad_w_query,
        grad_w_key,
        grad_w_value,
        out_grad,
        own_grads[1],
        own_grads[2],
        own_grads[3],
        own_grads[4],
        grad_w_gate,
        grad_w_up,
        grad_w_down,
    )


def solution(mesh):
    rows = P(("expert", "fsdp"), None)
    return jax.shard_map(
        per_device,
        mesh=mesh,
        in_specs=(
            rows,
            rows,
            rows,
            P("fsdp"),
            P("fsdp", None),
            P("fsdp", None),
            P("fsdp", None),
            P("fsdp", None),
            P("fsdp"),
            P("fsdp"),
            P("fsdp"),
            P("fsdp", None),
            P("expert", None, "fsdp"),
            P("expert", None, "fsdp"),
            P("expert", "fsdp", None),
            rows,
        ),
        out_specs=(
            rows,
            rows,
            P("fsdp"),
            P("fsdp", None),
            P("fsdp", None),
            P("fsdp", None),
            P("fsdp", None),
            P("fsdp"),
            P("fsdp"),
            P("fsdp"),
            P("fsdp", None),
            P("expert", None, "fsdp"),
            P("expert", None, "fsdp"),
            P("expert", "fsdp", None),
        ),
        check_vma=False,
    )
```
